256 devices in a mesh: dp: 16 (over x_hi, z), ctx: 16 (over y, x_lo, core).
Axes of the slice: x: 4 (x_hi: 2, x_lo: 2; x = x_hi * 2 + x_lo), y: 4, z: 8, core: 2. Of those that a mesh axis runs over, the one named last changes fastest.
Arguments:
- query: bfloat16 [16, 512, 4096], P('dp', None, 'ctx'), may hold values from -6 to 6
- key_act: bfloat16 [16, 512, 4096], P('dp', None, 'ctx'), may hold values from -6 to 6
- value_act: bfloat16 [16, 512, 4096], P('dp', None, 'ctx'), may hold values from -6 to 6
- filter_taps: float32 [512, 4096], P(None, 'ctx'), may hold values from -2 to 2
- grad_out: bfloat16 [16, 512, 4096], P('dp', None, 'ctx'), may hold values from -6 to 6
Outputs:
- output: bfloat16 [16, 512, 4096], P('dp', None, 'ctx')
- grad_query: bfloat16 [16, 512, 4096], P('dp', None, 'ctx')
- grad_key: bfloat16 [16, 512, 4096], P('dp', None, 'ctx')
- grad_value: bfloat16 [16, 512, 4096], P('dp', None, 'ctx')
- grad_filter: float32 [512, 4096], P(None, 'ctx')
The draws below stay inside these ranges and needn't reach their ends.
All inputs are finite; a program needn't handle non-finite values.
Results may differ from the reference program's by a relative error of at most 0.0011.
Values sent between devices are 32-bit elements; how exact they have to be, the bound alone decides.
A program may use at most 128 MiB of HBM per device.

```python
import math
import jax
import jax.numpy as jnp
from jax import lax

CH = 512
SEQ = 4096
BATCH = 16


def draw_filter_taps(key, part):
    key = jax.random.fold_in(key, 7)
    rate_key, noise_key = jax.random.split(key, 2)
    positions = jnp.arange(SEQ, dtype=jnp.float32)
    log_rate = jax.random.uniform(rate_key, (CH, 1), jnp.float32, math.log(0.25 / SEQ), math.log(1.0 / 40.0))
    noise = jnp.clip(jax.random.normal(noise_key, (CH, SEQ), jnp.float32), -6.0, 6.0)
    decay_rate = jnp.exp(log_rate)
    energy = jnp.expm1(-2.0 * decay_rate * SEQ) / jnp.expm1(-2.0 * decay_rate)
    amplitude = 1.0 / jnp.sqrt(energy)
    return noise * amplitude * jnp.exp(-decay_rate * positions)


def shard_levels(key, extent, shards, least, top_value):
    level = 1.0
    for dim, parts in shards:
        draws = jax.random.uniform(jax.random.fold_in(jax.random.fold_in(key, 6), dim), (parts,), jnp.float32, least / len(shards), top_value / len(shards))
        level = level * jnp.repeat(jnp.exp(draws), extent[dim] // parts).reshape((-1,) + (1,) * (len(extent) - 1 - dim))
    return level


def normal_values(stream_key, shape, width, reach, pieces=(), held_as=jnp.bfloat16):
    drawn = width * jax.random.normal(stream_key, shape, jnp.float32)
    if pieces:
        drawn = drawn * shard_levels(stream_key, shape, pieces, -0.22, 0.18)
    return jnp.clip(drawn, -reach, reach).astype(held_as)


def setup_inputs(seed: int = 0) -> dict:
    seeds = jax.random.split(jax.random.key(seed), 6)
    return {
        "query": normal_values(seeds[0], (BATCH, CH, SEQ), 1.0, 6.0, ((0, 16), (2, 16))),
        "key_act": normal_values(seeds[1], (BATCH, CH, SEQ), 1.0, 6.0, ((0, 16), (2, 16))),
        "value_act": normal_values(seeds[2], (BATCH, CH, SEQ), 1.0, 6.0, ((0, 16), (2, 16))),
        "filter_taps": draw_filter_taps(jax.random.fold_in(seeds[5], 71), 0),
        "grad_out": normal_values(seeds[4], (BATCH, CH, SEQ), 1.0, 6.0, ((0, 16), (2, 16))),
    }


def forward_transform(signal):
    return jnp.fft.rfft(signal, n=2 * SEQ, axis=-1)

def inverse_transform(spectrum):
    return jnp.fft.irfft(spectrum, n=2 * SEQ, axis=-1)[..., :SEQ].astype(jnp.float32)

def reference(query, key_act, value_act, filter_taps, grad_out):
    filt_spec = forward_transform(filter_taps)

    def one_sequence(inputs):
        query_one, key_one, value_one, grad_one = inputs
        query32 = query_one.astype(jnp.float32)
        key32 = key_one.astype(jnp.float32)
        value32 = value_one.astype(jnp.float32)
        grad32 = grad_one.astype(jnp.float32)
        mixed = key32 * value32
        z_spec = forward_transform(mixed)
        conv = inverse_transform(z_spec * filt_spec)
        output = (query32 * conv).astype(jnp.bfloat16)
        dconv = query32 * grad32
        dconv_spec = forward_transform(dconv)
        dmixed = inverse_transform(jnp.conj(filt_spec) * dconv_spec)
        grad_query = (grad32 * conv).astype(jnp.bfloat16)
        grad_key = (dmixed * value32).astype(jnp.bfloat16)
        grad_value = (dmixed * key32).astype(jnp.bfloat16)
        filter_term = inverse_transform(jnp.conj(z_spec) * dconv_spec)
        return (output, grad_query, grad_key, grad_value, filter_term)
    results = lax.map(one_sequence, (query, key_act, value_act, grad_out))
    grad_filter = lax.optimization_barrier(jnp.sum(results[4], axis=0)) / math.sqrt(SEQ * BATCH)
    return (results[0], results[1], results[2], results[3], grad_filter)
```

```python
import functools
import math

import jax
import jax.numpy as jnp
import numpy as np
from jax import lax
from jax.experimental import pallas as pl
from jax.experimental.pallas import tpu as pltpu
from jax.sharding import PartitionSpec as P

MESH = pl.DeviceIdType.MESH
LANES = 128
RADIX = 64
HALF = RADIX // 2
KEPT = HALF + 1


def turn(value, numerator, denominator):
    real, imag = value
    numerator %= denominator
    eighth = numerator * 8
    if eighth % denominator == 0:
        step = eighth // denominator
        if step == 0:
            return (real, imag)
        if step == 2:
            return (imag, -real)
        if step == 4:
            return (-real, -imag)
        if step == 6:
            return (-imag, real)
        root = math.sqrt(0.5)
        if step == 1:
            return ((real + imag) * root, (imag - real) * root)
        if step == 3:
            return ((imag - real) * root, (real + imag) * -root)
        if step == 5:
            return ((real + imag) * -root, (real - imag) * root)
        return ((real - imag) * root, (real + imag) * root)
    cos = math.cos(2.0 * math.pi * numerator / denominator)
    sin = math.sin(2.0 * math.pi * numerator / denominator)
    return (real * cos + imag * sin, imag * cos - real * sin)


def complex_fft(values, sign):
    size = len(values)
    if size == 1:
        return values
    even = complex_fft(values[0::2], sign)
    odd = complex_fft(values[1::2], sign)
    low, high = [], []
    for k in range(size // 2):
        real, imag = turn(odd[k], sign * k, size)
        low.append((even[k][0] + real, even[k][1] + imag))
        high.append((even[k][0] - real, even[k][1] - imag))
    return low + high


def odd_forward(values):
    quarter = len(values) // 2
    order = 4 * quarter
    packed = [turn((values[n], -values[n + quarter]), n, order) for n in range(quarter)]
    out = complex_fft(packed, 1)
    found = {}
    for j in range(quarter):
        k = 4 * j + 1
        if k < order // 2:
            found[k] = out[j]
        else:
            found[order - k] = (out[j][0], -out[j][1])
    return found


def real_forward(values):
    size = len(values)
    if size == 2:
        return {0: (values[0] + values[1], None), 1: (values[0] - values[1], None)}
    half = size // 2
    evens = real_forward([values[n] + values[n + half] for n in range(half)])
    found = {2 * k: value for k, value in evens.items()}
    found.update(odd_forward([values[n] - values[n + half] for n in range(half)]))
    return found


def padded_forward(values):
    found = {2 * k: value for k, value in real_forward(values).items()}
    found.update(odd_forward(values))
    return found


def odd_inverse(found, order):
    quarter = order // 4
    packed = []
    for j in range(quarter):
        k = 4 * j + 1
        if k < order // 2:
            packed.append(found[k])
        else:
            real, imag = found[order - k]
            packed.append((real, -imag))
    out = complex_fft(packed, -1)
    out = [turn(out[n], -n, order) for n in range(quarter)]
    return [value[0] for value in out] + [-value[1] for value in out]


def real_inverse(found, size):
    if size == 2:
        return [found[0][0] + found[1][0], found[0][0] - found[1][0]]
    half = size // 2
    evens = real_inverse({k // 2: value for k, value in found.items() if k % 2 == 0}, half)
    odds = odd_inverse(found, size)
    return [evens[n] + odds[n] for n in range(half)] + [evens[n] - odds[n] for n in range(half)]


def padded_inverse(found):
    evens = real_inverse({k // 2: value for k, value in found.items() if k % 2 == 0}, HALF)
    odds = odd_inverse(found, RADIX)
    return [evens[n] + odds[n] for n in range(HALF)]


def tables():
    k = np.arange(LANES)
    angles = 2.0 * np.pi * (k[:, None] * k[None, :] % LANES) / LANES
    cos, sin = np.cos(angles), np.sin(angles)
    forward = np.block([[cos, -sin], [sin, cos]])
    inverse = forward.T

    def split(matrix):
        high = matrix.astype(np.float32).astype(jnp.bfloat16)
        low = (matrix - high.astype(np.float64)).astype(np.float32).astype(jnp.bfloat16)
        return high, low

    matrices = np.stack([*split(forward), *split(inverse)])
    length = RADIX * LANES
    first = np.arange(KEPT)
    angles = 2.0 * np.pi * (first[:, None] * k[None, :]) / length
    scale = np.where((first == 0) | (first == HALF), 1.0, 2.0)[:, None] / length
    twists = np.stack(
        [np.cos(angles), np.sin(angles), np.cos(angles) * scale, np.sin(angles) * scale]
    ).astype(np.float32)
    return matrices, twists


CHUNKS = 2


def body(
    ctx,
    dp,
    q_ref,
    k_ref,
    v_ref,
    g_ref,
    f_ref,
    w_ref,
    t_ref,
    out_ref,
    gq_ref,
    gk_ref,
    gv_ref,
    gf_ref,
    send_x,
    recv_x,
    send_y,
    recv_y,
    part_g,
    recv_g,
    own_g,
    swap_g,
    spec_a,
    spec_b,
    sx_send,
    sx_recv,
    sf_send,
    sf_recv,
    sy_send,
    sy_recv,
    sg_send,
    sg_recv,
    sp_send,
    sp_recv,
    sa_send,
    sa_recv,
):
    me_c = lax.axis_index("ctx")
    me_d = lax.axis_index("dp")
    share = q_ref.shape[0] // ctx
    rows = share // CHUNKS
    subs = rows // 8
    width = q_ref.shape[1]

    barrier = pltpu.get_barrier_semaphore()

    def greet_ctx(i, carry):
        pl.semaphore_signal(
            barrier, inc=1, device_id=(me_d, (me_c + i) % ctx), device_id_type=MESH
        )
        return carry

    def greet_dp(i, carry):
        pl.semaphore_signal(
            barrier, inc=1, device_id=((me_d + i) % dp, me_c), device_id_type=MESH
        )
        return carry

    lax.fori_loop(1, ctx, greet_ctx, 0)
    lax.fori_loop(1, dp, greet_dp, 0)

    @pl.when(me_c != me_d)
    def _():
        pl.semaphore_signal(barrier, inc=1, device_id=(me_c, me_d), device_id_type=MESH)

    def products(b, carry):
        for ck in range(CHUNKS):
            at = pl.ds(b * share + ck * rows, rows)
            send_x[ck, 0, b] = k_ref[at, :].astype(jnp.float32) * v_ref[at, :].astype(jnp.float32)
            send_x[ck, 1, b] = q_ref[at, :].astype(jnp.float32) * g_ref[at, :].astype(jnp.float32)
        return carry

    lax.fori_loop(0, ctx, products, 0)
    for ck in range(CHUNKS):
        recv_x[ck, 0, me_c] = send_x[ck, 0, me_c]
        recv_x[ck, 1, me_c] = send_x[ck, 1, me_c]
        recv_x[ck, 2, me_c] = f_ref[pl.ds(me_c * share + ck * rows, rows), :]

    @pl.when(me_c != me_d)
    def _():
        pl.semaphore_wait(barrier, ctx + dp - 1)

    @pl.when(me_c == me_d)
    def _():
        pl.semaphore_wait(barrier, ctx + dp - 2)

    def copy_x(ck, i):
        peer = (me_c + i) % ctx
        return pltpu.make_async_remote_copy(
            src_ref=send_x.at[ck, :, peer],
            dst_ref=recv_x.at[ck, pl.ds(0, 2), me_c],
            send_sem=sx_send.at[ck, i],
            recv_sem=sx_recv.at[ck, i],
            device_id=(me_d, peer),
            device_id_type=MESH,
        )

    def copy_f(ck, i):
        peer = (me_c + i) % ctx
        return pltpu.make_async_remote_copy(
            src_ref=f_ref.at[pl.ds(peer * share + ck * rows, rows), :],
            dst_ref=recv_x.at[ck, 2, me_c],
            send_sem=sf_send.at[ck, i],
            recv_sem=sf_recv.at[ck, i],
            device_id=(me_d, peer),
            device_id_type=MESH,
        )

    def copy_y(ck, i):
        peer = (me_c + i) % ctx
        return pltpu.make_async_remote_copy(
            src_ref=send_y.at[ck, :, peer],
            dst_ref=recv_y.at[ck, :, me_c],
            send_sem=sy_send.at[ck, i],
            recv_sem=sy_recv.at[ck, i],
            device_id=(me_d, peer),
            device_id_type=MESH,
        )

    def copy_g(ck, i):
        peer = (me_d + i) % dp
        return pltpu.make_async_remote_copy(
            src_ref=part_g.at[ck, peer],
            dst_ref=recv_g.at[ck, i],
            send_sem=sg_send.at[ck, i],
            recv_sem=sg_recv.at[ck, i],
            device_id=(peer, me_c),
            device_id_type=MESH,
        )

    def copy_a(i):
        peer = (me_d + i) % dp
        return pltpu.make_async_remote_copy(
            src_ref=swap_g,
            dst_ref=gf_ref.at[me_d],
            send_sem=sa_send.at[i],
            recv_sem=sa_recv.at[i],
            device_id=(peer, me_c),
            device_id_type=MESH,
        )

    swap = pltpu.make_async_remote_copy(
        src_ref=own_g,
        dst_ref=swap_g,
        send_sem=sp_send.at[0],
        recv_sem=sp_recv.at[0],
        device_id=(me_c, me_d),
        device_id_type=MESH,
    )

    def each(count, act):
        def step(i, carry):
            act(i)
            return carry

        lax.fori_loop(1, count, step, 0)

    for ck in range(CHUNKS):
        each(ctx, lambda i: copy_x(ck, i).start())
        each(ctx, lambda i: copy_f(ck, i).start())

    def matmul(sig, which):
        data = spec_a[sig]
        high = data.astype(jnp.bfloat16)
        low = (data - high.astype(jnp.float32)).astype(jnp.bfloat16)
        w_high = w_ref[2 * which]
        w_low = w_ref[2 * which + 1]
        spec_b[sig] = (
            jnp.dot(high, w_high, preferred_element_type=jnp.float32)
            + jnp.dot(low, w_high, preferred_element_type=jnp.float32)
            + jnp.dot(high, w_low, preferred_element_type=jnp.float32)
        )

    def chunk(ck):
        each(ctx, lambda i: copy_x(ck, i).wait_recv())
        each(ctx, lambda i: copy_f(ck, i).wait_recv())

        def forward(step, carry):
            sig, sub = step // subs, step % subs
            at = pl.ds(sub * 8, 8)
            values = [
                recv_x[ck, sig, n // 2, at, pl.ds((n % 2) * LANES, LANES)] for n in range(HALF)
            ]
            found = padded_forward(values)
            for k in range(KEPT):
                cos, sin = t_ref[0, pl.ds(k, 1), :], t_ref[1, pl.ds(k, 1), :]
                real, imag = found[k]
                to = pl.ds(k * rows + sub * 8, 8)
                if k == 0:
                    spec_a[sig, to, pl.ds(0, LANES)] = real
                    spec_a[sig, to, pl.ds(LANES, LANES)] = jnp.zeros_like(real)
                elif imag is None:
                    spec_a[sig, to, pl.ds(0, LANES)] = real * cos
                    spec_a[sig, to, pl.ds(LANES, LANES)] = -(real * sin)
                else:
                    spec_a[sig, to, pl.ds(0, LANES)] = real * cos + imag * sin
                    spec_a[sig, to, pl.ds(LANES, LANES)] = imag * cos - real * sin
            return carry

        lax.fori_loop(0, 3 * subs, forward, 0)
        lax.fori_loop(0, 3, lambda sig, carry: (matmul(sig, 0), carry)[1], 0)

        def pointwise(k, carry):
            at = pl.ds(k * rows, rows)
            re, im = pl.ds(0, LANES), pl.ds(LANES, LANES)
            z_re, z_im = spec_b[0, at, re], spec_b[0, at, im]
            d_re, d_im = spec_b[1, at, re], spec_b[1, at, im]
            f_re, f_im = spec_b[2, at, re], spec_b[2, at, im]
            spec_a[0, at, re] = z_re * f_re - z_im * f_im
            spec_a[0, at, im] = z_re * f_im + z_im * f_re
            spec_a[1, at, re] = f_re * d_re + f_im * d_im
            spec_a[1, at, im] = f_re * d_im - f_im * d_re
            spec_a[2, at, re] = z_re * d_re + z_im * d_im
            spec_a[2, at, im] = z_re * d_im - z_im * d_re
            return carry

        lax.fori_loop(0, KEPT, pointwise, 0)
        lax.fori_loop(0, 3, lambda sig, carry: (matmul(sig, 1), carry)[1], 0)

        def inverse(sig, sub, store):
            found = {}
            for k in range(KEPT):
                cos, sin = t_ref[2, pl.ds(k, 1), :], t_ref[3, pl.ds(k, 1), :]
                at = pl.ds(k * rows + sub * 8, 8)
                real = spec_b[sig, at, pl.ds(0, LANES)]
                imag = spec_b[sig, at, pl.ds(LANES, LANES)]
                if k == 0 or k == HALF:
                    found[k] = (real * cos - imag * sin, None)
                else:
                    found[k] = (real * cos - imag * sin, imag * cos + real * sin)
            values = padded_inverse(found)
            for n in range(HALF):
                store(n // 2, pl.ds(sub * 8, 8), pl.ds((n % 2) * LANES, LANES), values[n])

        def back_y(step, carry):
            sig, sub = step // subs, step % subs

            def store(block, at, lanes, value):
                send_y[ck, sig, block, at, lanes] = value

            inverse(sig, sub, store)
            return carry

        def back_g(sub, carry):
            def store(block, at, lanes, value):
                part_g[ck, block, at, lanes] = value

            inverse(2, sub, store)
            return carry

        lax.fori_loop(0, subs, back_g, 0)
        each(dp, lambda i: copy_g(ck, i).start())
        lax.fori_loop(0, 2 * subs, back_y, 0)
        each(ctx, lambda i: copy_y(ck, i).start())
        recv_y[ck, 0, me_c] = send_y[ck, 0, me_c]
        recv_y[ck, 1, me_c] = send_y[ck, 1, me_c]

    for ck in range(CHUNKS):
        chunk(ck)

    scale = 1.0 / math.sqrt(dp * ctx * width)
    for ck in range(CHUNKS):
        each(dp, lambda i: copy_g(ck, i).wait_recv())
        total = part_g[ck, me_d]
        for i in range(1, dp):
            total = total + recv_g[ck, i]
        own_g[pl.ds(ck * rows, rows), :] = total * scale

    @pl.when(me_c != me_d)
    def _():
        swap.start()
        swap.wait()

    @pl.when(me_c == me_d)
    def _():
        swap_g[...] = own_g[...]

    each(dp, lambda i: copy_a(i).start())
    gf_ref[me_d] = swap_g[...]

    for ck in range(CHUNKS):
        each(ctx, lambda i: copy_y(ck, i).wait_recv())

        def outputs(b, carry):
            at = pl.ds(b * share + ck * rows, rows)
            conv = recv_y[ck, 0, b]
            dmixed = recv_y[ck, 1, b]
            out_ref[at, :] = (q_ref[at, :].astype(jnp.float32) * conv).astype(jnp.bfloat16)
            gq_ref[at, :] = (g_ref[at, :].astype(jnp.float32) * conv).astype(jnp.bfloat16)
            gk_ref[at, :] = (v_ref[at, :].astype(jnp.float32) * dmixed).astype(jnp.bfloat16)
            gv_ref[at, :] = (k_ref[at, :].astype(jnp.float32) * dmixed).astype(jnp.bfloat16)
            return carry

        lax.fori_loop(0, ctx, outputs, 0)

    each(dp, lambda i: copy_a(i).wait_recv())
    for ck in range(CHUNKS):
        each(ctx, lambda i: copy_x(ck, i).wait_send())
        each(ctx, lambda i: copy_f(ck, i).wait_send())
        each(ctx, lambda i: copy_y(ck, i).wait_send())
        each(dp, lambda i: copy_g(ck, i).wait_send())
    each(dp, lambda i: copy_a(i).wait_send())


def shards(ctx, dp, query, key_act, value_act, filter_taps, grad_out):
    _, channels, width = query.shape
    share = channels // ctx
    rows = share // CHUNKS
    matrices, twists = tables()
    vmem = pl.BlockSpec(memory_space=pltpu.VMEM)
    half = jax.ShapeDtypeStruct((channels, width), jnp.bfloat16)
    dma = pltpu.SemaphoreType.DMA
    outs = pl.pallas_call(
        functools.partial(body, ctx, dp),
        out_shape=[half] * 4 + [jax.ShapeDtypeStruct((dp, share, width), jnp.float32)],
        in_specs=[vmem] * 7,
        out_specs=[vmem] * 5,
        scratch_shapes=[
            pltpu.VMEM((CHUNKS, 2, ctx, rows, width), jnp.float32),
            pltpu.VMEM((CHUNKS, 3, ctx, rows, width), jnp.float32),
            pltpu.VMEM((CHUNKS, 2, ctx, rows, width), jnp.float32),
            pltpu.VMEM((CHUNKS, 2, ctx, rows, width), jnp.float32),
            pltpu.VMEM((CHUNKS, ctx, rows, width), jnp.float32),
            pltpu.VMEM((CHUNKS, dp, rows, width), jnp.float32),
            pltpu.VMEM((share, width), jnp.float32),
            pltpu.VMEM((share, width), jnp.float32),
            pltpu.VMEM((3, KEPT * rows, 2 * LANES), jnp.float32),
            pltpu.VMEM((3, KEPT * rows, 2 * LANES), jnp.float32),
            dma((CHUNKS, ctx)),
            dma((CHUNKS, ctx)),
            dma((CHUNKS, ctx)),
            dma((CHUNKS, ctx)),
            dma((CHUNKS, ctx)),
            dma((CHUNKS, ctx)),
            dma((CHUNKS, dp)),
            dma((CHUNKS, dp)),
            dma((1,)),
            dma((1,)),
            dma((dp,)),
            dma((dp,)),
        ],
        compiler_params=pltpu.CompilerParams(
            collective_id=0, has_side_effects=True, vmem_limit_bytes=40 * 1024 * 1024
        ),
        cost_estimate=pl.CostEstimate(
            flops=3 * 2 * 6 * KEPT * share * 256 * 256, bytes_accessed=4 * 2**20, transcendentals=0
        ),
    )(
        query.reshape(channels, width),
        key_act.reshape(channels, width),
        value_act.reshape(channels, width),
        grad_out.reshape(channels, width),
        filter_taps,
        jnp.asarray(matrices),
        jnp.asarray(twists),
    )
    shape = query.shape
    return (
        outs[0].reshape(shape),
        outs[1].reshape(shape),
        outs[2].reshape(shape),
        outs[3].reshape(shape),
        outs[4].reshape(channels, width),
    )


def solution(mesh):
    row = P("dp", None, "ctx")
    taps = P(None, "ctx")
    return jax.shard_map(
        functools.partial(shards, mesh.shape["ctx"], mesh.shape["dp"]),
        mesh=mesh,
        in_specs=(row, row, row, taps, row),
        out_specs=(row, row, row, row, taps),
        check_vma=False,
    )
```

```python
import functools
import math

import jax
import jax.numpy as jnp
import numpy as np
from jax import lax
from jax.experimental import pallas as pl
from jax.experimental.pallas import tpu as pltpu
from jax.sharding import PartitionSpec as P

MESH = pl.DeviceIdType.MESH
LANES = 128
RADIX = 64
HALF = RADIX // 2
KEPT = HALF + 1


def turn(value, numerator, denominator):
    real, imag = value
    numerator %= denominator
    eighth = numerator * 8
    if eighth % denominator == 0:
        step = eighth // denominator
        if step == 0:
            return (real, imag)
        if step == 2:
            return (imag, -real)
        if step == 4:
            return (-real, -imag)
        if step == 6:
            return (-imag, real)
        root = math.sqrt(0.5)
        if step == 1:
            return ((real + imag) * root, (imag - real) * root)
        if step == 3:
            return ((imag - real) * root, (real + imag) * -root)
        if step == 5:
            return ((real + imag) * -root, (real - imag) * root)
        return ((real - imag) * root, (real + imag) * root)
    cos = math.cos(2.0 * math.pi * numerator / denominator)
    sin = math.sin(2.0 * math.pi * numerator / denominator)
    return (real * cos + imag * sin, imag * cos - real * sin)


def complex_fft(values, sign):
    size = len(values)
    if size == 1:
        return values
    even = complex_fft(values[0::2], sign)
    odd = complex_fft(values[1::2], sign)
    low, high = [], []
    for k in range(size // 2):
        real, imag = turn(odd[k], sign * k, size)
        low.append((even[k][0] + real, even[k][1] + imag))
        high.append((even[k][0] - real, even[k][1] - imag))
    return low + high


def odd_forward(values):
    quarter = len(values) // 2
    order = 4 * quarter
    packed = [turn((values[n], -values[n + quarter]), n, order) for n in range(quarter)]
    out = complex_fft(packed, 1)
    found = {}
    for j in range(quarter):
        k = 4 * j + 1
        if k < order // 2:
            found[k] = out[j]
        else:
            found[order - k] = (out[j][0], -out[j][1])
    return found


def real_forward(values):
    size = len(values)
    if size == 2:
        return {0: (values[0] + values[1], None), 1: (values[0] - values[1], None)}
    half = size // 2
    evens = real_forward([values[n] + values[n + half] for n in range(half)])
    found = {2 * k: value for k, value in evens.items()}
    found.update(odd_forward([values[n] - values[n + half] for n in range(half)]))
    return found


def padded_forward(values):
    found = {2 * k: value for k, value in real_forward(values).items()}
    found.update(odd_forward(values))
    return found


def odd_inverse(found, order):
    quarter = order // 4
    packed = []
    for j in range(quarter):
        k = 4 * j + 1
        if k < order // 2:
            packed.append(found[k])
        else:
            real, imag = found[order - k]
            packed.append((real, -imag))
    out = complex_fft(packed, -1)
    out = [turn(out[n], -n, order) for n in range(quarter)]
    return [value[0] for value in out] + [-value[1] for value in out]


def real_inverse(found, size):
    if size == 2:
        return [found[0][0] + found[1][0], found[0][0] - found[1][0]]
    half = size // 2
    evens = real_inverse({k // 2: value for k, value in found.items() if k % 2 == 0}, half)
    odds = odd_inverse(found, size)
    return [evens[n] + odds[n] for n in range(half)] + [evens[n] - odds[n] for n in range(half)]


def padded_inverse(found):
    evens = real_inverse({k // 2: value for k, value in found.items() if k % 2 == 0}, HALF)
    odds = odd_inverse(found, RADIX)
    return [evens[n] + odds[n] for n in range(HALF)]


def tables():
    k = np.arange(LANES)
    angles = 2.0 * np.pi * (k[:, None] * k[None, :] % LANES) / LANES
    cos, sin = np.cos(angles), np.sin(angles)
    forward = np.block([[cos, -sin], [sin, cos]])
    inverse = forward.T

    def split(matrix):
        high = matrix.astype(np.float32).astype(jnp.bfloat16)
        low = (matrix - high.astype(np.float64)).astype(np.float32).astype(jnp.bfloat16)
        return high, low

    matrices = np.stack([*split(forward), *split(inverse)])
    length = RADIX * LANES
    first = np.arange(KEPT)
    angles = 2.0 * np.pi * (first[:, None] * k[None, :]) / length
    scale = np.where((first == 0) | (first == HALF), 1.0, 2.0)[:, None] / length
    twists = np.stack(
        [np.cos(angles), np.sin(angles), np.cos(angles) * scale, np.sin(angles) * scale]
    ).astype(np.float32)
    return matrices, twists


CHUNKS = 2
PLANES = 2
GRANT = 60 * 1024 * 1024


def body(
    ctx,
    dp,
    q_hbm,
    k_hbm,
    v_hbm,
    g_hbm,
    f_hbm,
    w_hbm,
    t_hbm,
    out_hbm,
    gq_hbm,
    gk_hbm,
    gv_hbm,
    gf_ref,
    out_ref,
    gq_ref,
    gk_ref,
    gv_ref,
    q_ref,
    k_ref,
    v_ref,
    g_ref,
    w_ref,
    t_ref,
    send_x,
    recv_x,
    send_y,
    recv_y,
    part_g,
    recv_g,
    sum_g,
    recv_s,
    own_s,
    spec_a,
    spec_b,
    load_sem,
    save_sem,
    own_sem,
    keep_sem,
    sx_send,
    sx_recv,
    sf_send,
    sf_recv,
    sy_send,
    sy_recv,
    sg_send,
    sg_recv,
    ss_send,
    ss_recv,
    sa_send,
    sa_recv,
):
    me_c = lax.axis_index("ctx")
    me_d = lax.axis_index("dp")
    ring = dp // PLANES
    channels, width = q_ref.shape
    share = channels // ctx
    rows = share // CHUNKS
    subs = rows // 8
    me_p, me_z = me_d // ring, lax.rem(me_d, ring)
    c_p, c_z = me_c // ring, lax.rem(me_c, ring)

    loads = [
        pltpu.make_async_copy(src, dst, load_sem.at[n])
        for n, (src, dst) in enumerate(
            [
                (k_hbm, k_ref),
                (v_hbm, v_ref),
                (q_hbm, q_ref),
                (g_hbm, g_ref),
                (w_hbm, w_ref),
                (t_hbm, t_ref),
            ]
        )
    ]
    for load in loads:
        load.start()

    def each(first, last, act):
        def step(i, carry):
            act(i)
            return carry

        lax.fori_loop(first, last, step, 0, unroll=True)

    def ctx_peer(i):
        return (me_d, lax.rem(me_c + i, ctx))

    def ring_peer(i):
        return (me_p * ring + lax.rem(me_z + i, ring), me_c)

    def swap_peer(plane, part):
        return (plane * ring + c_z, part * ring + me_z)

    def is_self(plane, part):
        return (c_z == me_z) & (plane == me_p) & (part == c_p)

    barrier = pltpu.get_barrier_semaphore()

    def greet(peer):
        pl.semaphore_signal(barrier, inc=1, device_id=peer, device_id_type=MESH)

    each(1, ctx, lambda i: greet(ctx_peer(i)))
    each(1, ring, lambda i: greet(ring_peer(i)))
    swaps = [(plane, part) for plane in range(PLANES) for part in range(PLANES)]
    for plane, part in swaps:
        pl.when(jnp.logical_not(is_self(plane, part)))(
            functools.partial(greet, swap_peer(plane, part))
        )

    for load in loads[:4]:
        load.wait()

    def products(b, carry):
        at = pl.ds(b * share, share)
        mixed = k_ref[at, :].astype(jnp.float32) * v_ref[at, :].astype(jnp.float32)
        dconv = q_ref[at, :].astype(jnp.float32) * g_ref[at, :].astype(jnp.float32)
        for ck in range(CHUNKS):
            send_x[ck, 0, b] = mixed[ck * rows : (ck + 1) * rows]
            send_x[ck, 1, b] = dconv[ck * rows : (ck + 1) * rows]
        return carry

    lax.fori_loop(0, ctx, products, 0)

    met = ctx - 1 + ring - 1 + len(swaps)

    @pl.when(c_z == me_z)
    def _():
        pl.semaphore_wait(barrier, met - 1)

    @pl.when(c_z != me_z)
    def _():
        pl.semaphore_wait(barrier, met)

    def remote(src, dst, send, recv, peer):
        return pltpu.make_async_remote_copy(
            src_ref=src,
            dst_ref=dst,
            send_sem=send,
            recv_sem=recv,
            device_id=peer,
            device_id_type=MESH,
        )

    def copy_x(ck, i):
        peer = ctx_peer(i)
        return remote(
            send_x.at[ck, :, peer[1]],
            recv_x.at[ck, pl.ds(0, 2), me_c],
            sx_send.at[ck],
            sx_recv.at[ck],
            peer,
        )

    def copy_f(ck, i):
        peer = ctx_peer(i)
        return remote(
            f_hbm.at[pl.ds(peer[1] * share + ck * rows, rows), :],
            recv_x.at[ck, 2, me_c],
            sf_send.at[ck],
            sf_recv.at[ck],
            peer,
        )

    def own_f(ck):
        return pltpu.make_async_copy(
            f_hbm.at[pl.ds(me_c * share + ck * rows, rows), :],
            recv_x.at[ck, 2, me_c],
            own_sem.at[ck],
        )

    def copy_y(ck, i):
        peer = ctx_peer(i)
        return remote(
            send_y.at[ck, :, peer[1]],
            recv_y.at[ck, :, me_c],
            sy_send.at[ck],
            sy_recv.at[ck],
            peer,
        )

    def copy_g(ck, i):
        peer = ring_peer(i)
        return remote(
            part_g.at[ck, :, lax.rem(me_z + i, ring)],
            recv_g.at[ck, i - 1],
            sg_send.at[ck],
            sg_recv.at[ck],
            peer,
        )

    def copy_s(ck, plane, part):
        return remote(
            sum_g.at[ck, part],
            recv_s.at[ck, c_p, me_p],
            ss_send.at[ck, plane, part],
            ss_recv.at[ck, c_p, me_p],
            swap_peer(plane, part),
        )

    def copy_a(ck, i):
        return remote(
            own_s.at[ck],
            gf_ref.at[:, me_z, ck],
            sa_send.at[ck],
            sa_recv.at[ck],
            ring_peer(i),
        )

    def keep(ck):
        return pltpu.make_async_copy(own_s.at[ck], gf_ref.at[:, me_z, ck], keep_sem.at[ck])

    def drain(ref, sem):
        pltpu.make_async_copy(ref, ref, sem).wait()

    def chunks(act):
        def step(ck, carry):
            act(ck)
            return carry

        lax.fori_loop(0, CHUNKS, step, 0)

    chunks(lambda ck: each(1, ctx, lambda i: copy_x(ck, i).start()))

    def first_f(ck):
        each(1, ctx, lambda i: copy_f(ck, i).start())
        own_f(ck).start()

    chunks(first_f)

    def own_x(ck):
        recv_x[ck, 0, me_c] = send_x[ck, 0, me_c]
        recv_x[ck, 1, me_c] = send_x[ck, 1, me_c]

    chunks(own_x)
    for load in loads[4:]:
        load.wait()

    re, im = pl.ds(0, LANES), pl.ds(LANES, LANES)

    def forward(ck, sig, sub):
        at = pl.ds(sub * 8, 8)
        values = [
            recv_x[ck, sig, n // 2, at, pl.ds((n % 2) * LANES, LANES)] for n in range(HALF)
        ]
        found = padded_forward(values)
        for k in range(KEPT):
            cos, sin = t_ref[0, pl.ds(k, 1), :], t_ref[1, pl.ds(k, 1), :]
            real, imag = found[k]
            to = pl.ds(k * rows + sub * 8, 8)
            if k == 0:
                spec_a[sig, to, re] = real
                spec_a[sig, to, im] = jnp.zeros_like(real)
            elif imag is None:
                spec_a[sig, to, re] = real * cos
                spec_a[sig, to, im] = -(real * sin)
            else:
                spec_a[sig, to, re] = real * cos + imag * sin
                spec_a[sig, to, im] = imag * cos - real * sin

    def inverse(ck, sig, sub, store):
        found = {}
        for k in range(KEPT):
            cos, sin = t_ref[2, pl.ds(k, 1), :], t_ref[3, pl.ds(k, 1), :]
            at = pl.ds(k * rows + sub * 8, 8)
            real = spec_a[sig, at, re]
            imag = spec_a[sig, at, im]
            if k == 0 or k == HALF:
                found[k] = (real * cos - imag * sin, None)
            else:
                found[k] = (real * cos - imag * sin, imag * cos + real * sin)
        values = padded_inverse(found)
        for n in range(HALF):
            store(n // 2, pl.ds(sub * 8, 8), pl.ds((n % 2) * LANES, LANES), values[n])

    def matmul(src, dst, which):
        data = src[...]
        high = data.astype(jnp.bfloat16)
        low = (data - high.astype(jnp.float32)).astype(jnp.bfloat16)
        w_high = w_ref[2 * which]
        w_low = w_ref[2 * which + 1]
        dst[...] = (
            jnp.dot(high, w_high, preferred_element_type=jnp.float32)
            + jnp.dot(low, w_high, preferred_element_type=jnp.float32)
            + jnp.dot(high, w_low, preferred_element_type=jnp.float32)
        )

    def loop(count, act, unroll=1):
        def step(i, carry):
            act(i)
            return carry

        lax.fori_loop(0, count, step, 0, unroll=unroll)

    def filter_grad(ck):
        drain(recv_x.at[ck, pl.ds(0, 2), pl.ds(0, ctx - 1)], sx_recv.at[ck])
        loop(2 * subs, lambda n: forward(ck, n // subs, lax.rem(n, subs)))
        loop(2, lambda sig: matmul(spec_a.at[sig], spec_b.at[ck, sig], 0))

        def pointwise(k):
            at = pl.ds(k * rows, rows)
            z_re, z_im = spec_b[ck, 0, at, re], spec_b[ck, 0, at, im]
            d_re, d_im = spec_b[ck, 1, at, re], spec_b[ck, 1, at, im]
            spec_a[0, at, re] = z_re * d_re + z_im * d_im
            spec_a[0, at, im] = z_re * d_im - z_im * d_re

        loop(KEPT, pointwise, 3)
        matmul(spec_a.at[0], spec_a.at[1], 1)

        def store(block, at, lanes, value):
            part_g[ck, block // ring, block % ring, at, lanes] = value

        loop(subs, lambda sub: inverse(ck, 1, sub, store))
        each(1, ring, lambda i: copy_g(ck, i).start())

    def convolutions(ck):
        drain(recv_x.at[ck, 2, pl.ds(0, ctx - 1)], sf_recv.at[ck])
        own_f(ck).wait()
        loop(subs, lambda sub: forward(ck, 2, sub))
        matmul(spec_a.at[2], spec_b.at[ck, 2], 0)

        def pointwise(k):
            at = pl.ds(k * rows, rows)
            z_re, z_im = spec_b[ck, 0, at, re], spec_b[ck, 0, at, im]
            d_re, d_im = spec_b[ck, 1, at, re], spec_b[ck, 1, at, im]
            f_re, f_im = spec_b[ck, 2, at, re], spec_b[ck, 2, at, im]
            spec_a[0, at, re] = z_re * f_re - z_im * f_im
            spec_a[0, at, im] = z_re * f_im + z_im * f_re
            spec_a[1, at, re] = f_re * d_re + f_im * d_im
            spec_a[1, at, im] = f_re * d_im - f_im * d_re

        loop(KEPT, pointwise, 3)
        loop(2, lambda sig: matmul(spec_a.at[sig], spec_a.at[sig], 1))

        def back(n):
            sig, sub = n // subs, lax.rem(n, subs)

            def store(block, at, lanes, value):
                send_y[ck, sig, block, at, lanes] = value

            inverse(ck, sig, sub, store)

        loop(2 * subs, back)
        each(1, ctx, lambda i: copy_y(ck, i).start())
        recv_y[ck, 0, me_c] = send_y[ck, 0, me_c]
        recv_y[ck, 1, me_c] = send_y[ck, 1, me_c]

        drain(recv_g.at[ck], sg_recv.at[ck])
        for part in range(PLANES):
            total = part_g[ck, part, me_z]
            for i in range(ring - 1):
                total = total + recv_g[ck, i, part]
            sum_g[ck, part] = total
        for plane, part in swaps:
            mine = is_self(plane, part)

            @pl.when(jnp.logical_not(mine))
            def _():
                copy_s(ck, plane, part).start()

            @pl.when(mine)
            def _():
                recv_s[ck, part, plane] = sum_g[ck, part]

    chunks(filter_grad)
    chunks(convolutions)

    scale = 1.0 / math.sqrt(dp * ctx * width)

    def gather(ck):
        for plane, part in swaps:

            @pl.when(jnp.logical_not(is_self(plane, part)))
            def _():
                drain(recv_s.at[ck, part, plane], ss_recv.at[ck, part, plane])

        for part in range(PLANES):
            total = recv_s[ck, part, 0]
            for plane in range(1, PLANES):
                total = total + recv_s[ck, part, plane]
            own_s[ck, part] = total * scale
        each(1, ring, lambda i: copy_a(ck, i).start())
        keep(ck).start()

    chunks(gather)

    for ck in range(CHUNKS):
        drain(recv_y.at[ck, :, pl.ds(0, ctx - 1)], sy_recv.at[ck])

    def outputs(b):
        at = pl.ds(b * share, share)
        conv = jnp.concatenate([recv_y[ck, 0, b] for ck in range(CHUNKS)], axis=0)
        dmixed = jnp.concatenate([recv_y[ck, 1, b] for ck in range(CHUNKS)], axis=0)
        out_ref[at, :] = (q_ref[at, :].astype(jnp.float32) * conv).astype(jnp.bfloat16)
        gq_ref[at, :] = (g_ref[at, :].astype(jnp.float32) * conv).astype(jnp.bfloat16)
        gk_ref[at, :] = (v_ref[at, :].astype(jnp.float32) * dmixed).astype(jnp.bfloat16)
        gv_ref[at, :] = (k_ref[at, :].astype(jnp.float32) * dmixed).astype(jnp.bfloat16)

    loop(ctx, outputs)
    saves = [
        pltpu.make_async_copy(src, dst, save_sem.at[n])
        for n, (src, dst) in enumerate(
            [(out_ref, out_hbm), (gq_ref, gq_hbm), (gk_ref, gk_hbm), (gv_ref, gv_hbm)]
        )
    ]
    for save in saves:
        save.start()

    def finish(ck):
        drain(recv_x.at[ck, pl.ds(0, 2), pl.ds(0, ctx - 1)], sx_send.at[ck])
        drain(recv_x.at[ck, 2, pl.ds(0, ctx - 1)], sf_send.at[ck])
        drain(recv_y.at[ck, :, pl.ds(0, ctx - 1)], sy_send.at[ck])
        drain(recv_g.at[ck], sg_send.at[ck])
        for plane, part in swaps:

            @pl.when(jnp.logical_not(is_self(plane, part)))
            def _():
                drain(sum_g.at[ck, part], ss_send.at[ck, plane, part])

        keep(ck).wait()
        drain(gf_ref.at[:, pl.ds(0, ring - 1), ck], sa_send.at[ck])
        drain(gf_ref.at[:, pl.ds(0, ring - 1), ck], sa_recv.at[ck])

    chunks(finish)
    for save in saves:
        save.wait()


def write_out(count, *refs):
    sources, targets, sem = refs[:count], refs[count:-1], refs[-1]
    copies = [
        pltpu.make_async_copy(sources[n], targets[n], sem.at[n]) for n in range(count)
    ]
    for copy in copies:
        copy.start()
    for copy in copies:
        copy.wait()


def shards(ctx, dp, query, key_act, value_act, filter_taps, grad_out):
    _, channels, width = query.shape
    share = channels // ctx
    rows = share // CHUNKS
    ring = dp // PLANES
    matrices, twists = tables()
    hbm = pl.BlockSpec(memory_space=pltpu.HBM)
    half = jax.ShapeDtypeStruct((channels, width), jnp.bfloat16)
    whole = jax.ShapeDtypeStruct((PLANES, ring, CHUNKS, rows, width), jnp.float32)
    dma = pltpu.SemaphoreType.DMA
    full = pltpu.VMEM((channels, width), jnp.bfloat16)
    outs = pl.pallas_call(
        functools.partial(body, ctx, dp),
        out_shape=[half] * 4 + [whole],
        in_specs=[hbm] * 7,
        out_specs=[hbm] * 5,
        scratch_shapes=[
            full,
            full,
            full,
            full,
            full,
            full,
            full,
            full,
            pltpu.VMEM(matrices.shape, jnp.bfloat16),
            pltpu.VMEM(twists.shape, jnp.float32),
            pltpu.VMEM((CHUNKS, 2, ctx, rows, width), jnp.float32),
            pltpu.VMEM((CHUNKS, 3, ctx, rows, width), jnp.float32),
            pltpu.VMEM((CHUNKS, 2, ctx, rows, width), jnp.float32),
            pltpu.VMEM((CHUNKS, 2, ctx, rows, width), jnp.float32),
            pltpu.VMEM((CHUNKS, PLANES, ring, rows, width), jnp.float32),
            pltpu.VMEM((CHUNKS, ring - 1, PLANES, rows, width), jnp.float32),
            pltpu.VMEM((CHUNKS, PLANES, rows, width), jnp.float32),
            pltpu.VMEM((CHUNKS, PLANES, PLANES, rows, width), jnp.float32),
            pltpu.VMEM((CHUNKS, PLANES, rows, width), jnp.float32),
            pltpu.VMEM((3, KEPT * rows, 2 * LANES), jnp.float32),
            pltpu.VMEM((CHUNKS, 3, KEPT * rows, 2 * LANES), jnp.float32),
            dma((6,)),
            dma((4,)),
            dma((CHUNKS,)),
            dma((CHUNKS,)),
            dma((CHUNKS,)),
            dma((CHUNKS,)),
            dma((CHUNKS,)),
            dma((CHUNKS,)),
            dma((CHUNKS,)),
            dma((CHUNKS,)),
            dma((CHUNKS,)),
            dma((CHUNKS,)),
            dma((CHUNKS, PLANES, PLANES)),
            dma((CHUNKS, PLANES, PLANES)),
            dma((CHUNKS,)),
            dma((CHUNKS,)),
        ],
        compiler_params=pltpu.CompilerParams(
            collective_id=0, has_side_effects=True, vmem_limit_bytes=GRANT
        ),
        cost_estimate=pl.CostEstimate(
            flops=3 * 2 * 6 * KEPT * share * 256 * 256, bytes_accessed=4 * 2**20, transcendentals=0
        ),
        name="hyena",
    )(
        query.reshape(channels, width),
        key_act.reshape(channels, width),
        value_act.reshape(channels, width),
        grad_out.reshape(channels, width),
        filter_taps,
        jnp.asarray(matrices),
        jnp.asarray(twists),
    )
    outs = pl.pallas_call(
        functools.partial(write_out, 5),
        out_shape=[half] * 4 + [whole],
        in_specs=[hbm] * 5,
        out_specs=[hbm] * 5,
        scratch_shapes=[dma((5,))],
        compiler_params=pltpu.CompilerParams(vmem_limit_bytes=GRANT),
        name="write_out",
    )(*outs)
    shape = query.shape
    return (
        outs[0].reshape(shape),
        outs[1].reshape(shape),
        outs[2].reshape(shape),
        outs[3].reshape(shape),
        outs[4].reshape(channels, width),
    )


def solution(mesh):
    row = P("dp", None, "ctx")
    taps = P(None, "ctx")
    return jax.shard_map(
        functools.partial(shards, mesh.shape["ctx"], mesh.shape["dp"]),
        mesh=mesh,
        in_specs=(row, row, row, taps, row),
        out_specs=(row, row, row, row, taps),
        check_vma=False,
    )
```

```python
import functools
import math

import jax
import jax.numpy as jnp
import numpy as np
from jax import lax
from jax.experimental import pallas as pl
from jax.experimental.pallas import tpu as pltpu
from jax.sharding import PartitionSpec as P

MESH = pl.DeviceIdType.MESH
LANES = 128
RADIX = 64
HALF = RADIX // 2
KEPT = HALF + 1


def turn(value, numerator, denominator):
    real, imag = value
    numerator %= denominator
    eighth = numerator * 8
    if eighth % denominator == 0:
        step = eighth // denominator
        if step == 0:
            return (real, imag)
        if step == 2:
            return (imag, -real)
        if step == 4:
            return (-real, -imag)
        if step == 6:
            return (-imag, real)
        root = math.sqrt(0.5)
        if step == 1:
            return ((real + imag) * root, (imag - real) * root)
        if step == 3:
            return ((imag - real) * root, (real + imag) * -root)
        if step == 5:
            return ((real + imag) * -root, (real - imag) * root)
        return ((real - imag) * root, (real + imag) * root)
    cos = math.cos(2.0 * math.pi * numerator / denominator)
    sin = math.sin(2.0 * math.pi * numerator / denominator)
    return (real * cos + imag * sin, imag * cos - real * sin)


def complex_fft(values, sign):
    size = len(values)
    if size == 1:
        return values
    even = complex_fft(values[0::2], sign)
    odd = complex_fft(values[1::2], sign)
    low, high = [], []
    for k in range(size // 2):
        real, imag = turn(odd[k], sign * k, size)
        low.append((even[k][0] + real, even[k][1] + imag))
        high.append((even[k][0] - real, even[k][1] - imag))
    return low + high


def odd_forward(values):
    quarter = len(values) // 2
    order = 4 * quarter
    packed = [turn((values[n], -values[n + quarter]), n, order) for n in range(quarter)]
    out = complex_fft(packed, 1)
    found = {}
    for j in range(quarter):
        k = 4 * j + 1
        if k < order // 2:
            found[k] = out[j]
        else:
            found[order - k] = (out[j][0], -out[j][1])
    return found


def real_forward(values):
    size = len(values)
    if size == 2:
        return {0: (values[0] + values[1], None), 1: (values[0] - values[1], None)}
    half = size // 2
    evens = real_forward([values[n] + values[n + half] for n in range(half)])
    found = {2 * k: value for k, value in evens.items()}
    found.update(odd_forward([values[n] - values[n + half] for n in range(half)]))
    return found


def padded_forward(values):
    found = {2 * k: value for k, value in real_forward(values).items()}
    found.update(odd_forward(values))
    return found


def odd_inverse(found, order):
    quarter = order // 4
    packed = []
    for j in range(quarter):
        k = 4 * j + 1
        if k < order // 2:
            packed.append(found[k])
        else:
            real, imag = found[order - k]
            packed.append((real, -imag))
    out = complex_fft(packed, -1)
    out = [turn(out[n], -n, order) for n in range(quarter)]
    return [value[0] for value in out] + [-value[1] for value in out]


def real_inverse(found, size):
    if size == 2:
        return [found[0][0] + found[1][0], found[0][0] - found[1][0]]
    half = size // 2
    evens = real_inverse({k // 2: value for k, value in found.items() if k % 2 == 0}, half)
    odds = odd_inverse(found, size)
    return [evens[n] + odds[n] for n in range(half)] + [evens[n] - odds[n] for n in range(half)]


def padded_inverse(found):
    evens = real_inverse({k // 2: value for k, value in found.items() if k % 2 == 0}, HALF)
    odds = odd_inverse(found, RADIX)
    return [evens[n] + odds[n] for n in range(HALF)]


def tables():
    k = np.arange(LANES)
    angles = 2.0 * np.pi * (k[:, None] * k[None, :] % LANES) / LANES
    cos, sin = np.cos(angles), np.sin(angles)
    forward = np.block([[cos, -sin], [sin, cos]])
    inverse = forward.T

    def split(matrix):
        high = matrix.astype(np.float32).astype(jnp.bfloat16)
        low = (matrix - high.astype(np.float64)).astype(np.float32).astype(jnp.bfloat16)
        return high, low

    matrices = np.stack([*split(forward), *split(inverse)])
    length = RADIX * LANES
    first = np.arange(KEPT)
    angles = 2.0 * np.pi * (first[:, None] * k[None, :]) / length
    scale = np.where((first == 0) | (first == HALF), 1.0, 2.0)[:, None] / length
    twists = np.stack(
        [np.cos(angles), np.sin(angles), np.cos(angles) * scale, np.sin(angles) * scale]
    ).astype(np.float32)
    return matrices, twists


CHUNKS = 4
PLANES = 2
GRANT = 60 * 1024 * 1024


def body(
    ctx,
    dp,
    q_hbm,
    k_hbm,
    v_hbm,
    g_hbm,
    f_hbm,
    w_hbm,
    t_hbm,
    out_hbm,
    gq_hbm,
    gk_hbm,
    gv_hbm,
    gf_ref,
    out_ref,
    gq_ref,
    gk_ref,
    gv_ref,
    q_ref,
    k_ref,
    v_ref,
    g_ref,
    w_ref,
    t_ref,
    send_x,
    recv_x,
    send_y,
    recv_y,
    part_g,
    recv_g,
    sum_g,
    recv_s,
    own_s,
    spec_a,
    spec_b,
    load_sem,
    save_sem,
    own_sem,
    keep_sem,
    sx_send,
    sx_recv,
    sf_send,
    sf_recv,
    sy_send,
    sy_recv,
    sg_send,
    sg_recv,
    ss_send,
    ss_recv,
    sa_send,
    sa_recv,
):
    me_c = lax.axis_index("ctx")
    me_d = lax.axis_index("dp")
    ring = dp // PLANES
    channels, width = q_ref.shape
    share = channels // ctx
    rows = share // CHUNKS
    subs = rows // 8
    me_p, me_z = me_d // ring, lax.rem(me_d, ring)
    c_p, c_z = me_c // ring, lax.rem(me_c, ring)
    slot = lax.rem(me_z + ctx - me_c, ring)

    loads = [
        pltpu.make_async_copy(src, dst, load_sem.at[n])
        for n, (src, dst) in enumerate(
            [
                (k_hbm, k_ref),
                (v_hbm, v_ref),
                (q_hbm, q_ref),
                (g_hbm, g_ref),
                (w_hbm, w_ref),
                (t_hbm, t_ref),
            ]
        )
    ]
    for load in loads:
        load.start()

    def each(first, last, act):
        def step(i, carry):
            act(i)
            return carry

        lax.fori_loop(first, last, step, 0, unroll=True)

    def ctx_peer(i):
        return (me_d, lax.rem(me_c + i, ctx))

    def ring_peer(i):
        return (me_p * ring + lax.rem(me_z + i, ring), me_c)

    def swap_peer(plane, part):
        return (plane * ring + me_z, part * ring + slot)

    def is_self(plane, part):
        return (c_z == slot) & (plane == me_p) & (part == c_p)

    barrier = pltpu.get_barrier_semaphore()

    def greet(peer):
        pl.semaphore_signal(barrier, inc=1, device_id=peer, device_id_type=MESH)

    each(1, ctx, lambda i: greet(ctx_peer(i)))
    each(1, ring, lambda i: greet(ring_peer(i)))
    swaps = [(plane, part) for plane in range(PLANES) for part in range(PLANES)]
    for plane, part in swaps:
        pl.when(jnp.logical_not(is_self(plane, part)))(
            functools.partial(greet, swap_peer(plane, part))
        )

    for load in loads[:4]:
        load.wait()

    def products(b, carry):
        at = pl.ds(b * share, share)
        mixed = k_ref[at, :].astype(jnp.float32) * v_ref[at, :].astype(jnp.float32)
        dconv = q_ref[at, :].astype(jnp.float32) * g_ref[at, :].astype(jnp.float32)
        for ck in range(CHUNKS):
            send_x[ck, 0, b] = mixed[ck * rows : (ck + 1) * rows]
            send_x[ck, 1, b] = dconv[ck * rows : (ck + 1) * rows]
        return carry

    lax.fori_loop(0, ctx, products, 0)

    met = ctx - 1 + ring - 1 + len(swaps)

    @pl.when(c_z == slot)
    def _():
        pl.semaphore_wait(barrier, met - 1)

    @pl.when(c_z != slot)
    def _():
        pl.semaphore_wait(barrier, met)

    def remote(src, dst, send, recv, peer):
        return pltpu.make_async_remote_copy(
            src_ref=src,
            dst_ref=dst,
            send_sem=send,
            recv_sem=recv,
            device_id=peer,
            device_id_type=MESH,
        )

    def copy_x(ck, i):
        peer = ctx_peer(i)
        return remote(
            send_x.at[ck, :, peer[1]],
            recv_x.at[ck, pl.ds(0, 2), me_c],
            sx_send.at[ck],
            sx_recv.at[ck],
            peer,
        )

    def copy_f(ck, i):
        peer = ctx_peer(i)
        return remote(
            f_hbm.at[pl.ds(peer[1] * share + ck * rows, rows), :],
            recv_x.at[ck, 2, me_c],
            sf_send.at[ck],
            sf_recv.at[ck],
            peer,
        )

    def own_f(ck):
        return pltpu.make_async_copy(
            f_hbm.at[pl.ds(me_c * share + ck * rows, rows), :],
            recv_x.at[ck, 2, me_c],
            own_sem.at[ck],
        )

    def copy_y(ck, i):
        peer = ctx_peer(i)
        return remote(
            send_y.at[ck, :, peer[1]],
            recv_y.at[ck, :, me_c],
            sy_send.at[ck],
            sy_recv.at[ck],
            peer,
        )

    def copy_g(ck, i):
        peer = ring_peer(i)
        return remote(
            part_g.at[ck, :, lax.rem(slot + i, ring)],
            recv_g.at[ck, i - 1],
            sg_send.at[ck],
            sg_recv.at[ck],
            peer,
        )

    def copy_s(ck, plane, part):
        return remote(
            sum_g.at[ck, part],
            recv_s.at[ck, c_p, me_p],
            ss_send.at[ck, plane, part],
            ss_recv.at[ck, c_p, me_p],
            swap_peer(plane, part),
        )

    def copy_a(ck, i):
        return remote(
            own_s.at[ck],
            gf_ref.at[:, slot, ck],
            sa_send.at[ck],
            sa_recv.at[ck],
            ring_peer(i),
        )

    def keep(ck):
        return pltpu.make_async_copy(own_s.at[ck], gf_ref.at[:, slot, ck], keep_sem.at[ck])

    def drain(ref, sem):
        pltpu.make_async_copy(ref, ref, sem).wait()

    def chunks(act):
        def step(ck, carry):
            act(ck)
            return carry

        lax.fori_loop(0, CHUNKS, step, 0)

    chunks(lambda ck: each(1, ctx, lambda i: copy_x(ck, i).start()))

    def first_f(ck):
        each(1, ctx, lambda i: copy_f(ck, i).start())
        own_f(ck).start()

    chunks(first_f)

    def own_x(ck):
        recv_x[ck, 0, me_c] = send_x[ck, 0, me_c]
        recv_x[ck, 1, me_c] = send_x[ck, 1, me_c]

    chunks(own_x)
    for load in loads[4:]:
        load.wait()

    re, im = pl.ds(0, LANES), pl.ds(LANES, LANES)

    def forward(ck, sig, sub):
        at = pl.ds(sub * 8, 8)
        values = [
            recv_x[ck, sig, n // 2, at, pl.ds((n % 2) * LANES, LANES)] for n in range(HALF)
        ]
        found = padded_forward(values)
        for k in range(KEPT):
            cos, sin = t_ref[0, pl.ds(k, 1), :], t_ref[1, pl.ds(k, 1), :]
            real, imag = found[k]
            to = pl.ds(k * rows + sub * 8, 8)
            if k == 0:
                spec_a[sig, to, re] = real
                spec_a[sig, to, im] = jnp.zeros_like(real)
            elif imag is None:
                spec_a[sig, to, re] = real * cos
                spec_a[sig, to, im] = -(real * sin)
            else:
                spec_a[sig, to, re] = real * cos + imag * sin
                spec_a[sig, to, im] = imag * cos - real * sin

    def inverse(ck, sig, sub, store):
        found = {}
        for k in range(KEPT):
            cos, sin = t_ref[2, pl.ds(k, 1), :], t_ref[3, pl.ds(k, 1), :]
            at = pl.ds(k * rows + sub * 8, 8)
            real = spec_a[sig, at, re]
            imag = spec_a[sig, at, im]
            if k == 0 or k == HALF:
                found[k] = (real * cos - imag * sin, None)
            else:
                found[k] = (real * cos - imag * sin, imag * cos + real * sin)
        values = padded_inverse(found)
        for n in range(HALF):
            store(n // 2, pl.ds(sub * 8, 8), pl.ds((n % 2) * LANES, LANES), values[n])

    def matmul(src, dst, which):
        data = src[...]
        high = data.astype(jnp.bfloat16)
        low = (data - high.astype(jnp.float32)).astype(jnp.bfloat16)
        w_high = w_ref[2 * which]
        w_low = w_ref[2 * which + 1]
        dst[...] = (
            jnp.dot(high, w_high, preferred_element_type=jnp.float32)
            + jnp.dot(low, w_high, preferred_element_type=jnp.float32)
            + jnp.dot(high, w_low, preferred_element_type=jnp.float32)
        )

    def loop(count, act, unroll=1):
        def step(i, carry):
            act(i)
            return carry

        lax.fori_loop(0, count, step, 0, unroll=unroll)

    def filter_grad(ck):
        drain(recv_x.at[ck, pl.ds(0, 2), pl.ds(0, ctx - 1)], sx_recv.at[ck])
        loop(2 * subs, lambda n: forward(ck, n // subs, lax.rem(n, subs)))
        loop(2, lambda sig: matmul(spec_a.at[sig], spec_b.at[ck, sig], 0))

        def pointwise(k):
            at = pl.ds(k * rows, rows)
            z_re, z_im = spec_b[ck, 0, at, re], spec_b[ck, 0, at, im]
            d_re, d_im = spec_b[ck, 1, at, re], spec_b[ck, 1, at, im]
            spec_a[0, at, re] = z_re * d_re + z_im * d_im
            spec_a[0, at, im] = z_re * d_im - z_im * d_re

        loop(KEPT, pointwise, 3)
        matmul(spec_a.at[0], spec_a.at[1], 1)

        def store(block, at, lanes, value):
            part_g[ck, block // ring, block % ring, at, lanes] = value

        loop(subs, lambda sub: inverse(ck, 1, sub, store))
        each(1, ring, lambda i: copy_g(ck, i).start())

    def convolutions(ck):
        drain(recv_x.at[ck, 2, pl.ds(0, ctx - 1)], sf_recv.at[ck])
        own_f(ck).wait()
        loop(subs, lambda sub: forward(ck, 2, sub))
        matmul(spec_a.at[2], spec_b.at[ck, 2], 0)

        def pointwise(k):
            at = pl.ds(k * rows, rows)
            z_re, z_im = spec_b[ck, 0, at, re], spec_b[ck, 0, at, im]
            d_re, d_im = spec_b[ck, 1, at, re], spec_b[ck, 1, at, im]
            f_re, f_im = spec_b[ck, 2, at, re], spec_b[ck, 2, at, im]
            spec_a[0, at, re] = z_re * f_re - z_im * f_im
            spec_a[0, at, im] = z_re * f_im + z_im * f_re
            spec_a[1, at, re] = f_re * d_re + f_im * d_im
            spec_a[1, at, im] = f_re * d_im - f_im * d_re

        loop(KEPT, pointwise, 3)
        loop(2, lambda sig: matmul(spec_a.at[sig], spec_a.at[sig], 1))

        def back(n):
            sig, sub = n // subs, lax.rem(n, subs)

            def store(block, at, lanes, value):
                send_y[ck, sig, block, at, lanes] = value

            inverse(ck, sig, sub, store)

        loop(2 * subs, back)
        each(1, ctx, lambda i: copy_y(ck, i).start())
        recv_y[ck, 0, me_c] = send_y[ck, 0, me_c]
        recv_y[ck, 1, me_c] = send_y[ck, 1, me_c]

    def reduce(ck):
        drain(recv_g.at[ck], sg_recv.at[ck])
        for part in range(PLANES):
            total = part_g[ck, part, slot]
            for i in range(ring - 1):
                total = total + recv_g[ck, i, part]
            sum_g[ck, part] = total
        for plane, part in swaps:
            mine = is_self(plane, part)

            @pl.when(jnp.logical_not(mine))
            def _():
                copy_s(ck, plane, part).start()

            @pl.when(mine)
            def _():
                recv_s[ck, part, plane] = sum_g[ck, part]

    scale = 1.0 / math.sqrt(dp * ctx * width)

    def gather(ck):
        for plane, part in swaps:

            @pl.when(jnp.logical_not(is_self(plane, part)))
            def _():
                drain(recv_s.at[ck, part, plane], ss_recv.at[ck, part, plane])

        for part in range(PLANES):
            total = recv_s[ck, part, 0]
            for plane in range(1, PLANES):
                total = total + recv_s[ck, part, plane]
            own_s[ck, part] = total * scale
        each(1, ring, lambda i: copy_a(ck, i).start())
        keep(ck).start()

    def stage(step):
        pl.when(step < CHUNKS)(lambda: filter_grad(step))
        pl.when((step >= 2) & (step < CHUNKS + 2))(lambda: reduce(step - 2))

        @pl.when(step >= 3)
        def _():
            convolutions(step - 3)
            gather(step - 3)

    loop(CHUNKS + 3, stage)

    for ck in range(CHUNKS):
        drain(recv_y.at[ck, :, pl.ds(0, ctx - 1)], sy_recv.at[ck])

    def outputs(b):
        at = pl.ds(b * share, share)
        conv = jnp.concatenate([recv_y[ck, 0, b] for ck in range(CHUNKS)], axis=0)
        dmixed = jnp.concatenate([recv_y[ck, 1, b] for ck in range(CHUNKS)], axis=0)
        out_ref[at, :] = (q_ref[at, :].astype(jnp.float32) * conv).astype(jnp.bfloat16)
        gq_ref[at, :] = (g_ref[at, :].astype(jnp.float32) * conv).astype(jnp.bfloat16)
        gk_ref[at, :] = (v_ref[at, :].astype(jnp.float32) * dmixed).astype(jnp.bfloat16)
        gv_ref[at, :] = (k_ref[at, :].astype(jnp.float32) * dmixed).astype(jnp.bfloat16)

    loop(ctx, outputs)
    saves = [
        pltpu.make_async_copy(src, dst, save_sem.at[n])
        for n, (src, dst) in enumerate(
            [(out_ref, out_hbm), (gq_ref, gq_hbm), (gk_ref, gk_hbm), (gv_ref, gv_hbm)]
        )
    ]
    for save in saves:
        save.start()

    def finish(ck):
        drain(recv_x.at[ck, pl.ds(0, 2), pl.ds(0, ctx - 1)], sx_send.at[ck])
        drain(recv_x.at[ck, 2, pl.ds(0, ctx - 1)], sf_send.at[ck])
        drain(recv_y.at[ck, :, pl.ds(0, ctx - 1)], sy_send.at[ck])
        drain(recv_g.at[ck], sg_send.at[ck])
        for plane, part in swaps:

            @pl.when(jnp.logical_not(is_self(plane, part)))
            def _():
                drain(sum_g.at[ck, part], ss_send.at[ck, plane, part])

        keep(ck).wait()
        drain(gf_ref.at[:, pl.ds(0, ring - 1), ck], sa_send.at[ck])
        drain(gf_ref.at[:, pl.ds(0, ring - 1), ck], sa_recv.at[ck])

    chunks(finish)
    for save in saves:
        save.wait()


def write_out(count, *refs):
    sources, targets = refs[:count], refs[count : 2 * count]
    stages, sems = refs[2 * count : 3 * count], refs[3 * count]
    reads = [
        pltpu.make_async_copy(sources[n], stages[n], sems.at[0, n]) for n in range(count)
    ]
    writes = [
        pltpu.make_async_copy(stages[n], targets[n], sems.at[1, n]) for n in range(count)
    ]
    for read in reads:
        read.start()
    for read, write in zip(reads, writes):
        read.wait()
        write.start()
    for write in writes:
        write.wait()


def shards(ctx, dp, query, key_act, value_act, filter_taps, grad_out):
    _, channels, width = query.shape
    share = channels // ctx
    rows = share // CHUNKS
    ring = dp // PLANES
    matrices, twists = tables()
    hbm = pl.BlockSpec(memory_space=pltpu.HBM)
    half = jax.ShapeDtypeStruct((channels, width), jnp.bfloat16)
    whole = jax.ShapeDtypeStruct((PLANES, ring, CHUNKS, rows, width), jnp.float32)
    dma = pltpu.SemaphoreType.DMA
    full = pltpu.VMEM((channels, width), jnp.bfloat16)
    outs = pl.pallas_call(
        functools.partial(body, ctx, dp),
        out_shape=[half] * 4 + [whole],
        in_specs=[hbm] * 7,
        out_specs=[hbm] * 5,
        scratch_shapes=[
            full,
            full,
            full,
            full,
            full,
            full,
            full,
            full,
            pltpu.VMEM(matrices.shape, jnp.bfloat16),
            pltpu.VMEM(twists.shape, jnp.float32),
            pltpu.VMEM((CHUNKS, 2, ctx, rows, width), jnp.float32),
            pltpu.VMEM((CHUNKS, 3, ctx, rows, width), jnp.float32),
            pltpu.VMEM((CHUNKS, 2, ctx, rows, width), jnp.float32),
            pltpu.VMEM((CHUNKS, 2, ctx, rows, width), jnp.float32),
            pltpu.VMEM((CHUNKS, PLANES, ring, rows, width), jnp.float32),
            pltpu.VMEM((CHUNKS, ring - 1, PLANES, rows, width), jnp.float32),
            pltpu.VMEM((CHUNKS, PLANES, rows, width), jnp.float32),
            pltpu.VMEM((CHUNKS, PLANES, PLANES, rows, width), jnp.float32),
            pltpu.VMEM((CHUNKS, PLANES, rows, width), jnp.float32),
            pltpu.VMEM((3, KEPT * rows, 2 * LANES), jnp.float32),
            pltpu.VMEM((CHUNKS, 3, KEPT * rows, 2 * LANES), jnp.float32),
            dma((6,)),
            dma((4,)),
            dma((CHUNKS,)),
            dma((CHUNKS,)),
            dma((CHUNKS,)),
            dma((CHUNKS,)),
            dma((CHUNKS,)),
            dma((CHUNKS,)),
            dma((CHUNKS,)),
            dma((CHUNKS,)),
            dma((CHUNKS,)),
            dma((CHUNKS,)),
            dma((CHUNKS, PLANES, PLANES)),
            dma((CHUNKS, PLANES, PLANES)),
            dma((CHUNKS,)),
            dma((CHUNKS,)),
        ],
        compiler_params=pltpu.CompilerParams(
            collective_id=0, has_side_effects=True, vmem_limit_bytes=GRANT
        ),
        cost_estimate=pl.CostEstimate(
            flops=3 * 2 * 6 * KEPT * share * 256 * 256, bytes_accessed=4 * 2**20, transcendentals=0
        ),
        name="hyena",
    )(
        query.reshape(channels, width),
        key_act.reshape(channels, width),
        value_act.reshape(channels, width),
        grad_out.reshape(channels, width),
        filter_taps,
        jnp.asarray(matrices),
        jnp.asarray(twists),
    )
    outs = pl.pallas_call(
        functools.partial(write_out, 5),
        out_shape=[half] * 4 + [whole],
        in_specs=[hbm] * 5,
        out_specs=[hbm] * 5,
        scratch_shapes=[full] * 4 + [pltpu.VMEM(whole.shape, jnp.float32), dma((2, 5))],
        compiler_params=pltpu.CompilerParams(vmem_limit_bytes=GRANT),
        name="write_out",
    )(*outs)
    shape = query.shape
    return (
        outs[0].reshape(shape),
        outs[1].reshape(shape),
        outs[2].reshape(shape),
        outs[3].reshape(shape),
        outs[4].reshape(channels, width),
    )


def solution(mesh):
    row = P("dp", None, "ctx")
    taps = P(None, "ctx")
    return jax.shard_map(
        functools.partial(shards, mesh.shape["ctx"], mesh.shape["dp"]),
        mesh=mesh,
        in_specs=(row, row, row, taps, row),
        out_specs=(row, row, row, row, taps),
        check_vma=False,
    )
```

```python
import functools
import math

import jax
import jax.numpy as jnp
import numpy as np
from jax import lax
from jax.experimental import pallas as pl
from jax.experimental.pallas import tpu as pltpu
from jax.sharding import PartitionSpec as P

MESH = pl.DeviceIdType.MESH
LANES = 128
RADIX = 64
HALF = RADIX // 2
KEPT = HALF + 1
STRIDE = 40


def turn(value, numerator, denominator):
    real, imag = value
    numerator %= denominator
    eighth = numerator * 8
    if eighth % denominator == 0:
        step = eighth // denominator
        if step == 0:
            return (real, imag)
        if step == 2:
            return (imag, -real)
        if step == 4:
            return (-real, -imag)
        if step == 6:
            return (-imag, real)
        root = math.sqrt(0.5)
        if step == 1:
            return ((real + imag) * root, (imag - real) * root)
        if step == 3:
            return ((imag - real) * root, (real + imag) * -root)
        if step == 5:
            return ((real + imag) * -root, (real - imag) * root)
        return ((real - imag) * root, (real + imag) * root)
    cos = math.cos(2.0 * math.pi * numerator / denominator)
    sin = math.sin(2.0 * math.pi * numerator / denominator)
    return (real * cos + imag * sin, imag * cos - real * sin)


def complex_fft(values, sign):
    size = len(values)
    if size == 1:
        return values
    even = complex_fft(values[0::2], sign)
    odd = complex_fft(values[1::2], sign)
    low, high = [], []
    for k in range(size // 2):
        real, imag = turn(odd[k], sign * k, size)
        low.append((even[k][0] + real, even[k][1] + imag))
        high.append((even[k][0] - real, even[k][1] - imag))
    return low + high


def odd_forward(values):
    quarter = len(values) // 2
    order = 4 * quarter
    packed = [turn((values[n], -values[n + quarter]), n, order) for n in range(quarter)]
    out = complex_fft(packed, 1)
    found = {}
    for j in range(quarter):
        k = 4 * j + 1
        if k < order // 2:
            found[k] = out[j]
        else:
            found[order - k] = (out[j][0], -out[j][1])
    return found


def real_forward(values):
    size = len(values)
    if size == 2:
        return {0: (values[0] + values[1], None), 1: (values[0] - values[1], None)}
    half = size // 2
    evens = real_forward([values[n] + values[n + half] for n in range(half)])
    found = {2 * k: value for k, value in evens.items()}
    found.update(odd_forward([values[n] - values[n + half] for n in range(half)]))
    return found


def padded_forward(values):
    found = {2 * k: value for k, value in real_forward(values).items()}
    found.update(odd_forward(values))
    return found


def odd_inverse(found, order):
    quarter = order // 4
    packed = []
    for j in range(quarter):
        k = 4 * j + 1
        if k < order // 2:
            packed.append(found[k])
        else:
            real, imag = found[order - k]
            packed.append((real, -imag))
    out = complex_fft(packed, -1)
    out = [turn(out[n], -n, order) for n in range(quarter)]
    return [value[0] for value in out] + [-value[1] for value in out]


def real_inverse(found, size):
    if size == 2:
        return [found[0][0] + found[1][0], found[0][0] - found[1][0]]
    half = size // 2
    evens = real_inverse({k // 2: value for k, value in found.items() if k % 2 == 0}, half)
    odds = odd_inverse(found, size)
    return [evens[n] + odds[n] for n in range(half)] + [evens[n] - odds[n] for n in range(half)]


def padded_inverse(found):
    evens = real_inverse({k // 2: value for k, value in found.items() if k % 2 == 0}, HALF)
    odds = odd_inverse(found, RADIX)
    return [evens[n] + odds[n] for n in range(HALF)]


def tables():
    k = np.arange(LANES)
    angles = 2.0 * np.pi * (k[:, None] * k[None, :] % LANES) / LANES
    cos, sin = np.cos(angles), np.sin(angles)
    forward = np.block([[cos, -sin], [sin, cos]])
    inverse = forward.T

    def split(matrix):
        high = matrix.astype(np.float32).astype(jnp.bfloat16)
        low = (matrix - high.astype(np.float64)).astype(np.float32).astype(jnp.bfloat16)
        return high, low

    matrices = np.stack([*split(forward), *split(inverse)])
    length = RADIX * LANES
    first = np.arange(KEPT)
    angles = 2.0 * np.pi * (first[:, None] * k[None, :]) / length
    scale = np.where((first == 0) | (first == HALF), 1.0, 2.0)[:, None] / length
    twists = np.stack(
        [np.cos(angles), np.sin(angles), np.cos(angles) * scale, np.sin(angles) * scale]
    ).astype(np.float32)
    table = np.zeros((4, STRIDE, 2 * LANES), np.float32)
    table[:, :KEPT, :LANES] = twists
    return np.concatenate(
        [matrices.astype(np.float32).reshape(-1, 2 * LANES), table.reshape(-1, 2 * LANES)]
    )


CHUNKS = 4
PLANES = 2
GRANT = int(52.3 * 1024 * 1024)


def body(
    ctx,
    dp,
    q_hbm,
    k_hbm,
    v_hbm,
    g_hbm,
    f_hbm,
    c_hbm,
    out_ref,
    gq_ref,
    gk_ref,
    gv_ref,
    *rest,
):
    gf_refs = rest[:CHUNKS]
    (
        q_ref,
        k_ref,
        v_ref,
        g_ref,
        c_ref,
        w_ref,
        send_x,
        recv_x,
        send_y,
        recv_y,
        part_g,
        recv_g,
        sum_g,
        recv_s,
        own_s,
        spec_a,
        spec_b,
        load_sem,
        own_sem,
        keep_sem,
        sx_send,
        sx_recv,
        sf_send,
        sf_recv,
        sy_send,
        sy_recv,
        sg_send,
        sg_recv,
        ss_send,
        ss_recv,
        sa_send,
        sa_recv,
    ) = rest[CHUNKS:]
    me_c = lax.axis_index("ctx")
    me_d = lax.axis_index("dp")
    ring = dp // PLANES
    channels, width = q_ref.shape
    share = channels // ctx
    rows = share // CHUNKS
    subs = rows // 8
    me_p, me_z = me_d // ring, lax.rem(me_d, ring)
    c_p, c_z = me_c // ring, lax.rem(me_c, ring)
    slot = lax.rem(me_z + ctx - me_c, ring)

    loads = [
        pltpu.make_async_copy(src, dst, load_sem.at[n])
        for n, (src, dst) in enumerate(
            [
                (k_hbm, k_ref),
                (v_hbm, v_ref),
                (q_hbm, q_ref),
                (g_hbm, g_ref),
                (c_hbm, c_ref),
            ]
        )
    ]
    for load in loads:
        load.start()

    def each(first, last, act):
        def step(i, carry):
            act(i)
            return carry

        lax.fori_loop(first, last, step, 0, unroll=True)

    def ctx_peer(i):
        return (me_d, lax.rem(me_c + i, ctx))

    def ring_peer(i):
        return (me_p * ring + lax.rem(me_z + i, ring), me_c)

    def swap_peer(plane, part):
        return (plane * ring + me_z, part * ring + slot)

    def is_self(plane, part):
        return (c_z == slot) & (plane == me_p) & (part == c_p)

    barrier = pltpu.get_barrier_semaphore()

    def greet(peer):
        pl.semaphore_signal(barrier, inc=1, device_id=peer, device_id_type=MESH)

    each(1, ctx, lambda i: greet(ctx_peer(i)))
    each(1, ring, lambda i: greet(ring_peer(i)))
    swaps = [(plane, part) for plane in range(PLANES) for part in range(PLANES)]
    for plane, part in swaps:
        pl.when(jnp.logical_not(is_self(plane, part)))(
            functools.partial(greet, swap_peer(plane, part))
        )

    for load in loads[:4]:
        load.wait()

    def products(b, carry):
        at = pl.ds(b * share, share)
        mixed = k_ref[at, :].astype(jnp.float32) * v_ref[at, :].astype(jnp.float32)
        dconv = q_ref[at, :].astype(jnp.float32) * g_ref[at, :].astype(jnp.float32)
        for ck in range(CHUNKS):
            send_x[ck, 0, b] = mixed[ck * rows : (ck + 1) * rows]
            send_x[ck, 1, b] = dconv[ck * rows : (ck + 1) * rows]
        return carry

    lax.fori_loop(0, ctx, products, 0)

    met = ctx - 1 + ring - 1 + len(swaps)

    @pl.when(c_z == slot)
    def _():
        pl.semaphore_wait(barrier, met - 1)

    @pl.when(c_z != slot)
    def _():
        pl.semaphore_wait(barrier, met)

    def remote(src, dst, send, recv, peer):
        return pltpu.make_async_remote_copy(
            src_ref=src,
            dst_ref=dst,
            send_sem=send,
            recv_sem=recv,
            device_id=peer,
            device_id_type=MESH,
        )

    def copy_x(ck, i):
        peer = ctx_peer(i)
        return remote(
            send_x.at[ck, :, peer[1]],
            recv_x.at[ck, pl.ds(0, 2), me_c],
            sx_send.at[ck],
            sx_recv.at[ck],
            peer,
        )

    def copy_f(ck, i):
        peer = ctx_peer(i)
        return remote(
            f_hbm.at[pl.ds(peer[1] * share + ck * rows, rows), :],
            recv_x.at[ck, 2, me_c],
            sf_send.at[ck],
            sf_recv.at[ck],
            peer,
        )

    def own_f(ck):
        return pltpu.make_async_copy(
            f_hbm.at[pl.ds(me_c * share + ck * rows, rows), :],
            recv_x.at[ck, 2, me_c],
            own_sem.at[ck],
        )

    def copy_y(ck, i):
        peer = ctx_peer(i)
        return remote(
            send_y.at[ck, :, peer[1]],
            recv_y.at[ck, :, me_c],
            sy_send.at[ck],
            sy_recv.at[ck],
            peer,
        )

    def copy_g(ck, i):
        peer = ring_peer(i)
        return remote(
            part_g.at[ck, :, lax.rem(slot + i, ring)],
            recv_g.at[ck, i - 1],
            sg_send.at[ck],
            sg_recv.at[ck],
            peer,
        )

    def copy_s(ck, plane, part):
        return remote(
            sum_g.at[ck, part],
            recv_s.at[ck, c_p, me_p],
            ss_send.at[ck, plane, part],
            ss_recv.at[ck, c_p, me_p],
            swap_peer(plane, part),
        )

    def copy_a(ck, i):
        return remote(
            own_s.at[ck],
            gf_refs[ck].at[:, slot],
            sa_send.at[ck],
            sa_recv.at[ck],
            ring_peer(i),
        )

    def keep(ck):
        return pltpu.make_async_copy(own_s.at[ck], gf_refs[ck].at[:, slot], keep_sem.at[ck])

    def drain(ref, sem):
        pltpu.make_async_copy(ref, ref, sem).wait()

    def chunks(act):
        def step(ck, carry):
            act(ck)
            return carry

        lax.fori_loop(0, CHUNKS, step, 0)

    chunks(lambda ck: each(1, ctx, lambda i: copy_x(ck, i).start()))

    def first_f(ck):
        each(1, ctx, lambda i: copy_f(ck, i).start())
        own_f(ck).start()

    def own_x(ck):
        recv_x[ck, 0, me_c] = send_x[ck, 0, me_c]
        recv_x[ck, 1, me_c] = send_x[ck, 1, me_c]

    chunks(own_x)
    for load in loads[4:]:
        load.wait()
    w_ref[...] = c_ref[pl.ds(0, w_ref.shape[0]), :].astype(jnp.bfloat16)

    def twist(which, k):
        return c_ref[pl.ds(w_ref.shape[0] + which * STRIDE + k, 1), pl.ds(0, LANES)]

    def weight(which):
        return w_ref[pl.ds(which * 2 * LANES, 2 * LANES), :]

    re, im = pl.ds(0, LANES), pl.ds(LANES, LANES)

    def forward(ck, sig, sub):
        at = pl.ds(sub * 8, 8)
        values = [
            recv_x[ck, sig, n // 2, at, pl.ds((n % 2) * LANES, LANES)] for n in range(HALF)
        ]
        found = padded_forward(values)
        for k in range(KEPT):
            cos, sin = twist(0, k), twist(1, k)
            real, imag = found[k]
            to = pl.ds(k * rows + sub * 8, 8)
            if k == 0:
                spec_a[sig, to, re] = real
                spec_a[sig, to, im] = jnp.zeros_like(real)
            elif imag is None:
                spec_a[sig, to, re] = real * cos
                spec_a[sig, to, im] = -(real * sin)
            else:
                spec_a[sig, to, re] = real * cos + imag * sin
                spec_a[sig, to, im] = imag * cos - real * sin

    def inverse(ck, sig, sub, store):
        found = {}
        for k in range(KEPT):
            cos, sin = twist(2, k), twist(3, k)
            at = pl.ds(k * rows + sub * 8, 8)
            real = spec_a[sig, at, re]
            imag = spec_a[sig, at, im]
            if k == 0 or k == HALF:
                found[k] = (real * cos - imag * sin, None)
            else:
                found[k] = (real * cos - imag * sin, imag * cos + real * sin)
        values = padded_inverse(found)
        for n in range(HALF):
            store(n // 2, pl.ds(sub * 8, 8), pl.ds((n % 2) * LANES, LANES), values[n])

    def matmul(src, dst, which):
        data = src[...]
        high = data.astype(jnp.bfloat16)
        low = (data - high.astype(jnp.float32)).astype(jnp.bfloat16)
        w_high = weight(2 * which)
        w_low = weight(2 * which + 1)
        dst[...] = (
            jnp.dot(high, w_high, preferred_element_type=jnp.float32)
            + jnp.dot(low, w_high, preferred_element_type=jnp.float32)
            + jnp.dot(high, w_low, preferred_element_type=jnp.float32)
        )

    def loop(count, act, unroll=1):
        def step(i, carry):
            act(i)
            return carry

        lax.fori_loop(0, count, step, 0, unroll=unroll)

    def filter_grad(ck):
        drain(recv_x.at[ck, pl.ds(0, 2), pl.ds(0, ctx - 1)], sx_recv.at[ck])
        loop(2 * subs, lambda n: forward(ck, n // subs, lax.rem(n, subs)))
        loop(2, lambda sig: matmul(spec_a.at[sig], spec_b.at[ck, sig], 0))

        def pointwise(k):
            at = pl.ds(k * rows, rows)
            z_re, z_im = spec_b[ck, 0, at, re], spec_b[ck, 0, at, im]
            d_re, d_im = spec_b[ck, 1, at, re], spec_b[ck, 1, at, im]
            spec_a[0, at, re] = z_re * d_re + z_im * d_im
            spec_a[0, at, im] = z_re * d_im - z_im * d_re

        loop(KEPT, pointwise, 3)
        matmul(spec_a.at[0], spec_a.at[1], 1)

        def store(block, at, lanes, value):
            part_g[ck, block // ring, block % ring, at, lanes] = value

        loop(subs, lambda sub: inverse(ck, 1, sub, store))
        each(1, ring, lambda i: copy_g(ck, i).start())

    def convolutions(ck):
        drain(recv_x.at[ck, 2, pl.ds(0, ctx - 1)], sf_recv.at[ck])
        own_f(ck).wait()
        loop(subs, lambda sub: forward(ck, 2, sub))
        matmul(spec_a.at[2], spec_b.at[ck, 2], 0)

        def pointwise(k):
            at = pl.ds(k * rows, rows)
            z_re, z_im = spec_b[ck, 0, at, re], spec_b[ck, 0, at, im]
            d_re, d_im = spec_b[ck, 1, at, re], spec_b[ck, 1, at, im]
            f_re, f_im = spec_b[ck, 2, at, re], spec_b[ck, 2, at, im]
            spec_a[0, at, re] = z_re * f_re - z_im * f_im
            spec_a[0, at, im] = z_re * f_im + z_im * f_re
            spec_a[1, at, re] = f_re * d_re + f_im * d_im
            spec_a[1, at, im] = f_re * d_im - f_im * d_re

        loop(KEPT, pointwise, 3)
        loop(2, lambda sig: matmul(spec_a.at[sig], spec_a.at[sig], 1))

        def back(n):
            sig, sub = n // subs, lax.rem(n, subs)

            def store(block, at, lanes, value):
                send_y[ck, sig, block, at, lanes] = value

            inverse(ck, sig, sub, store)

        loop(2 * subs, back)
        each(1, ctx, lambda i: copy_y(ck, i).start())
        recv_y[ck, 0, me_c] = send_y[ck, 0, me_c]
        recv_y[ck, 1, me_c] = send_y[ck, 1, me_c]

    def reduce(ck):
        drain(recv_g.at[ck], sg_recv.at[ck])
        for part in range(PLANES):
            total = part_g[ck, part, slot]
            for i in range(ring - 1):
                total = total + recv_g[ck, i, part]
            sum_g[ck, part] = total
        for plane, part in swaps:
            mine = is_self(plane, part)

            @pl.when(jnp.logical_not(mine))
            def _():
                copy_s(ck, plane, part).start()

            @pl.when(mine)
            def _():
                recv_s[ck, part, plane] = sum_g[ck, part]

    scale = 1.0 / math.sqrt(dp * ctx * width)

    def gather(ck):
        for plane, part in swaps:

            @pl.when(jnp.logical_not(is_self(plane, part)))
            def _():
                drain(recv_s.at[ck, part, plane], ss_recv.at[ck, part, plane])

        for part in range(PLANES):
            total = recv_s[ck, part, 0]
            for plane in range(1, PLANES):
                total = total + recv_s[ck, part, plane]
            own_s[ck, part] = total * scale
        for chunk in range(CHUNKS):

            @pl.when(ck == chunk)
            def _():
                each(1, ring, lambda i: copy_a(chunk, i).start())
                keep(chunk).start()

    def stage(step):
        pl.when(step < CHUNKS)(lambda: filter_grad(step))
        pl.when(step == 1)(lambda: chunks(first_f))
        pl.when((step >= 2) & (step < CHUNKS + 2))(lambda: reduce(step - 2))

        @pl.when(step >= 3)
        def _():
            convolutions(step - 3)
            gather(step - 3)

    loop(CHUNKS + 3, stage)

    for ck in range(CHUNKS):
        drain(recv_y.at[ck, :, pl.ds(0, ctx - 1)], sy_recv.at[ck])

    def outputs(b):
        at = pl.ds(b * share, share)
        conv = jnp.concatenate([recv_y[ck, 0, b] for ck in range(CHUNKS)], axis=0)
        dmixed = jnp.concatenate([recv_y[ck, 1, b] for ck in range(CHUNKS)], axis=0)
        out_ref[at, :] = (q_ref[at, :].astype(jnp.float32) * conv).astype(jnp.bfloat16)
        gq_ref[at, :] = (g_ref[at, :].astype(jnp.float32) * conv).astype(jnp.bfloat16)
        gk_ref[at, :] = (v_ref[at, :].astype(jnp.float32) * dmixed).astype(jnp.bfloat16)
        gv_ref[at, :] = (k_ref[at, :].astype(jnp.float32) * dmixed).astype(jnp.bfloat16)

    loop(ctx, outputs)

    def finish(ck):
        drain(recv_x.at[ck, pl.ds(0, 2), pl.ds(0, ctx - 1)], sx_send.at[ck])
        drain(recv_x.at[ck, 2, pl.ds(0, ctx - 1)], sf_send.at[ck])
        drain(recv_y.at[ck, :, pl.ds(0, ctx - 1)], sy_send.at[ck])
        drain(recv_g.at[ck], sg_send.at[ck])
        for plane, part in swaps:

            @pl.when(jnp.logical_not(is_self(plane, part)))
            def _():
                drain(sum_g.at[ck, part], ss_send.at[ck, plane, part])


    chunks(finish)
    for ck in range(CHUNKS):
        keep(ck).wait()
        drain(gf_refs[ck].at[:, pl.ds(0, ring - 1)], sa_send.at[ck])
        drain(gf_refs[ck].at[:, pl.ds(0, ring - 1)], sa_recv.at[ck])


def write_out(count, *refs):
    sources, targets, sem = refs[: count + CHUNKS], refs[count + CHUNKS : -1], refs[-1]
    copies = [
        pltpu.make_async_copy(sources[n], targets[n], sem.at[n]) for n in range(count)
    ]
    for ck in range(CHUNKS):
        n = count + ck
        copies.append(
            pltpu.make_async_copy(sources[n], targets[count].at[:, :, ck], sem.at[n])
        )
    for copy in copies:
        copy.start()
    for copy in copies:
        copy.wait()


def shards(ctx, dp, query, key_act, value_act, filter_taps, grad_out):
    _, channels, width = query.shape
    share = channels // ctx
    rows = share // CHUNKS
    ring = dp // PLANES
    constants = tables()
    vmem = pl.BlockSpec(memory_space=pltpu.VMEM)
    hbm = pl.BlockSpec(memory_space=pltpu.HBM)
    half = jax.ShapeDtypeStruct((channels, width), jnp.bfloat16)
    whole = jax.ShapeDtypeStruct((PLANES, ring, CHUNKS, rows, width), jnp.float32)
    part = jax.ShapeDtypeStruct((PLANES, ring, rows, width), jnp.float32)
    dma = pltpu.SemaphoreType.DMA
    full = pltpu.VMEM((channels, width), jnp.bfloat16)
    outs = pl.pallas_call(
        functools.partial(body, ctx, dp),
        out_shape=[half] * 4 + [part] * CHUNKS,
        in_specs=[hbm] * 6,
        out_specs=[vmem] * (4 + CHUNKS),
        scratch_shapes=[
            full,
            full,
            full,
            full,
            pltpu.VMEM(constants.shape, jnp.float32),
            pltpu.VMEM((8 * LANES, 2 * LANES), jnp.bfloat16),
            pltpu.VMEM((CHUNKS, 2, ctx, rows, width), jnp.float32),
            pltpu.VMEM((CHUNKS, 3, ctx, rows, width), jnp.float32),
            pltpu.VMEM((CHUNKS, 2, ctx, rows, width), jnp.float32),
            pltpu.VMEM((CHUNKS, 2, ctx, rows, width), jnp.float32),
            pltpu.VMEM((CHUNKS, PLANES, ring, rows, width), jnp.float32),
            pltpu.VMEM((CHUNKS, ring - 1, PLANES, rows, width), jnp.float32),
            pltpu.VMEM((CHUNKS, PLANES, rows, width), jnp.float32),
            pltpu.VMEM((CHUNKS, PLANES, PLANES, rows, width), jnp.float32),
            pltpu.VMEM((CHUNKS, PLANES, rows, width), jnp.float32),
            pltpu.VMEM((3, KEPT * rows, 2 * LANES), jnp.float32),
            pltpu.VMEM((CHUNKS, 3, KEPT * rows, 2 * LANES), jnp.float32),
            dma((5,)),
            dma((CHUNKS,)),
            dma((CHUNKS,)),
            dma((CHUNKS,)),
            dma((CHUNKS,)),
            dma((CHUNKS,)),
            dma((CHUNKS,)),
            dma((CHUNKS,)),
            dma((CHUNKS,)),
            dma((CHUNKS,)),
            dma((CHUNKS,)),
            dma((CHUNKS, PLANES, PLANES)),
            dma((CHUNKS, PLANES, PLANES)),
            dma((CHUNKS,)),
            dma((CHUNKS,)),
        ],
        compiler_params=pltpu.CompilerParams(
            collective_id=0, has_side_effects=True, vmem_limit_bytes=GRANT
        ),
        cost_estimate=pl.CostEstimate(
            flops=3 * 2 * 6 * KEPT * share * 256 * 256, bytes_accessed=4 * 2**20, transcendentals=0
        ),
        name="hyena",
    )(
        query.reshape(channels, width),
        key_act.reshape(channels, width),
        value_act.reshape(channels, width),
        grad_out.reshape(channels, width),
        filter_taps,
        jnp.asarray(constants),
    )
    outs = pl.pallas_call(
        functools.partial(write_out, 4),
        out_shape=[half] * 4 + [whole],
        in_specs=[vmem] * (4 + CHUNKS),
        out_specs=[hbm] * 5,
        scratch_shapes=[dma((4 + CHUNKS,))],
        compiler_params=pltpu.CompilerParams(vmem_limit_bytes=4 * 1024 * 1024),
        name="write_out",
    )(*outs)
    shape = query.shape
    return (
        outs[0].reshape(shape),
        outs[1].reshape(shape),
        outs[2].reshape(shape),
        outs[3].reshape(shape),
        outs[4].reshape(channels, width),
    )


def solution(mesh):
    row = P("dp", None, "ctx")
    taps = P(None, "ctx")
    return jax.shard_map(
        functools.partial(shards, mesh.shape["ctx"], mesh.shape["dp"]),
        mesh=mesh,
        in_specs=(row, row, row, taps, row),
        out_specs=(row, row, row, row, taps),
        check_vma=False,
    )
```

```python
import functools
import math

import jax
import jax.numpy as jnp
import numpy as np
from jax import lax
from jax.experimental import pallas as pl
from jax.experimental.pallas import tpu as pltpu
from jax.sharding import PartitionSpec as P

MESH = pl.DeviceIdType.MESH
LANES = 128
RADIX = 64
HALF = RADIX // 2
KEPT = HALF + 1
STRIDE = 40


def turn(value, numerator, denominator):
    real, imag = value
    numerator %= denominator
    eighth = numerator * 8
    if eighth % denominator == 0:
        step = eighth // denominator
        if step == 0:
            return (real, imag)
        if step == 2:
            return (imag, -real)
        if step == 4:
            return (-real, -imag)
        if step == 6:
            return (-imag, real)
        root = math.sqrt(0.5)
        if step == 1:
            return ((real + imag) * root, (imag - real) * root)
        if step == 3:
            return ((imag - real) * root, (real + imag) * -root)
        if step == 5:
            return ((real + imag) * -root, (real - imag) * root)
        return ((real - imag) * root, (real + imag) * root)
    cos = math.cos(2.0 * math.pi * numerator / denominator)
    sin = math.sin(2.0 * math.pi * numerator / denominator)
    return (real * cos + imag * sin, imag * cos - real * sin)


def complex_fft(values, sign):
    size = len(values)
    if size == 1:
        return values
    even = complex_fft(values[0::2], sign)
    odd = complex_fft(values[1::2], sign)
    low, high = [], []
    for k in range(size // 2):
        real, imag = turn(odd[k], sign * k, size)
        low.append((even[k][0] + real, even[k][1] + imag))
        high.append((even[k][0] - real, even[k][1] - imag))
    return low + high


def odd_forward(values):
    quarter = len(values) // 2
    order = 4 * quarter
    packed = [turn((values[n], -values[n + quarter]), n, order) for n in range(quarter)]
    out = complex_fft(packed, 1)
    found = {}
    for j in range(quarter):
        k = 4 * j + 1
        if k < order // 2:
            found[k] = out[j]
        else:
            found[order - k] = (out[j][0], -out[j][1])
    return found


def real_forward(values):
    size = len(values)
    if size == 2:
        return {0: (values[0] + values[1], None), 1: (values[0] - values[1], None)}
    half = size // 2
    evens = real_forward([values[n] + values[n + half] for n in range(half)])
    found = {2 * k: value for k, value in evens.items()}
    found.update(odd_forward([values[n] - values[n + half] for n in range(half)]))
    return found


def padded_forward(values):
    found = {2 * k: value for k, value in real_forward(values).items()}
    found.update(odd_forward(values))
    return found


def odd_inverse(found, order):
    quarter = order // 4
    packed = []
    for j in range(quarter):
        k = 4 * j + 1
        if k < order // 2:
            packed.append(found[k])
        else:
            real, imag = found[order - k]
            packed.append((real, -imag))
    out = complex_fft(packed, -1)
    out = [turn(out[n], -n, order) for n in range(quarter)]
    return [value[0] for value in out] + [-value[1] for value in out]


def real_inverse(found, size):
    if size == 2:
        return [found[0][0] + found[1][0], found[0][0] - found[1][0]]
    half = size // 2
    evens = real_inverse({k // 2: value for k, value in found.items() if k % 2 == 0}, half)
    odds = odd_inverse(found, size)
    return [evens[n] + odds[n] for n in range(half)] + [evens[n] - odds[n] for n in range(half)]


def padded_inverse(found):
    evens = real_inverse({k // 2: value for k, value in found.items() if k % 2 == 0}, HALF)
    odds = odd_inverse(found, RADIX)
    return [evens[n] + odds[n] for n in range(HALF)]


def tables():
    k = np.arange(LANES)
    angles = 2.0 * np.pi * (k[:, None] * k[None, :] % LANES) / LANES
    cos, sin = np.cos(angles), np.sin(angles)
    forward = np.block([[cos, -sin], [sin, cos]])
    inverse = forward.T

    def split(matrix):
        high = matrix.astype(np.float32).astype(jnp.bfloat16)
        low = (matrix - high.astype(np.float64)).astype(np.float32).astype(jnp.bfloat16)
        return high, low

    matrices = np.stack([*split(forward), *split(inverse)])
    length = RADIX * LANES
    first = np.arange(KEPT)
    angles = 2.0 * np.pi * (first[:, None] * k[None, :]) / length
    scale = np.where((first == 0) | (first == HALF), 1.0, 2.0)[:, None] / length
    twists = np.stack(
        [np.cos(angles), np.sin(angles), np.cos(angles) * scale, np.sin(angles) * scale]
    ).astype(np.float32)
    table = np.zeros((4, STRIDE, 2 * LANES), np.float32)
    table[:, :KEPT, :LANES] = twists
    return np.concatenate(
        [matrices.astype(np.float32).reshape(-1, 2 * LANES), table.reshape(-1, 2 * LANES)]
    )


CHUNKS = 4
PLANES = 2
GRANT = int(52.3 * 1024 * 1024)


def body(
    ctx,
    dp,
    q_hbm,
    k_hbm,
    v_hbm,
    g_hbm,
    f_hbm,
    c_hbm,
    out_ref,
    gq_ref,
    gk_ref,
    gv_ref,
    *rest,
):
    gf_refs = rest[:CHUNKS]
    (
        q_ref,
        k_ref,
        v_ref,
        g_ref,
        c_ref,
        w_ref,
        send_x,
        recv_x,
        send_y,
        recv_y,
        part_g,
        recv_g,
        sum_g,
        recv_s,
        own_s,
        spec_a,
        spec_b,
        plane_sem,
        go_sem,
        load_sem,
        own_sem,
        keep_sem,
        sx_send,
        sx_recv,
        sf_send,
        sf_recv,
        sy_send,
        sy_recv,
        sg_send,
        sg_recv,
        ss_send,
        ss_recv,
        sa_send,
        sa_recv,
    ) = rest[CHUNKS:]
    me_c = lax.axis_index("ctx")
    me_d = lax.axis_index("dp")
    ring = dp // PLANES
    channels, width = q_ref.shape
    share = channels // ctx
    rows = share // CHUNKS
    subs = rows // 8
    me_p, me_z = me_d // ring, lax.rem(me_d, ring)
    c_p, c_z = me_c // ring, lax.rem(me_c, ring)
    slot = lax.rem(me_z + ctx - me_c, ring)

    loads = [
        pltpu.make_async_copy(src, dst, load_sem.at[n])
        for n, (src, dst) in enumerate(
            [
                (k_hbm, k_ref),
                (v_hbm, v_ref),
                (q_hbm, q_ref),
                (g_hbm, g_ref),
                (c_hbm, c_ref),
            ]
        )
    ]
    for load in loads:
        load.start()

    def each(first, last, act):
        def step(i, carry):
            act(i)
            return carry

        lax.fori_loop(first, last, step, 0, unroll=True)

    def ctx_peer(i):
        return (me_d, lax.rem(me_c + i, ctx))

    def ring_peer(i):
        return (me_p * ring + lax.rem(me_z + i, ring), me_c)

    def swap_peer(plane, part):
        return (plane * ring + me_z, part * ring + slot)

    def is_self(plane, part):
        return (c_z == slot) & (plane == me_p) & (part == c_p)

    barrier = pltpu.get_barrier_semaphore()

    def signal(sem, peer):
        pl.semaphore_signal(sem, inc=1, device_id=peer, device_id_type=MESH)

    leads = me_c == 0

    def greet(i):
        peer = ctx_peer(i)
        pl.when(peer[1] != 0)(lambda: signal(barrier, peer))

    each(1, ctx, greet)
    swaps = [(plane, part) for plane in range(PLANES) for part in range(PLANES)]

    for load in loads[:4]:
        load.wait()

    def products(b, carry):
        at = pl.ds(b * share, share)
        mixed = k_ref[at, :].astype(jnp.float32) * v_ref[at, :].astype(jnp.float32)
        dconv = q_ref[at, :].astype(jnp.float32) * g_ref[at, :].astype(jnp.float32)
        for ck in range(CHUNKS):
            send_x[ck, 0, b] = mixed[ck * rows : (ck + 1) * rows]
            send_x[ck, 1, b] = dconv[ck * rows : (ck + 1) * rows]
        return carry

    lax.fori_loop(0, ctx, products, 0)

    @pl.when(jnp.logical_not(leads))
    def _():
        pl.semaphore_wait(barrier, ctx - 1)

    pl.when(me_c == 1)(lambda: signal(plane_sem, (me_d, 0)))

    @pl.when(leads)
    def _():
        pl.semaphore_wait(plane_sem, 1)
        each(1, ring, lambda i: signal(barrier, ring_peer(i)))
        for plane in range(PLANES):
            pl.when(plane != me_p)(lambda: signal(barrier, (plane * ring + me_z, me_c)))

    def remote(src, dst, send, recv, peer):
        return pltpu.make_async_remote_copy(
            src_ref=src,
            dst_ref=dst,
            send_sem=send,
            recv_sem=recv,
            device_id=peer,
            device_id_type=MESH,
        )

    def copy_x(ck, i):
        peer = ctx_peer(i)
        return remote(
            send_x.at[ck, :, peer[1]],
            recv_x.at[ck, pl.ds(0, 2), me_c],
            sx_send.at[ck],
            sx_recv.at[ck],
            peer,
        )

    def copy_f(ck, i):
        peer = ctx_peer(i)
        return remote(
            f_hbm.at[pl.ds(peer[1] * share + ck * rows, rows), :],
            recv_x.at[ck, 2, me_c],
            sf_send.at[ck],
            sf_recv.at[ck],
            peer,
        )

    def own_f(ck):
        return pltpu.make_async_copy(
            f_hbm.at[pl.ds(me_c * share + ck * rows, rows), :],
            recv_x.at[ck, 2, me_c],
            own_sem.at[ck],
        )

    def copy_y(ck, i):
        peer = ctx_peer(i)
        return remote(
            send_y.at[ck, :, peer[1]],
            recv_y.at[ck, :, me_c],
            sy_send.at[ck],
            sy_recv.at[ck],
            peer,
        )

    def copy_g(ck, i):
        peer = ring_peer(i)
        return remote(
            part_g.at[ck, :, lax.rem(slot + i, ring)],
            recv_g.at[ck, i - 1],
            sg_send.at[ck],
            sg_recv.at[ck],
            peer,
        )

    def copy_s(ck, plane, part):
        return remote(
            sum_g.at[ck, part],
            recv_s.at[ck, c_p, me_p],
            ss_send.at[ck, plane, part],
            ss_recv.at[ck, c_p, me_p],
            swap_peer(plane, part),
        )

    def copy_a(ck, i):
        return remote(
            own_s.at[ck],
            gf_refs[ck].at[:, slot],
            sa_send.at[ck],
            sa_recv.at[ck],
            ring_peer(i),
        )

    def keep(ck):
        return pltpu.make_async_copy(own_s.at[ck], gf_refs[ck].at[:, slot], keep_sem.at[ck])

    def drain(ref, sem):
        pltpu.make_async_copy(ref, ref, sem).wait()

    def chunks(act):
        def step(ck, carry):
            act(ck)
            return carry

        lax.fori_loop(0, CHUNKS, step, 0)

    chunks(lambda ck: each(1, ctx, lambda i: copy_x(ck, i).start()))

    @pl.when(leads)
    def _():
        pl.semaphore_wait(barrier, ring - 1 + PLANES - 1)
        each(1, ctx, lambda i: signal(go_sem, ctx_peer(i)))


    def first_f(ck):
        each(1, ctx, lambda i: copy_f(ck, i).start())
        own_f(ck).start()

    def own_x(ck):
        recv_x[ck, 0, me_c] = send_x[ck, 0, me_c]
        recv_x[ck, 1, me_c] = send_x[ck, 1, me_c]

    chunks(own_x)
    for load in loads[4:]:
        load.wait()
    w_ref[...] = c_ref[pl.ds(0, w_ref.shape[0]), :].astype(jnp.bfloat16)

    def twist(which, k):
        return c_ref[pl.ds(w_ref.shape[0] + which * STRIDE + k, 1), pl.ds(0, LANES)]

    def weight(which):
        return w_ref[pl.ds(which * 2 * LANES, 2 * LANES), :]

    re, im = pl.ds(0, LANES), pl.ds(LANES, LANES)

    def forward(ck, sig, sub):
        at = pl.ds(sub * 8, 8)
        values = [
            recv_x[ck, sig, n // 2, at, pl.ds((n % 2) * LANES, LANES)] for n in range(HALF)
        ]
        found = padded_forward(values)
        for k in range(KEPT):
            cos, sin = twist(0, k), twist(1, k)
            real, imag = found[k]
            to = pl.ds(k * rows + sub * 8, 8)
            if k == 0:
                spec_a[sig, to, re] = real
                spec_a[sig, to, im] = jnp.zeros_like(real)
            elif imag is None:
                spec_a[sig, to, re] = real * cos
                spec_a[sig, to, im] = -(real * sin)
            else:
                spec_a[sig, to, re] = real * cos + imag * sin
                spec_a[sig, to, im] = imag * cos - real * sin

    def inverse(ck, sig, sub, store):
        found = {}
        for k in range(KEPT):
            cos, sin = twist(2, k), twist(3, k)
            at = pl.ds(k * rows + sub * 8, 8)
            real = spec_a[sig, at, re]
            imag = spec_a[sig, at, im]
            if k == 0 or k == HALF:
                found[k] = (real * cos - imag * sin, None)
            else:
                found[k] = (real * cos - imag * sin, imag * cos + real * sin)
        values = padded_inverse(found)
        for n in range(HALF):
            store(n // 2, pl.ds(sub * 8, 8), pl.ds((n % 2) * LANES, LANES), values[n])

    def matmul(src, dst, which):
        data = src[...].reshape(-1, 2 * LANES)
        height = data.shape[0]
        high = data.astype(jnp.bfloat16)
        low = (data - high.astype(jnp.float32)).astype(jnp.bfloat16)
        both = jnp.dot(
            jnp.concatenate([high, low], axis=0),
            weight(2 * which),
            preferred_element_type=jnp.float32,
        )
        rest = jnp.dot(high, weight(2 * which + 1), preferred_element_type=jnp.float32)
        dst[...] = (both[:height] + both[height:] + rest).reshape(dst.shape)

    def loop(count, act, unroll=1):
        def step(i, carry):
            act(i)
            return carry

        lax.fori_loop(0, count, step, 0, unroll=unroll)

    def filter_grad(ck):
        drain(recv_x.at[ck, pl.ds(0, 2), pl.ds(0, ctx - 1)], sx_recv.at[ck])
        loop(2 * subs, lambda n: forward(ck, n // subs, lax.rem(n, subs)))
        matmul(spec_a.at[pl.ds(0, 2)], spec_b.at[ck, pl.ds(0, 2)], 0)

        def pointwise(k):
            at = pl.ds(k * rows, rows)
            z_re, z_im = spec_b[ck, 0, at, re], spec_b[ck, 0, at, im]
            d_re, d_im = spec_b[ck, 1, at, re], spec_b[ck, 1, at, im]
            spec_a[0, at, re] = z_re * d_re + z_im * d_im
            spec_a[0, at, im] = z_re * d_im - z_im * d_re

        loop(KEPT, pointwise, 11)
        matmul(spec_a.at[0], spec_a.at[1], 1)

        def store(block, at, lanes, value):
            part_g[ck, block // ring, block % ring, at, lanes] = value

        loop(subs, lambda sub: inverse(ck, 1, sub, store))

        @pl.when((ck == 0) & jnp.logical_not(leads))
        def _():
            pl.semaphore_wait(go_sem, 1)

        each(1, ring, lambda i: copy_g(ck, i).start())

    def convolutions(ck):
        drain(recv_x.at[ck, 2, pl.ds(0, ctx - 1)], sf_recv.at[ck])
        own_f(ck).wait()
        loop(subs, lambda sub: forward(ck, 2, sub))
        matmul(spec_a.at[2], spec_b.at[ck, 2], 0)

        def pointwise(k):
            at = pl.ds(k * rows, rows)
            z_re, z_im = spec_b[ck, 0, at, re], spec_b[ck, 0, at, im]
            d_re, d_im = spec_b[ck, 1, at, re], spec_b[ck, 1, at, im]
            f_re, f_im = spec_b[ck, 2, at, re], spec_b[ck, 2, at, im]
            spec_a[0, at, re] = z_re * f_re - z_im * f_im
            spec_a[0, at, im] = z_re * f_im + z_im * f_re
            spec_a[1, at, re] = f_re * d_re + f_im * d_im
            spec_a[1, at, im] = f_re * d_im - f_im * d_re

        loop(KEPT, pointwise, 11)
        matmul(spec_a.at[pl.ds(0, 2)], spec_a.at[pl.ds(0, 2)], 1)

        def back(n):
            sig, sub = n // subs, lax.rem(n, subs)

            def store(block, at, lanes, value):
                send_y[ck, sig, block, at, lanes] = value

            inverse(ck, sig, sub, store)

        loop(2 * subs, back)
        each(1, ctx, lambda i: copy_y(ck, i).start())
        recv_y[ck, 0, me_c] = send_y[ck, 0, me_c]
        recv_y[ck, 1, me_c] = send_y[ck, 1, me_c]

    def reduce(ck):
        drain(recv_g.at[ck], sg_recv.at[ck])
        for part in range(PLANES):
            total = part_g[ck, part, slot]
            for i in range(ring - 1):
                total = total + recv_g[ck, i, part]
            sum_g[ck, part] = total
        for plane, part in swaps:
            mine = is_self(plane, part)

            @pl.when(jnp.logical_not(mine))
            def _():
                copy_s(ck, plane, part).start()

            @pl.when(mine)
            def _():
                recv_s[ck, part, plane] = sum_g[ck, part]

    scale = 1.0 / math.sqrt(dp * ctx * width)

    def gather(ck):
        for plane, part in swaps:

            @pl.when(jnp.logical_not(is_self(plane, part)))
            def _():
                drain(recv_s.at[ck, part, plane], ss_recv.at[ck, part, plane])

        for part in range(PLANES):
            total = recv_s[ck, part, 0]
            for plane in range(1, PLANES):
                total = total + recv_s[ck, part, plane]
            own_s[ck, part] = total * scale
        for chunk in range(CHUNKS):

            @pl.when(ck == chunk)
            def _():
                each(1, ring, lambda i: copy_a(chunk, i).start())
                keep(chunk).start()

    def stage(step):
        pl.when(step < CHUNKS)(lambda: filter_grad(step))
        pl.when(step == 1)(lambda: chunks(first_f))
        pl.when((step >= 2) & (step < CHUNKS + 2))(lambda: reduce(step - 2))

        @pl.when(step >= 3)
        def _():
            convolutions(step - 3)
            gather(step - 3)

    loop(CHUNKS + 3, stage)

    for ck in range(CHUNKS):
        drain(recv_y.at[ck, :, pl.ds(0, ctx - 1)], sy_recv.at[ck])

    def outputs(b):
        at = pl.ds(b * share, share)
        conv = jnp.concatenate([recv_y[ck, 0, b] for ck in range(CHUNKS)], axis=0)
        dmixed = jnp.concatenate([recv_y[ck, 1, b] for ck in range(CHUNKS)], axis=0)
        out_ref[at, :] = (q_ref[at, :].astype(jnp.float32) * conv).astype(jnp.bfloat16)
        gq_ref[at, :] = (g_ref[at, :].astype(jnp.float32) * conv).astype(jnp.bfloat16)
        gk_ref[at, :] = (v_ref[at, :].astype(jnp.float32) * dmixed).astype(jnp.bfloat16)
        gv_ref[at, :] = (k_ref[at, :].astype(jnp.float32) * dmixed).astype(jnp.bfloat16)

    loop(ctx, outputs)

    def finish(ck):
        drain(recv_x.at[ck, pl.ds(0, 2), pl.ds(0, ctx - 1)], sx_send.at[ck])
        drain(recv_x.at[ck, 2, pl.ds(0, ctx - 1)], sf_send.at[ck])
        drain(recv_y.at[ck, :, pl.ds(0, ctx - 1)], sy_send.at[ck])
        drain(recv_g.at[ck], sg_send.at[ck])
        for plane, part in swaps:

            @pl.when(jnp.logical_not(is_self(plane, part)))
            def _():
                drain(sum_g.at[ck, part], ss_send.at[ck, plane, part])


    chunks(finish)
    for ck in range(CHUNKS):
        keep(ck).wait()
        drain(gf_refs[ck].at[:, pl.ds(0, ring - 1)], sa_send.at[ck])
        drain(gf_refs[ck].at[:, pl.ds(0, ring - 1)], sa_recv.at[ck])


def write_out(count, *refs):
    sources, targets, sem = refs[: count + CHUNKS], refs[count + CHUNKS : -1], refs[-1]
    copies = [
        pltpu.make_async_copy(sources[n], targets[n], sem.at[n]) for n in range(count)
    ]
    for ck in range(CHUNKS):
        n = count + ck
        copies.append(
            pltpu.make_async_copy(sources[n], targets[count].at[:, :, ck], sem.at[n])
        )
    for copy in copies:
        copy.start()
    for copy in copies:
        copy.wait()


def shards(ctx, dp, query, key_act, value_act, filter_taps, grad_out):
    _, channels, width = query.shape
    share = channels // ctx
    rows = share // CHUNKS
    ring = dp // PLANES
    constants = tables()
    vmem = pl.BlockSpec(memory_space=pltpu.VMEM)
    hbm = pl.BlockSpec(memory_space=pltpu.HBM)
    half = jax.ShapeDtypeStruct((channels, width), jnp.bfloat16)
    whole = jax.ShapeDtypeStruct((PLANES, ring, CHUNKS, rows, width), jnp.float32)
    part = jax.ShapeDtypeStruct((PLANES, ring, rows, width), jnp.float32)
    dma = pltpu.SemaphoreType.DMA
    full = pltpu.VMEM((channels, width), jnp.bfloat16)
    outs = pl.pallas_call(
        functools.partial(body, ctx, dp),
        out_shape=[half] * 4 + [part] * CHUNKS,
        in_specs=[hbm] * 6,
        out_specs=[vmem] * (4 + CHUNKS),
        scratch_shapes=[
            full,
            full,
            full,
            full,
            pltpu.VMEM(constants.shape, jnp.float32),
            pltpu.VMEM((8 * LANES, 2 * LANES), jnp.bfloat16),
            pltpu.VMEM((CHUNKS, 2, ctx, rows, width), jnp.float32),
            pltpu.VMEM((CHUNKS, 3, ctx, rows, width), jnp.float32),
            pltpu.VMEM((CHUNKS, 2, ctx, rows, width), jnp.float32),
            pltpu.VMEM((CHUNKS, 2, ctx, rows, width), jnp.float32),
            pltpu.VMEM((CHUNKS, PLANES, ring, rows, width), jnp.float32),
            pltpu.VMEM((CHUNKS, ring - 1, PLANES, rows, width), jnp.float32),
            pltpu.VMEM((CHUNKS, PLANES, rows, width), jnp.float32),
            pltpu.VMEM((CHUNKS, PLANES, PLANES, rows, width), jnp.float32),
            pltpu.VMEM((CHUNKS, PLANES, rows, width), jnp.float32),
            pltpu.VMEM((3, KEPT * rows, 2 * LANES), jnp.float32),
            pltpu.VMEM((CHUNKS, 3, KEPT * rows, 2 * LANES), jnp.float32),
            pltpu.SemaphoreType.REGULAR,
            pltpu.SemaphoreType.REGULAR,
            dma((5,)),
            dma((CHUNKS,)),
            dma((CHUNKS,)),
            dma((CHUNKS,)),
            dma((CHUNKS,)),
            dma((CHUNKS,)),
            dma((CHUNKS,)),
            dma((CHUNKS,)),
            dma((CHUNKS,)),
            dma((CHUNKS,)),
            dma((CHUNKS,)),
            dma((CHUNKS, PLANES, PLANES)),
            dma((CHUNKS, PLANES, PLANES)),
            dma((CHUNKS,)),
            dma((CHUNKS,)),
        ],
        compiler_params=pltpu.CompilerParams(
            collective_id=0, has_side_effects=True, vmem_limit_bytes=GRANT
        ),
        cost_estimate=pl.CostEstimate(
            flops=3 * 2 * 6 * KEPT * share * 256 * 256, bytes_accessed=4 * 2**20, transcendentals=0
        ),
        name="hyena",
    )(
        query.reshape(channels, width),
        key_act.reshape(channels, width),
        value_act.reshape(channels, width),
        grad_out.reshape(channels, width),
        filter_taps,
        jnp.asarray(constants),
    )
    outs = pl.pallas_call(
        functools.partial(write_out, 4),
        out_shape=[half] * 4 + [whole],
        in_specs=[vmem] * (4 + CHUNKS),
        out_specs=[hbm] * 5,
        scratch_shapes=[dma((4 + CHUNKS,))],
        compiler_params=pltpu.CompilerParams(vmem_limit_bytes=4 * 1024 * 1024),
        name="write_out",
    )(*outs)
    shape = query.shape
    return (
        outs[0].reshape(shape),
        outs[1].reshape(shape),
        outs[2].reshape(shape),
        outs[3].reshape(shape),
        outs[4].reshape(channels, width),
    )


def solution(mesh):
    row = P("dp", None, "ctx")
    taps = P(None, "ctx")
    return jax.shard_map(
        functools.partial(shards, mesh.shape["ctx"], mesh.shape["dp"]),
        mesh=mesh,
        in_specs=(row, row, row, taps, row),
        out_specs=(row, row, row, row, taps),
        check_vma=False,
    )
```

```python
import functools
import math

import jax
import jax.numpy as jnp
import numpy as np
from jax import lax
from jax.experimental import pallas as pl
from jax.experimental.pallas import tpu as pltpu
from jax.sharding import PartitionSpec as P

MESH = pl.DeviceIdType.MESH
LANES = 128
RADIX = 64
HALF = RADIX // 2
KEPT = HALF + 1
STRIDE = 40


def turn(value, numerator, denominator):
    real, imag = value
    numerator %= denominator
    eighth = numerator * 8
    if eighth % denominator == 0:
        step = eighth // denominator
        if step == 0:
            return (real, imag)
        if step == 2:
            return (imag, -real)
        if step == 4:
            return (-real, -imag)
        if step == 6:
            return (-imag, real)
        root = math.sqrt(0.5)
        if step == 1:
            return ((real + imag) * root, (imag - real) * root)
        if step == 3:
            return ((imag - real) * root, (real + imag) * -root)
        if step == 5:
            return ((real + imag) * -root, (real - imag) * root)
        return ((real - imag) * root, (real + imag) * root)
    cos = math.cos(2.0 * math.pi * numerator / denominator)
    sin = math.sin(2.0 * math.pi * numerator / denominator)
    return (real * cos + imag * sin, imag * cos - real * sin)


def complex_fft(values, sign):
    size = len(values)
    if size == 1:
        return values
    even = complex_fft(values[0::2], sign)
    odd = complex_fft(values[1::2], sign)
    low, high = [], []
    for k in range(size // 2):
        real, imag = turn(odd[k], sign * k, size)
        low.append((even[k][0] + real, even[k][1] + imag))
        high.append((even[k][0] - real, even[k][1] - imag))
    return low + high


def odd_forward(values):
    quarter = len(values) // 2
    order = 4 * quarter
    packed = [turn((values[n], -values[n + quarter]), n, order) for n in range(quarter)]
    out = complex_fft(packed, 1)
    found = {}
    for j in range(quarter):
        k = 4 * j + 1
        if k < order // 2:
            found[k] = out[j]
        else:
            found[order - k] = (out[j][0], -out[j][1])
    return found


def real_forward(values):
    size = len(values)
    if size == 2:
        return {0: (values[0] + values[1], None), 1: (values[0] - values[1], None)}
    half = size // 2
    evens = real_forward([values[n] + values[n + half] for n in range(half)])
    found = {2 * k: value for k, value in evens.items()}
    found.update(odd_forward([values[n] - values[n + half] for n in range(half)]))
    return found


def padded_forward(values):
    found = {2 * k: value for k, value in real_forward(values).items()}
    found.update(odd_forward(values))
    return found


def odd_inverse(found, order):
    quarter = order // 4
    packed = []
    for j in range(quarter):
        k = 4 * j + 1
        if k < order // 2:
            packed.append(found[k])
        else:
            real, imag = found[order - k]
            packed.append((real, -imag))
    out = complex_fft(packed, -1)
    out = [turn(out[n], -n, order) for n in range(quarter)]
    return [value[0] for value in out] + [-value[1] for value in out]


def real_inverse(found, size):
    if size == 2:
        return [found[0][0] + found[1][0], found[0][0] - found[1][0]]
    half = size // 2
    evens = real_inverse({k // 2: value for k, value in found.items() if k % 2 == 0}, half)
    odds = odd_inverse(found, size)
    return [evens[n] + odds[n] for n in range(half)] + [evens[n] - odds[n] for n in range(half)]


def padded_inverse(found):
    evens = real_inverse({k // 2: value for k, value in found.items() if k % 2 == 0}, HALF)
    odds = odd_inverse(found, RADIX)
    return [evens[n] + odds[n] for n in range(HALF)]


def tables():
    k = np.arange(LANES)
    angles = 2.0 * np.pi * (k[:, None] * k[None, :] % LANES) / LANES
    cos, sin = np.cos(angles), np.sin(angles)
    forward = np.block([[cos, -sin], [sin, cos]])
    inverse = forward.T

    def split(matrix):
        high = matrix.astype(np.float32).astype(jnp.bfloat16)
        low = (matrix - high.astype(np.float64)).astype(np.float32).astype(jnp.bfloat16)
        return high, low

    matrices = np.stack([*split(forward), *split(inverse)])
    length = RADIX * LANES
    first = np.arange(KEPT)
    angles = 2.0 * np.pi * (first[:, None] * k[None, :]) / length
    scale = np.where((first == 0) | (first == HALF), 1.0, 2.0)[:, None] / length
    twists = np.stack(
        [np.cos(angles), np.sin(angles), np.cos(angles) * scale, np.sin(angles) * scale]
    ).astype(np.float32)
    table = np.zeros((4, STRIDE, 2 * LANES), np.float32)
    table[:, :KEPT, :LANES] = twists
    return np.concatenate(
        [matrices.astype(np.float32).reshape(-1, 2 * LANES), table.reshape(-1, 2 * LANES)]
    )


CHUNKS = 4
PLANES = 2
GRANT = int(52.3 * 1024 * 1024)


def body(
    ctx,
    dp,
    q_hbm,
    k_hbm,
    v_hbm,
    g_hbm,
    f_hbm,
    c_hbm,
    out_ref,
    gq_ref,
    gk_ref,
    gv_ref,
    *rest,
):
    gf_refs = rest[:CHUNKS]
    (
        q_ref,
        k_ref,
        v_ref,
        g_ref,
        c_ref,
        w_ref,
        send_x,
        recv_x,
        send_y,
        recv_y,
        part_g,
        recv_g,
        sum_g,
        recv_s,
        own_s,
        spec_a,
        spec_b,
        plane_sem,
        go_sem,
        load_sem,
        own_sem,
        keep_sem,
        sx_send,
        sx_recv,
        sf_send,
        sf_recv,
        sy_send,
        sy_recv,
        sg_send,
        sg_recv,
        ss_send,
        ss_recv,
        sa_send,
        sa_recv,
    ) = rest[CHUNKS:]
    me_c = lax.axis_index("ctx")
    me_d = lax.axis_index("dp")
    ring = dp // PLANES
    channels, width = q_ref.shape
    share = channels // ctx
    rows = share // CHUNKS
    subs = rows // 8
    me_p, me_z = me_d // ring, lax.rem(me_d, ring)
    c_p, c_z = me_c // ring, lax.rem(me_c, ring)
    slot = lax.rem(me_z + ctx - me_c, ring)

    loads = [
        pltpu.make_async_copy(src, dst, load_sem.at[n])
        for n, (src, dst) in enumerate(
            [
                (k_hbm, k_ref),
                (v_hbm, v_ref),
                (q_hbm, q_ref),
                (g_hbm, g_ref),
                (c_hbm, c_ref),
            ]
        )
    ]
    for load in loads:
        load.start()

    def each(first, last, act):
        def step(i, carry):
            act(i)
            return carry

        lax.fori_loop(first, last, step, 0, unroll=True)

    def ctx_peer(i):
        return (me_d, lax.rem(me_c + i, ctx))

    def ring_peer(i):
        return (me_p * ring + lax.rem(me_z + i, ring), me_c)

    def swap_peer(plane, part):
        return (plane * ring + me_z, part * ring + slot)

    def is_self(plane, part):
        return (c_z == slot) & (plane == me_p) & (part == c_p)

    barrier = pltpu.get_barrier_semaphore()

    def signal(sem, peer):
        pl.semaphore_signal(sem, inc=1, device_id=peer, device_id_type=MESH)

    leads = me_c == 0

    def greet(i):
        peer = ctx_peer(i)
        pl.when(peer[1] != 0)(lambda: signal(barrier, peer))

    each(1, ctx, greet)
    swaps = [(plane, part) for plane in range(PLANES) for part in range(PLANES)]

    for load in loads[:4]:
        load.wait()

    def products(b, carry):
        at = pl.ds(b * share, share)
        mixed = k_ref[at, :].astype(jnp.float32) * v_ref[at, :].astype(jnp.float32)
        dconv = q_ref[at, :].astype(jnp.float32) * g_ref[at, :].astype(jnp.float32)
        for ck in range(CHUNKS):
            send_x[ck, 0, b] = mixed[ck * rows : (ck + 1) * rows]
            send_x[ck, 1, b] = dconv[ck * rows : (ck + 1) * rows]
        return carry

    lax.fori_loop(0, ctx, products, 0)

    @pl.when(jnp.logical_not(leads))
    def _():
        pl.semaphore_wait(barrier, ctx - 1)

    pl.when(me_c == 1)(lambda: signal(plane_sem, (me_d, 0)))

    @pl.when(leads)
    def _():
        pl.semaphore_wait(plane_sem, 1)
        each(1, ring, lambda i: signal(barrier, ring_peer(i)))
        for plane in range(PLANES):
            pl.when(plane != me_p)(lambda: signal(barrier, (plane * ring + me_z, me_c)))

    def remote(src, dst, send, recv, peer):
        return pltpu.make_async_remote_copy(
            src_ref=src,
            dst_ref=dst,
            send_sem=send,
            recv_sem=recv,
            device_id=peer,
            device_id_type=MESH,
        )

    def copy_x(ck, i):
        peer = ctx_peer(i)
        return remote(
            send_x.at[ck, :, peer[1]],
            recv_x.at[ck, pl.ds(0, 2), me_c],
            sx_send.at[ck],
            sx_recv.at[ck],
            peer,
        )

    def copy_f(ck, i):
        peer = ctx_peer(i)
        return remote(
            f_hbm.at[pl.ds(peer[1] * share + ck * rows, rows), :],
            recv_x.at[ck, 2, me_c],
            sf_send.at[ck],
            sf_recv.at[ck],
            peer,
        )

    def own_f(ck):
        return pltpu.make_async_copy(
            f_hbm.at[pl.ds(me_c * share + ck * rows, rows), :],
            recv_x.at[ck, 2, me_c],
            own_sem.at[ck],
        )

    def copy_y(ck, i):
        peer = ctx_peer(i)
        return remote(
            send_y.at[ck, :, peer[1]],
            recv_y.at[ck, :, me_c],
            sy_send.at[ck],
            sy_recv.at[ck],
            peer,
        )

    def copy_g(ck, i):
        peer = ring_peer(i)
        return remote(
            part_g.at[ck, :, lax.rem(slot + i, ring)],
            recv_g.at[ck, i - 1],
            sg_send.at[ck],
            sg_recv.at[ck],
            peer,
        )

    def copy_s(ck, plane, part):
        return remote(
            sum_g.at[ck, part],
            recv_s.at[ck, c_p, me_p],
            ss_send.at[ck, plane, part],
            ss_recv.at[ck, c_p, me_p],
            swap_peer(plane, part),
        )

    def copy_a(ck, i):
        return remote(
            own_s.at[ck],
            gf_refs[ck].at[:, slot],
            sa_send.at[ck],
            sa_recv.at[ck],
            ring_peer(i),
        )

    def keep(ck):
        return pltpu.make_async_copy(own_s.at[ck], gf_refs[ck].at[:, slot], keep_sem.at[ck])

    def drain(ref, sem):
        pltpu.make_async_copy(ref, ref, sem).wait()

    def chunks(act):
        def step(ck, carry):
            act(ck)
            return carry

        lax.fori_loop(0, CHUNKS, step, 0)

    chunks(lambda ck: each(1, ctx, lambda i: copy_x(ck, i).start()))

    @pl.when(leads)
    def _():
        pl.semaphore_wait(barrier, ring - 1 + PLANES - 1)
        each(1, ctx, lambda i: signal(go_sem, ctx_peer(i)))


    def first_f(ck):
        each(1, ctx, lambda i: copy_f(ck, i).start())
        own_f(ck).start()

    def own_x(ck):
        recv_x[ck, 0, me_c] = send_x[ck, 0, me_c]
        recv_x[ck, 1, me_c] = send_x[ck, 1, me_c]

    chunks(own_x)
    for load in loads[4:]:
        load.wait()
    w_ref[...] = c_ref[pl.ds(0, w_ref.shape[0]), :].astype(jnp.bfloat16)

    def twist(which, k):
        return c_ref[pl.ds(w_ref.shape[0] + which * STRIDE + k, 1), pl.ds(0, LANES)]

    def weight(which):
        return w_ref[pl.ds(which * 2 * LANES, 2 * LANES), :]

    re, im = pl.ds(0, LANES), pl.ds(LANES, LANES)

    def forward(ck, sig, sub):
        at = pl.ds(sub * 8, 8)
        values = [
            recv_x[ck, sig, n // 2, at, pl.ds((n % 2) * LANES, LANES)] for n in range(HALF)
        ]
        found = padded_forward(values)
        for k in range(KEPT):
            cos, sin = twist(0, k), twist(1, k)
            real, imag = found[k]
            to = pl.ds(k * rows + sub * 8, 8)
            if k == 0:
                spec_a[sig, to, re] = real
                spec_a[sig, to, im] = jnp.zeros_like(real)
            elif imag is None:
                spec_a[sig, to, re] = real * cos
                spec_a[sig, to, im] = -(real * sin)
            else:
                spec_a[sig, to, re] = real * cos + imag * sin
                spec_a[sig, to, im] = imag * cos - real * sin

    def inverse(ck, sig, sub, store):
        found = {}
        for k in range(KEPT):
            cos, sin = twist(2, k), twist(3, k)
            at = pl.ds(k * rows + sub * 8, 8)
            real = spec_a[sig, at, re]
            imag = spec_a[sig, at, im]
            if k == 0 or k == HALF:
                found[k] = (real * cos - imag * sin, None)
            else:
                found[k] = (real * cos - imag * sin, imag * cos + real * sin)
        values = padded_inverse(found)
        for n in range(HALF):
            store(n // 2, pl.ds(sub * 8, 8), pl.ds((n % 2) * LANES, LANES), values[n])

    def matmul(src, dst, which):
        data = src[...].reshape(-1, 2 * LANES)
        height = data.shape[0]
        high = data.astype(jnp.bfloat16)
        low = (data - high.astype(jnp.float32)).astype(jnp.bfloat16)
        both = jnp.dot(
            jnp.concatenate([high, low], axis=0),
            weight(2 * which),
            preferred_element_type=jnp.float32,
        )
        rest = jnp.dot(high, weight(2 * which + 1), preferred_element_type=jnp.float32)
        dst[...] = (both[:height] + both[height:] + rest).reshape(dst.shape)

    def loop(count, act, unroll=1):
        def step(i, carry):
            act(i)
            return carry

        lax.fori_loop(0, count, step, 0, unroll=unroll)

    def filter_grad(ck):
        drain(recv_x.at[ck, pl.ds(0, 2), pl.ds(0, ctx - 1)], sx_recv.at[ck])
        loop(2 * subs, lambda n: forward(ck, n // subs, lax.rem(n, subs)))
        matmul(spec_a.at[pl.ds(0, 2)], spec_b.at[ck, pl.ds(0, 2)], 0)

        def pointwise(k):
            at = pl.ds(k * rows, rows)
            z_re, z_im = spec_b[ck, 0, at, re], spec_b[ck, 0, at, im]
            d_re, d_im = spec_b[ck, 1, at, re], spec_b[ck, 1, at, im]
            spec_a[0, at, re] = z_re * d_re + z_im * d_im
            spec_a[0, at, im] = z_re * d_im - z_im * d_re

        loop(KEPT, pointwise, 11)
        matmul(spec_a.at[0], spec_a.at[1], 1)

        def store(block, at, lanes, value):
            part_g[ck, block // ring, block % ring, at, lanes] = value

        loop(subs, lambda sub: inverse(ck, 1, sub, store))

        @pl.when((ck == 0) & jnp.logical_not(leads))
        def _():
            pl.semaphore_wait(go_sem, 1)

        each(1, ring, lambda i: copy_g(ck, i).start())

    def convolutions(ck):
        drain(recv_x.at[ck, 2, pl.ds(0, ctx - 1)], sf_recv.at[ck])
        own_f(ck).wait()
        loop(subs, lambda sub: forward(ck, 2, sub))
        matmul(spec_a.at[2], spec_b.at[ck, 2], 0)

        def pointwise(k):
            at = pl.ds(k * rows, rows)
            z_re, z_im = spec_b[ck, 0, at, re], spec_b[ck, 0, at, im]
            d_re, d_im = spec_b[ck, 1, at, re], spec_b[ck, 1, at, im]
            f_re, f_im = spec_b[ck, 2, at, re], spec_b[ck, 2, at, im]
            spec_a[0, at, re] = z_re * f_re - z_im * f_im
            spec_a[0, at, im] = z_re * f_im + z_im * f_re
            spec_a[1, at, re] = f_re * d_re + f_im * d_im
            spec_a[1, at, im] = f_re * d_im - f_im * d_re

        loop(KEPT, pointwise, 11)
        matmul(spec_a.at[pl.ds(0, 2)], spec_a.at[pl.ds(0, 2)], 1)

        def back(n):
            sig, sub = n // subs, lax.rem(n, subs)

            def store(block, at, lanes, value):
                send_y[ck, sig, block, at, lanes] = value

            inverse(ck, sig, sub, store)

        loop(2 * subs, back)
        each(1, ctx, lambda i: copy_y(ck, i).start())
        recv_y[ck, 0, me_c] = send_y[ck, 0, me_c]
        recv_y[ck, 1, me_c] = send_y[ck, 1, me_c]

    def reduce(ck):
        drain(recv_g.at[ck], sg_recv.at[ck])
        for part in range(PLANES):
            total = part_g[ck, part, slot]
            for i in range(ring - 1):
                total = total + recv_g[ck, i, part]
            sum_g[ck, part] = total
        for plane, part in swaps:
            mine = is_self(plane, part)

            @pl.when(jnp.logical_not(mine))
            def _():
                copy_s(ck, plane, part).start()

            @pl.when(mine)
            def _():
                recv_s[ck, part, plane] = sum_g[ck, part]

    scale = 1.0 / math.sqrt(dp * ctx * width)

    def gather(ck):
        for plane, part in swaps:

            @pl.when(jnp.logical_not(is_self(plane, part)))
            def _():
                drain(recv_s.at[ck, part, plane], ss_recv.at[ck, part, plane])

        for part in range(PLANES):
            total = recv_s[ck, part, 0]
            for plane in range(1, PLANES):
                total = total + recv_s[ck, part, plane]
            own_s[ck, part] = total * scale
        for chunk in range(CHUNKS):

            @pl.when(ck == chunk)
            def _():
                each(1, ring, lambda i: copy_a(chunk, i).start())
                keep(chunk).start()

    def stage(step):
        pl.when(step < CHUNKS)(lambda: first_f(step))
        pl.when(step < CHUNKS)(lambda: filter_grad(step))
        pl.when((step >= 2) & (step < CHUNKS + 2))(lambda: reduce(step - 2))

        @pl.when(step >= 3)
        def _():
            convolutions(step - 3)
            gather(step - 3)

    loop(CHUNKS + 3, stage)

    for ck in range(CHUNKS):
        drain(recv_y.at[ck, :, pl.ds(0, ctx - 1)], sy_recv.at[ck])

    def outputs(b):
        at = pl.ds(b * share, share)
        conv = jnp.concatenate([recv_y[ck, 0, b] for ck in range(CHUNKS)], axis=0)
        dmixed = jnp.concatenate([recv_y[ck, 1, b] for ck in range(CHUNKS)], axis=0)
        out_ref[at, :] = (q_ref[at, :].astype(jnp.float32) * conv).astype(jnp.bfloat16)
        gq_ref[at, :] = (g_ref[at, :].astype(jnp.float32) * conv).astype(jnp.bfloat16)
        gk_ref[at, :] = (v_ref[at, :].astype(jnp.float32) * dmixed).astype(jnp.bfloat16)
        gv_ref[at, :] = (k_ref[at, :].astype(jnp.float32) * dmixed).astype(jnp.bfloat16)

    loop(ctx, outputs)

    def finish(ck):
        drain(recv_x.at[ck, pl.ds(0, 2), pl.ds(0, ctx - 1)], sx_send.at[ck])
        drain(recv_x.at[ck, 2, pl.ds(0, ctx - 1)], sf_send.at[ck])
        drain(recv_y.at[ck, :, pl.ds(0, ctx - 1)], sy_send.at[ck])
        drain(recv_g.at[ck], sg_send.at[ck])
        for plane, part in swaps:

            @pl.when(jnp.logical_not(is_self(plane, part)))
            def _():
                drain(sum_g.at[ck, part], ss_send.at[ck, plane, part])


    chunks(finish)
    for ck in range(CHUNKS):
        keep(ck).wait()
        drain(gf_refs[ck].at[:, pl.ds(0, ring - 1)], sa_send.at[ck])
        drain(gf_refs[ck].at[:, pl.ds(0, ring - 1)], sa_recv.at[ck])


def write_out(count, *refs):
    sources, targets, sem = refs[: count + CHUNKS], refs[count + CHUNKS : -1], refs[-1]
    copies = [
        pltpu.make_async_copy(sources[n], targets[n], sem.at[n]) for n in range(count)
    ]
    for ck in range(CHUNKS):
        n = count + ck
        copies.append(
            pltpu.make_async_copy(sources[n], targets[count].at[:, :, ck], sem.at[n])
        )
    for copy in copies:
        copy.start()
    for copy in copies:
        copy.wait()


def shards(ctx, dp, query, key_act, value_act, filter_taps, grad_out):
    _, channels, width = query.shape
    share = channels // ctx
    rows = share // CHUNKS
    ring = dp // PLANES
    constants = tables()
    vmem = pl.BlockSpec(memory_space=pltpu.VMEM)
    hbm = pl.BlockSpec(memory_space=pltpu.HBM)
    half = jax.ShapeDtypeStruct((channels, width), jnp.bfloat16)
    whole = jax.ShapeDtypeStruct((PLANES, ring, CHUNKS, rows, width), jnp.float32)
    part = jax.ShapeDtypeStruct((PLANES, ring, rows, width), jnp.float32)
    dma = pltpu.SemaphoreType.DMA
    full = pltpu.VMEM((channels, width), jnp.bfloat16)
    outs = pl.pallas_call(
        functools.partial(body, ctx, dp),
        out_shape=[half] * 4 + [part] * CHUNKS,
        in_specs=[hbm] * 6,
        out_specs=[vmem] * (4 + CHUNKS),
        scratch_shapes=[
            full,
            full,
            full,
            full,
            pltpu.VMEM(constants.shape, jnp.float32),
            pltpu.VMEM((8 * LANES, 2 * LANES), jnp.bfloat16),
            pltpu.VMEM((CHUNKS, 2, ctx, rows, width), jnp.float32),
            pltpu.VMEM((CHUNKS, 3, ctx, rows, width), jnp.float32),
            pltpu.VMEM((CHUNKS, 2, ctx, rows, width), jnp.float32),
            pltpu.VMEM((CHUNKS, 2, ctx, rows, width), jnp.float32),
            pltpu.VMEM((CHUNKS, PLANES, ring, rows, width), jnp.float32),
            pltpu.VMEM((CHUNKS, ring - 1, PLANES, rows, width), jnp.float32),
            pltpu.VMEM((CHUNKS, PLANES, rows, width), jnp.float32),
            pltpu.VMEM((CHUNKS, PLANES, PLANES, rows, width), jnp.float32),
            pltpu.VMEM((CHUNKS, PLANES, rows, width), jnp.float32),
            pltpu.VMEM((3, KEPT * rows, 2 * LANES), jnp.float32),
            pltpu.VMEM((CHUNKS, 3, KEPT * rows, 2 * LANES), jnp.float32),
            pltpu.SemaphoreType.REGULAR,
            pltpu.SemaphoreType.REGULAR,
            dma((5,)),
            dma((CHUNKS,)),
            dma((CHUNKS,)),
            dma((CHUNKS,)),
            dma((CHUNKS,)),
            dma((CHUNKS,)),
            dma((CHUNKS,)),
            dma((CHUNKS,)),
            dma((CHUNKS,)),
            dma((CHUNKS,)),
            dma((CHUNKS,)),
            dma((CHUNKS, PLANES, PLANES)),
            dma((CHUNKS, PLANES, PLANES)),
            dma((CHUNKS,)),
            dma((CHUNKS,)),
        ],
        compiler_params=pltpu.CompilerParams(
            collective_id=0, has_side_effects=True, vmem_limit_bytes=GRANT
        ),
        cost_estimate=pl.CostEstimate(
            flops=3 * 2 * 6 * KEPT * share * 256 * 256, bytes_accessed=4 * 2**20, transcendentals=0
        ),
        name="hyena",
    )(
        query.reshape(channels, width),
        key_act.reshape(channels, width),
        value_act.reshape(channels, width),
        grad_out.reshape(channels, width),
        filter_taps,
        jnp.asarray(constants),
    )
    outs = pl.pallas_call(
        functools.partial(write_out, 4),
        out_shape=[half] * 4 + [whole],
        in_specs=[vmem] * (4 + CHUNKS),
        out_specs=[hbm] * 5,
        scratch_shapes=[dma((4 + CHUNKS,))],
        compiler_params=pltpu.CompilerParams(vmem_limit_bytes=4 * 1024 * 1024),
        name="write_out",
    )(*outs)
    shape = query.shape
    return (
        outs[0].reshape(shape),
        outs[1].reshape(shape),
        outs[2].reshape(shape),
        outs[3].reshape(shape),
        outs[4].reshape(channels, width),
    )


def solution(mesh):
    row = P("dp", None, "ctx")
    taps = P(None, "ctx")
    return jax.shard_map(
        functools.partial(shards, mesh.shape["ctx"], mesh.shape["dp"]),
        mesh=mesh,
        in_specs=(row, row, row, taps, row),
        out_specs=(row, row, row, row, taps),
        check_vma=False,
    )
```

```python
import functools
import math

import jax
import jax.numpy as jnp
import numpy as np
from jax import lax
from jax.experimental import pallas as pl
from jax.experimental.pallas import tpu as pltpu
from jax.sharding import PartitionSpec as P

MESH = pl.DeviceIdType.MESH
LANES = 128
RADIX = 64
HALF = RADIX // 2
KEPT = HALF + 1
STRIDE = 40


def turn(value, numerator, denominator):
    real, imag = value
    numerator %= denominator
    eighth = numerator * 8
    if eighth % denominator == 0:
        step = eighth // denominator
        if step == 0:
            return (real, imag)
        if step == 2:
            return (imag, -real)
        if step == 4:
            return (-real, -imag)
        if step == 6:
            return (-imag, real)
        root = math.sqrt(0.5)
        if step == 1:
            return ((real + imag) * root, (imag - real) * root)
        if step == 3:
            return ((imag - real) * root, (real + imag) * -root)
        if step == 5:
            return ((real + imag) * -root, (real - imag) * root)
        return ((real - imag) * root, (real + imag) * root)
    cos = math.cos(2.0 * math.pi * numerator / denominator)
    sin = math.sin(2.0 * math.pi * numerator / denominator)
    return (real * cos + imag * sin, imag * cos - real * sin)


def complex_fft(values, sign):
    size = len(values)
    if size == 1:
        return values
    even = complex_fft(values[0::2], sign)
    odd = complex_fft(values[1::2], sign)
    low, high = [], []
    for k in range(size // 2):
        real, imag = turn(odd[k], sign * k, size)
        low.append((even[k][0] + real, even[k][1] + imag))
        high.append((even[k][0] - real, even[k][1] - imag))
    return low + high


def odd_forward(values):
    quarter = len(values) // 2
    order = 4 * quarter
    packed = [turn((values[n], -values[n + quarter]), n, order) for n in range(quarter)]
    out = complex_fft(packed, 1)
    found = {}
    for j in range(quarter):
        k = 4 * j + 1
        if k < order // 2:
            found[k] = out[j]
        else:
            found[order - k] = (out[j][0], -out[j][1])
    return found


def real_forward(values):
    size = len(values)
    if size == 2:
        return {0: (values[0] + values[1], None), 1: (values[0] - values[1], None)}
    half = size // 2
    evens = real_forward([values[n] + values[n + half] for n in range(half)])
    found = {2 * k: value for k, value in evens.items()}
    found.update(odd_forward([values[n] - values[n + half] for n in range(half)]))
    return found


def padded_forward(values):
    found = {2 * k: value for k, value in real_forward(values).items()}
    found.update(odd_forward(values))
    return found


def odd_inverse(found, order):
    quarter = order // 4
    packed = []
    for j in range(quarter):
        k = 4 * j + 1
        if k < order // 2:
            packed.append(found[k])
        else:
            real, imag = found[order - k]
            packed.append((real, -imag))
    out = complex_fft(packed, -1)
    out = [turn(out[n], -n, order) for n in range(quarter)]
    return [value[0] for value in out] + [-value[1] for value in out]


def real_inverse(found, size):
    if size == 2:
        return [found[0][0] + found[1][0], found[0][0] - found[1][0]]
    half = size // 2
    evens = real_inverse({k // 2: value for k, value in found.items() if k % 2 == 0}, half)
    odds = odd_inverse(found, size)
    return [evens[n] + odds[n] for n in range(half)] + [evens[n] - odds[n] for n in range(half)]


def padded_inverse(found):
    evens = real_inverse({k // 2: value for k, value in found.items() if k % 2 == 0}, HALF)
    odds = odd_inverse(found, RADIX)
    return [evens[n] + odds[n] for n in range(HALF)]


def tables():
    k = np.arange(LANES)
    angles = 2.0 * np.pi * (k[:, None] * k[None, :] % LANES) / LANES
    cos, sin = np.cos(angles), np.sin(angles)
    forward = np.block([[cos, -sin], [sin, cos]])
    inverse = forward.T

    def split(matrix):
        high = matrix.astype(np.float32).astype(jnp.bfloat16)
        low = (matrix - high.astype(np.float64)).astype(np.float32).astype(jnp.bfloat16)
        return high, low

    matrices = np.stack([*split(forward), *split(inverse)])
    length = RADIX * LANES
    first = np.arange(KEPT)
    angles = 2.0 * np.pi * (first[:, None] * k[None, :]) / length
    scale = np.where((first == 0) | (first == HALF), 1.0, 2.0)[:, None] / length
    twists = np.stack(
        [np.cos(angles), np.sin(angles), np.cos(angles) * scale, np.sin(angles) * scale]
    ).astype(np.float32)
    table = np.zeros((4, STRIDE, 2 * LANES), np.float32)
    table[:, :KEPT, :LANES] = twists
    return np.concatenate(
        [matrices.astype(np.float32).reshape(-1, 2 * LANES), table.reshape(-1, 2 * LANES)]
    )


CHUNKS = 4
PLANES = 2
GRANT = int(52.3 * 1024 * 1024)


def body(
    ctx,
    dp,
    q_hbm,
    k_hbm,
    v_hbm,
    g_hbm,
    f_hbm,
    c_hbm,
    out_ref,
    gq_ref,
    gk_ref,
    gv_ref,
    *rest,
):
    gf_refs = rest[:CHUNKS]
    (
        q_ref,
        k_ref,
        v_ref,
        g_ref,
        c_ref,
        w_ref,
        send_x,
        recv_x,
        send_y,
        recv_y,
        part_g,
        recv_g,
        sum_g,
        recv_s,
        own_s,
        spec_a,
        spec_b,
        plane_sem,
        go_sem,
        load_sem,
        own_sem,
        keep_sem,
        sx_send,
        sx_recv,
        sf_send,
        sf_recv,
        sy_send,
        sy_recv,
        sg_send,
        sg_recv,
        ss_send,
        ss_recv,
        sa_send,
        sa_recv,
    ) = rest[CHUNKS:]
    me_c = lax.axis_index("ctx")
    me_d = lax.axis_index("dp")
    ring = dp // PLANES
    channels, width = q_ref.shape
    share = channels // ctx
    rows = share // CHUNKS
    subs = rows // 8
    me_p, me_z = me_d // ring, lax.rem(me_d, ring)
    c_p, c_z = me_c // ring, lax.rem(me_c, ring)
    slot = lax.rem(me_z + ctx - me_c, ring)

    loads = [
        pltpu.make_async_copy(src, dst, load_sem.at[n])
        for n, (src, dst) in enumerate(
            [
                (k_hbm, k_ref),
                (v_hbm, v_ref),
                (q_hbm, q_ref),
                (g_hbm, g_ref),
                (c_hbm, c_ref),
            ]
        )
    ]
    for load in loads:
        load.start()

    far_first = sorted(range(1, ring), key=lambda i: -min(i, ring - i))

    def each(first, last, act):
        def step(i, carry):
            act(i)
            return carry

        lax.fori_loop(first, last, step, 0, unroll=True)

    def outward(act):
        for i in sorted(range(1, ctx), key=lambda i: -min(i, ctx - i)):
            act(i)

    def ctx_peer(i):
        return (me_d, lax.rem(me_c + i, ctx))

    def ring_peer(i):
        return (me_p * ring + lax.rem(me_z + i, ring), me_c)

    def swap_peer(plane, part):
        return (plane * ring + me_z, part * ring + slot)

    def is_self(plane, part):
        return (c_z == slot) & (plane == me_p) & (part == c_p)

    barrier = pltpu.get_barrier_semaphore()

    def signal(sem, peer):
        pl.semaphore_signal(sem, inc=1, device_id=peer, device_id_type=MESH)

    leads = me_c == 0

    def greet(i):
        peer = ctx_peer(i)
        pl.when(peer[1] != 0)(lambda: signal(barrier, peer))

    each(1, ctx, greet)
    swaps = [(plane, part) for plane in range(PLANES) for part in range(PLANES)]

    for load in loads[:4]:
        load.wait()

    def products(b, carry):
        at = pl.ds(b * share, share)
        mixed = k_ref[at, :].astype(jnp.float32) * v_ref[at, :].astype(jnp.float32)
        dconv = q_ref[at, :].astype(jnp.float32) * g_ref[at, :].astype(jnp.float32)
        for ck in range(CHUNKS):
            send_x[ck, 0, b] = mixed[ck * rows : (ck + 1) * rows]
            send_x[ck, 1, b] = dconv[ck * rows : (ck + 1) * rows]
        return carry

    lax.fori_loop(0, ctx, products, 0)

    @pl.when(jnp.logical_not(leads))
    def _():
        pl.semaphore_wait(barrier, ctx - 1)

    pl.when(me_c == 1)(lambda: signal(plane_sem, (me_d, 0)))

    @pl.when(leads)
    def _():
        pl.semaphore_wait(plane_sem, 1)
        each(1, ring, lambda i: signal(barrier, ring_peer(i)))
        for plane in range(PLANES):
            pl.when(plane != me_p)(lambda: signal(barrier, (plane * ring + me_z, me_c)))

    def remote(src, dst, send, recv, peer):
        return pltpu.make_async_remote_copy(
            src_ref=src,
            dst_ref=dst,
            send_sem=send,
            recv_sem=recv,
            device_id=peer,
            device_id_type=MESH,
        )

    def copy_x(ck, i):
        peer = ctx_peer(i)
        return remote(
            send_x.at[ck, :, peer[1]],
            recv_x.at[ck, pl.ds(0, 2), me_c],
            sx_send.at[ck],
            sx_recv.at[ck],
            peer,
        )

    def copy_f(ck, i):
        peer = ctx_peer(i)
        return remote(
            f_hbm.at[pl.ds(peer[1] * share + ck * rows, rows), :],
            recv_x.at[ck, 2, me_c],
            sf_send.at[ck],
            sf_recv.at[ck],
            peer,
        )

    def own_f(ck):
        return pltpu.make_async_copy(
            f_hbm.at[pl.ds(me_c * share + ck * rows, rows), :],
            recv_x.at[ck, 2, me_c],
            own_sem.at[ck],
        )

    def copy_y(ck, sig, i):
        peer = ctx_peer(i)
        return remote(
            send_y.at[ck, sig, peer[1]],
            recv_y.at[ck, sig, me_c],
            sy_send.at[ck],
            sy_recv.at[ck],
            peer,
        )

    def copy_g(ck, i):
        peer = ring_peer(i)
        return remote(
            part_g.at[ck, :, lax.rem(slot + i, ring)],
            recv_g.at[ck, i - 1],
            sg_send.at[ck],
            sg_recv.at[ck],
            peer,
        )

    def copy_s(ck, plane, part):
        return remote(
            sum_g.at[ck, part],
            recv_s.at[ck, c_p, me_p],
            ss_send.at[ck, plane, part],
            ss_recv.at[ck, c_p, me_p],
            swap_peer(plane, part),
        )

    def copy_a(ck, i):
        return remote(
            own_s.at[ck],
            gf_refs[ck].at[:, slot],
            sa_send.at[ck],
            sa_recv.at[ck],
            ring_peer(i),
        )

    def keep(ck):
        return pltpu.make_async_copy(own_s.at[ck], gf_refs[ck].at[:, slot], keep_sem.at[ck])

    def drain(ref, sem):
        pltpu.make_async_copy(ref, ref, sem).wait()

    def chunks(act):
        def step(ck, carry):
            act(ck)
            return carry

        lax.fori_loop(0, CHUNKS, step, 0)

    chunks(lambda ck: outward(lambda i: copy_x(ck, i).start()))

    @pl.when(leads)
    def _():
        pl.semaphore_wait(barrier, ring - 1 + PLANES - 1)
        each(1, ctx, lambda i: signal(go_sem, ctx_peer(i)))


    def first_f(ck):
        outward(lambda i: copy_f(ck, i).start())
        own_f(ck).start()

    def own_x(ck):
        recv_x[ck, 0, me_c] = send_x[ck, 0, me_c]
        recv_x[ck, 1, me_c] = send_x[ck, 1, me_c]

    chunks(own_x)
    for load in loads[4:]:
        load.wait()
    w_ref[...] = c_ref[pl.ds(0, w_ref.shape[0]), :].astype(jnp.bfloat16)

    def twist(which, k):
        return c_ref[pl.ds(w_ref.shape[0] + which * STRIDE + k, 1), pl.ds(0, LANES)]

    def weight(which):
        return w_ref[pl.ds(which * 2 * LANES, 2 * LANES), :]

    re, im = pl.ds(0, LANES), pl.ds(LANES, LANES)

    def forward(ck, sig, sub):
        at = pl.ds(sub * 8, 8)
        values = [
            recv_x[ck, sig, n // 2, at, pl.ds((n % 2) * LANES, LANES)] for n in range(HALF)
        ]
        found = padded_forward(values)
        for k in range(KEPT):
            cos, sin = twist(0, k), twist(1, k)
            real, imag = found[k]
            to = pl.ds(k * rows + sub * 8, 8)
            if k == 0:
                spec_a[sig, to, re] = real
                spec_a[sig, to, im] = jnp.zeros_like(real)
            elif imag is None:
                spec_a[sig, to, re] = real * cos
                spec_a[sig, to, im] = -(real * sin)
            else:
                spec_a[sig, to, re] = real * cos + imag * sin
                spec_a[sig, to, im] = imag * cos - real * sin

    def inverse(ck, sig, sub, store):
        found = {}
        for k in range(KEPT):
            cos, sin = twist(2, k), twist(3, k)
            at = pl.ds(k * rows + sub * 8, 8)
            real = spec_a[sig, at, re]
            imag = spec_a[sig, at, im]
            if k == 0 or k == HALF:
                found[k] = (real * cos - imag * sin, None)
            else:
                found[k] = (real * cos - imag * sin, imag * cos + real * sin)
        values = padded_inverse(found)
        for n in range(HALF):
            store(n // 2, pl.ds(sub * 8, 8), pl.ds((n % 2) * LANES, LANES), values[n])

    def matmul(src, dst, which):
        data = src[...].reshape(-1, 2 * LANES)
        height = data.shape[0]
        high = data.astype(jnp.bfloat16)
        low = (data - high.astype(jnp.float32)).astype(jnp.bfloat16)
        both = jnp.dot(
            jnp.concatenate([high, low], axis=0),
            weight(2 * which),
            preferred_element_type=jnp.float32,
        )
        rest = jnp.dot(high, weight(2 * which + 1), preferred_element_type=jnp.float32)
        dst[...] = (both[:height] + both[height:] + rest).reshape(dst.shape)

    def loop(count, act, unroll=1):
        def step(i, carry):
            act(i)
            return carry

        lax.fori_loop(0, count, step, 0, unroll=unroll)

    def filter_grad(ck):
        drain(recv_x.at[ck, pl.ds(0, 2), pl.ds(0, ctx - 1)], sx_recv.at[ck])
        loop(2 * subs, lambda n: forward(ck, n // subs, lax.rem(n, subs)))
        matmul(spec_a.at[pl.ds(0, 2)], spec_b.at[ck, pl.ds(0, 2)], 0)

        def pointwise(k):
            at = pl.ds(k * rows, rows)
            z_re, z_im = spec_b[ck, 0, at, re], spec_b[ck, 0, at, im]
            d_re, d_im = spec_b[ck, 1, at, re], spec_b[ck, 1, at, im]
            spec_a[0, at, re] = z_re * d_re + z_im * d_im
            spec_a[0, at, im] = z_re * d_im - z_im * d_re

        loop(KEPT, pointwise, 11)
        matmul(spec_a.at[0], spec_a.at[1], 1)

        def store(block, at, lanes, value):
            part_g[ck, block // ring, block % ring, at, lanes] = value

        loop(subs, lambda sub: inverse(ck, 1, sub, store))

        @pl.when((ck == 0) & jnp.logical_not(leads))
        def _():
            pl.semaphore_wait(go_sem, 1)

        for i in far_first:
            copy_g(ck, i).start()

    def convolutions(ck):
        drain(recv_x.at[ck, 2, pl.ds(0, ctx - 1)], sf_recv.at[ck])
        own_f(ck).wait()
        loop(subs, lambda sub: forward(ck, 2, sub))
        matmul(spec_a.at[2], spec_b.at[ck, 2], 0)

        def pointwise(k):
            at = pl.ds(k * rows, rows)
            z_re, z_im = spec_b[ck, 0, at, re], spec_b[ck, 0, at, im]
            d_re, d_im = spec_b[ck, 1, at, re], spec_b[ck, 1, at, im]
            f_re, f_im = spec_b[ck, 2, at, re], spec_b[ck, 2, at, im]
            spec_a[0, at, re] = z_re * f_re - z_im * f_im
            spec_a[0, at, im] = z_re * f_im + z_im * f_re
            spec_a[1, at, re] = f_re * d_re + f_im * d_im
            spec_a[1, at, im] = f_re * d_im - f_im * d_re

        loop(KEPT, pointwise, 11)
        matmul(spec_a.at[pl.ds(0, 2)], spec_a.at[pl.ds(0, 2)], 1)

        def back(n):
            sig, sub = n // subs, lax.rem(n, subs)

            def store(block, at, lanes, value):
                send_y[ck, sig, block, at, lanes] = value

            inverse(ck, sig, sub, store)

        for sig in range(2):
            loop(subs, lambda sub: back(sig * subs + sub))
            outward(lambda i: copy_y(ck, sig, i).start())
        recv_y[ck, 0, me_c] = send_y[ck, 0, me_c]
        recv_y[ck, 1, me_c] = send_y[ck, 1, me_c]

    def reduce(ck):
        drain(recv_g.at[ck], sg_recv.at[ck])
        for part in range(PLANES):
            total = part_g[ck, part, slot]
            for i in range(ring - 1):
                total = total + recv_g[ck, i, part]
            sum_g[ck, part] = total
        for step, part in swaps:
            plane = lax.rem(me_p + 1 + step, PLANES)
            mine = is_self(plane, part)

            @pl.when(jnp.logical_not(mine))
            def _():
                copy_s(ck, plane, part).start()

            @pl.when(mine)
            def _():
                recv_s[ck, part, plane] = sum_g[ck, part]

    scale = 1.0 / math.sqrt(dp * ctx * width)

    def gather(ck):
        for plane, part in swaps:

            @pl.when(jnp.logical_not(is_self(plane, part)))
            def _():
                drain(recv_s.at[ck, part, plane], ss_recv.at[ck, part, plane])

        for part in range(PLANES):
            total = recv_s[ck, part, 0]
            for plane in range(1, PLANES):
                total = total + recv_s[ck, part, plane]
            own_s[ck, part] = total * scale
        for chunk in range(CHUNKS):

            @pl.when(ck == chunk)
            def _():
                for i in far_first:
                    copy_a(chunk, i).start()
                keep(chunk).start()

    def stage(step):
        pl.when(step < CHUNKS)(lambda: first_f(step))
        pl.when(step < CHUNKS)(lambda: filter_grad(step))
        pl.when((step >= 2) & (step < CHUNKS + 2))(lambda: reduce(step - 2))

        @pl.when(step >= 3)
        def _():
            convolutions(step - 3)
            gather(step - 3)

    loop(CHUNKS + 3, stage)

    for ck in range(CHUNKS):
        drain(recv_y.at[ck, :, pl.ds(0, ctx - 1)], sy_recv.at[ck])

    def outputs(b):
        at = pl.ds(b * share, share)
        conv = jnp.concatenate([recv_y[ck, 0, b] for ck in range(CHUNKS)], axis=0)
        dmixed = jnp.concatenate([recv_y[ck, 1, b] for ck in range(CHUNKS)], axis=0)
        out_ref[at, :] = (q_ref[at, :].astype(jnp.float32) * conv).astype(jnp.bfloat16)
        gq_ref[at, :] = (g_ref[at, :].astype(jnp.float32) * conv).astype(jnp.bfloat16)
        gk_ref[at, :] = (v_ref[at, :].astype(jnp.float32) * dmixed).astype(jnp.bfloat16)
        gv_ref[at, :] = (k_ref[at, :].astype(jnp.float32) * dmixed).astype(jnp.bfloat16)

    loop(ctx, outputs)

    def finish(ck):
        drain(recv_x.at[ck, pl.ds(0, 2), pl.ds(0, ctx - 1)], sx_send.at[ck])
        drain(recv_x.at[ck, 2, pl.ds(0, ctx - 1)], sf_send.at[ck])
        drain(recv_y.at[ck, :, pl.ds(0, ctx - 1)], sy_send.at[ck])
        drain(recv_g.at[ck], sg_send.at[ck])
        for plane, part in swaps:

            @pl.when(jnp.logical_not(is_self(plane, part)))
            def _():
                drain(sum_g.at[ck, part], ss_send.at[ck, plane, part])


    chunks(finish)
    for ck in range(CHUNKS):
        keep(ck).wait()
        drain(gf_refs[ck].at[:, pl.ds(0, ring - 1)], sa_send.at[ck])
        drain(gf_refs[ck].at[:, pl.ds(0, ring - 1)], sa_recv.at[ck])


def write_out(count, *refs):
    sources, targets, sem = refs[: count + CHUNKS], refs[count + CHUNKS : -1], refs[-1]
    copies = [
        pltpu.make_async_copy(sources[n], targets[n], sem.at[n]) for n in range(count)
    ]
    for ck in range(CHUNKS):
        n = count + ck
        copies.append(
            pltpu.make_async_copy(sources[n], targets[count].at[:, :, ck], sem.at[n])
        )
    for copy in copies:
        copy.start()
    for copy in copies:
        copy.wait()


def shards(ctx, dp, query, key_act, value_act, filter_taps, grad_out):
    _, channels, width = query.shape
    share = channels // ctx
    rows = share // CHUNKS
    ring = dp // PLANES
    constants = tables()
    vmem = pl.BlockSpec(memory_space=pltpu.VMEM)
    hbm = pl.BlockSpec(memory_space=pltpu.HBM)
    half = jax.ShapeDtypeStruct((channels, width), jnp.bfloat16)
    whole = jax.ShapeDtypeStruct((PLANES, ring, CHUNKS, rows, width), jnp.float32)
    part = jax.ShapeDtypeStruct((PLANES, ring, rows, width), jnp.float32)
    dma = pltpu.SemaphoreType.DMA
    full = pltpu.VMEM((channels, width), jnp.bfloat16)
    outs = pl.pallas_call(
        functools.partial(body, ctx, dp),
        out_shape=[half] * 4 + [part] * CHUNKS,
        in_specs=[hbm] * 6,
        out_specs=[vmem] * (4 + CHUNKS),
        scratch_shapes=[
            full,
            full,
            full,
            full,
            pltpu.VMEM(constants.shape, jnp.float32),
            pltpu.VMEM((8 * LANES, 2 * LANES), jnp.bfloat16),
            pltpu.VMEM((CHUNKS, 2, ctx, rows, width), jnp.float32),
            pltpu.VMEM((CHUNKS, 3, ctx, rows, width), jnp.float32),
            pltpu.VMEM((CHUNKS, 2, ctx, rows, width), jnp.float32),
            pltpu.VMEM((CHUNKS, 2, ctx, rows, width), jnp.float32),
            pltpu.VMEM((CHUNKS, PLANES, ring, rows, width), jnp.float32),
            pltpu.VMEM((CHUNKS, ring - 1, PLANES, rows, width), jnp.float32),
            pltpu.VMEM((CHUNKS, PLANES, rows, width), jnp.float32),
            pltpu.VMEM((CHUNKS, PLANES, PLANES, rows, width), jnp.float32),
            pltpu.VMEM((CHUNKS, PLANES, rows, width), jnp.float32),
            pltpu.VMEM((3, KEPT * rows, 2 * LANES), jnp.float32),
            pltpu.VMEM((CHUNKS, 3, KEPT * rows, 2 * LANES), jnp.float32),
            pltpu.SemaphoreType.REGULAR,
            pltpu.SemaphoreType.REGULAR,
            dma((5,)),
            dma((CHUNKS,)),
            dma((CHUNKS,)),
            dma((CHUNKS,)),
            dma((CHUNKS,)),
            dma((CHUNKS,)),
            dma((CHUNKS,)),
            dma((CHUNKS,)),
            dma((CHUNKS,)),
            dma((CHUNKS,)),
            dma((CHUNKS,)),
            dma((CHUNKS, PLANES, PLANES)),
            dma((CHUNKS, PLANES, PLANES)),
            dma((CHUNKS,)),
            dma((CHUNKS,)),
        ],
        compiler_params=pltpu.CompilerParams(
            collective_id=0, has_side_effects=True, vmem_limit_bytes=GRANT
        ),
        cost_estimate=pl.CostEstimate(
            flops=3 * 2 * 6 * KEPT * share * 256 * 256, bytes_accessed=4 * 2**20, transcendentals=0
        ),
        name="hyena",
    )(
        query.reshape(channels, width),
        key_act.reshape(channels, width),
        value_act.reshape(channels, width),
        grad_out.reshape(channels, width),
        filter_taps,
        jnp.asarray(constants),
    )
    outs = pl.pallas_call(
        functools.partial(write_out, 4),
        out_shape=[half] * 4 + [whole],
        in_specs=[vmem] * (4 + CHUNKS),
        out_specs=[hbm] * 5,
        scratch_shapes=[dma((4 + CHUNKS,))],
        compiler_params=pltpu.CompilerParams(vmem_limit_bytes=4 * 1024 * 1024),
        name="write_out",
    )(*outs)
    shape = query.shape
    return (
        outs[0].reshape(shape),
        outs[1].reshape(shape),
        outs[2].reshape(shape),
        outs[3].reshape(shape),
        outs[4].reshape(channels, width),
    )


def solution(mesh):
    row = P("dp", None, "ctx")
    taps = P(None, "ctx")
    return jax.shard_map(
        functools.partial(shards, mesh.shape["ctx"], mesh.shape["dp"]),
        mesh=mesh,
        in_specs=(row, row, row, taps, row),
        out_specs=(row, row, row, row, taps),
        check_vma=False,
    )
```

```python
import functools
import math

import jax
import jax.numpy as jnp
import numpy as np
from jax import lax
from jax.experimental import pallas as pl
from jax.experimental.pallas import tpu as pltpu
from jax.sharding import PartitionSpec as P

MESH = pl.DeviceIdType.MESH
LANES = 128
RADIX = 64
HALF = RADIX // 2
KEPT = HALF + 1
STRIDE = 40


def turn(value, numerator, denominator):
    real, imag = value
    numerator %= denominator
    eighth = numerator * 8
    if eighth % denominator == 0:
        step = eighth // denominator
        if step == 0:
            return (real, imag)
        if step == 2:
            return (imag, -real)
        if step == 4:
            return (-real, -imag)
        if step == 6:
            return (-imag, real)
        root = math.sqrt(0.5)
        if step == 1:
            return ((real + imag) * root, (imag - real) * root)
        if step == 3:
            return ((imag - real) * root, (real + imag) * -root)
        if step == 5:
            return ((real + imag) * -root, (real - imag) * root)
        return ((real - imag) * root, (real + imag) * root)
    cos = math.cos(2.0 * math.pi * numerator / denominator)
    sin = math.sin(2.0 * math.pi * numerator / denominator)
    return (real * cos + imag * sin, imag * cos - real * sin)


def complex_fft(values, sign):
    size = len(values)
    if size == 1:
        return values
    even = complex_fft(values[0::2], sign)
    odd = complex_fft(values[1::2], sign)
    low, high = [], []
    for k in range(size // 2):
        real, imag = turn(odd[k], sign * k, size)
        low.append((even[k][0] + real, even[k][1] + imag))
        high.append((even[k][0] - real, even[k][1] - imag))
    return low + high


def odd_forward(values):
    quarter = len(values) // 2
    order = 4 * quarter
    packed = [turn((values[n], -values[n + quarter]), n, order) for n in range(quarter)]
    out = complex_fft(packed, 1)
    found = {}
    for j in range(quarter):
        k = 4 * j + 1
        if k < order // 2:
            found[k] = out[j]
        else:
            found[order - k] = (out[j][0], -out[j][1])
    return found


def real_forward(values):
    size = len(values)
    if size == 2:
        return {0: (values[0] + values[1], None), 1: (values[0] - values[1], None)}
    half = size // 2
    evens = real_forward([values[n] + values[n + half] for n in range(half)])
    found = {2 * k: value for k, value in evens.items()}
    found.update(odd_forward([values[n] - values[n + half] for n in range(half)]))
    return found


def padded_forward(values):
    found = {2 * k: value for k, value in real_forward(values).items()}
    found.update(odd_forward(values))
    return found


def odd_inverse(found, order):
    quarter = order // 4
    packed = []
    for j in range(quarter):
        k = 4 * j + 1
        if k < order // 2:
            packed.append(found[k])
        else:
            real, imag = found[order - k]
            packed.append((real, -imag))
    out = complex_fft(packed, -1)
    out = [turn(out[n], -n, order) for n in range(quarter)]
    return [value[0] for value in out] + [-value[1] for value in out]


def real_inverse(found, size):
    if size == 2:
        return [found[0][0] + found[1][0], found[0][0] - found[1][0]]
    half = size // 2
    evens = real_inverse({k // 2: value for k, value in found.items() if k % 2 == 0}, half)
    odds = odd_inverse(found, size)
    return [evens[n] + odds[n] for n in range(half)] + [evens[n] - odds[n] for n in range(half)]


def padded_inverse(found):
    evens = real_inverse({k // 2: value for k, value in found.items() if k % 2 == 0}, HALF)
    odds = odd_inverse(found, RADIX)
    return [evens[n] + odds[n] for n in range(HALF)]


def tables():
    k = np.arange(LANES)
    angles = 2.0 * np.pi * (k[:, None] * k[None, :] % LANES) / LANES
    cos, sin = np.cos(angles), np.sin(angles)
    forward = np.block([[cos, -sin], [sin, cos]])
    inverse = forward.T

    def split(matrix):
        high = matrix.astype(np.float32).astype(jnp.bfloat16)
        low = (matrix - high.astype(np.float64)).astype(np.float32).astype(jnp.bfloat16)
        return high, low

    matrices = np.stack([*split(forward), *split(inverse)])
    length = RADIX * LANES
    first = np.arange(KEPT)
    angles = 2.0 * np.pi * (first[:, None] * k[None, :]) / length
    scale = np.where((first == 0) | (first == HALF), 1.0, 2.0)[:, None] / length
    twists = np.stack(
        [np.cos(angles), np.sin(angles), np.cos(angles) * scale, np.sin(angles) * scale]
    ).astype(np.float32)
    table = np.zeros((4, STRIDE, 2 * LANES), np.float32)
    table[:, :KEPT, :LANES] = twists
    return np.concatenate(
        [matrices.astype(np.float32).reshape(-1, 2 * LANES), table.reshape(-1, 2 * LANES)]
    )


CHUNKS = 4
PLANES = 2
GRANT = int(52.3 * 1024 * 1024)


def body(
    ctx,
    dp,
    q_hbm,
    k_hbm,
    v_hbm,
    g_hbm,
    f_hbm,
    c_hbm,
    out_ref,
    gq_ref,
    gk_ref,
    gv_ref,
    *rest,
):
    gf_refs = rest[:CHUNKS]
    (
        q_ref,
        k_ref,
        v_ref,
        g_ref,
        c_ref,
        w_ref,
        send_x,
        recv_x,
        send_y,
        recv_y,
        part_g,
        recv_g,
        sum_g,
        recv_s,
        own_s,
        spec_a,
        spec_b,
        plane_sem,
        go_sem,
        load_sem,
        own_sem,
        keep_sem,
        sx_send,
        sx_recv,
        sf_send,
        sf_recv,
        sy_send,
        sy_recv,
        sg_send,
        sg_recv,
        ss_send,
        ss_recv,
        sa_send,
        sa_recv,
    ) = rest[CHUNKS:]
    me_c = lax.axis_index("ctx")
    me_d = lax.axis_index("dp")
    ring = dp // PLANES
    channels, width = q_ref.shape
    share = channels // ctx
    rows = share // CHUNKS
    subs = rows // 8
    me_p, me_z = me_d // ring, lax.rem(me_d, ring)
    c_p, c_z = me_c // ring, lax.rem(me_c, ring)
    slot = lax.rem(me_z + ctx - me_c, ring)

    loads = [
        pltpu.make_async_copy(src, dst, load_sem.at[n])
        for n, (src, dst) in enumerate(
            [
                (k_hbm, k_ref),
                (v_hbm, v_ref),
                (q_hbm, q_ref),
                (g_hbm, g_ref),
                (c_hbm, c_ref),
            ]
        )
    ]
    for load in loads:
        load.start()

    far_first = sorted(range(1, ring), key=lambda i: -min(i, ring - i))

    def each(first, last, act):
        def step(i, carry):
            act(i)
            return carry

        lax.fori_loop(first, last, step, 0, unroll=True)

    def outward(act):
        for i in sorted(range(1, ctx), key=lambda i: -min(i, ctx - i)):
            act(i)

    def ctx_peer(i):
        return (me_d, lax.rem(me_c + i, ctx))

    def ring_peer(i):
        return (me_p * ring + lax.rem(me_z + i, ring), me_c)

    def swap_peer(plane, part):
        return (plane * ring + me_z, part * ring + slot)

    def is_self(plane, part):
        return (c_z == slot) & (plane == me_p) & (part == c_p)

    barrier = pltpu.get_barrier_semaphore()

    def signal(sem, peer):
        pl.semaphore_signal(sem, inc=1, device_id=peer, device_id_type=MESH)

    leads = me_c == 0

    def greet(i):
        peer = ctx_peer(i)
        pl.when(peer[1] != 0)(lambda: signal(barrier, peer))

    each(1, ctx, greet)
    swaps = [(plane, part) for plane in range(PLANES) for part in range(PLANES)]

    for load in loads[:4]:
        load.wait()

    def products(b, carry):
        at = pl.ds(b * share, share)
        mixed = k_ref[at, :].astype(jnp.float32) * v_ref[at, :].astype(jnp.float32)
        dconv = q_ref[at, :].astype(jnp.float32) * g_ref[at, :].astype(jnp.float32)
        for ck in range(CHUNKS):
            send_x[ck, 0, b] = mixed[ck * rows : (ck + 1) * rows]
            send_x[ck, 1, b] = dconv[ck * rows : (ck + 1) * rows]
        return carry

    lax.fori_loop(0, ctx, products, 0)

    @pl.when(jnp.logical_not(leads))
    def _():
        pl.semaphore_wait(barrier, ctx - 1)

    pl.when(me_c == 1)(lambda: signal(plane_sem, (me_d, 0)))

    @pl.when(leads)
    def _():
        pl.semaphore_wait(plane_sem, 1)
        each(1, ring, lambda i: signal(barrier, ring_peer(i)))
        for plane in range(PLANES):
            pl.when(plane != me_p)(lambda: signal(barrier, (plane * ring + me_z, me_c)))

    def remote(src, dst, send, recv, peer):
        return pltpu.make_async_remote_copy(
            src_ref=src,
            dst_ref=dst,
            send_sem=send,
            recv_sem=recv,
            device_id=peer,
            device_id_type=MESH,
        )

    def copy_x(ck, i):
        peer = ctx_peer(i)
        return remote(
            send_x.at[ck, :, peer[1]],
            recv_x.at[ck, pl.ds(0, 2), me_c],
            sx_send.at[ck],
            sx_recv.at[ck],
            peer,
        )

    def copy_f(ck, i):
        peer = ctx_peer(i)
        return remote(
            f_hbm.at[pl.ds(peer[1] * share + ck * rows, rows), :],
            recv_x.at[ck, 2, me_c],
            sf_send.at[ck],
            sf_recv.at[ck],
            peer,
        )

    def own_f(ck):
        return pltpu.make_async_copy(
            f_hbm.at[pl.ds(me_c * share + ck * rows, rows), :],
            recv_x.at[ck, 2, me_c],
            own_sem.at[ck],
        )

    def copy_y(ck, sig, i):
        peer = ctx_peer(i)
        return remote(
            send_y.at[ck, sig, peer[1]],
            recv_y.at[ck, sig, me_c],
            sy_send.at[ck],
            sy_recv.at[ck, sig],
            peer,
        )

    def copy_g(ck, i):
        peer = ring_peer(i)
        return remote(
            part_g.at[ck, :, lax.rem(slot + i, ring)],
            recv_g.at[ck, i - 1],
            sg_send.at[ck],
            sg_recv.at[ck],
            peer,
        )

    def copy_s(ck, plane, part):
        return remote(
            sum_g.at[ck, part],
            recv_s.at[ck, c_p, me_p],
            ss_send.at[ck, plane, part],
            ss_recv.at[ck, c_p, me_p],
            swap_peer(plane, part),
        )

    def copy_a(ck, i):
        return remote(
            own_s.at[ck],
            gf_refs[ck].at[:, slot],
            sa_send.at[ck],
            sa_recv.at[ck],
            ring_peer(i),
        )

    def keep(ck):
        return pltpu.make_async_copy(own_s.at[ck], gf_refs[ck].at[:, slot], keep_sem.at[ck])

    def drain(ref, sem):
        pltpu.make_async_copy(ref, ref, sem).wait()

    def chunks(act):
        def step(ck, carry):
            act(ck)
            return carry

        lax.fori_loop(0, CHUNKS, step, 0)

    chunks(lambda ck: outward(lambda i: copy_x(ck, i).start()))

    @pl.when(leads)
    def _():
        pl.semaphore_wait(barrier, ring - 1 + PLANES - 1)
        each(1, ctx, lambda i: signal(go_sem, ctx_peer(i)))


    def first_f(ck):
        outward(lambda i: copy_f(ck, i).start())
        own_f(ck).start()

    def own_x(ck):
        recv_x[ck, 0, me_c] = send_x[ck, 0, me_c]
        recv_x[ck, 1, me_c] = send_x[ck, 1, me_c]

    chunks(own_x)
    for load in loads[4:]:
        load.wait()
    w_ref[...] = c_ref[pl.ds(0, w_ref.shape[0]), :].astype(jnp.bfloat16)

    def twist(which, k):
        return c_ref[pl.ds(w_ref.shape[0] + which * STRIDE + k, 1), pl.ds(0, LANES)]

    def weight(which):
        return w_ref[pl.ds(which * 2 * LANES, 2 * LANES), :]

    re, im = pl.ds(0, LANES), pl.ds(LANES, LANES)

    def forward(ck, sig, sub):
        at = pl.ds(sub * 8, 8)
        values = [
            recv_x[ck, sig, n // 2, at, pl.ds((n % 2) * LANES, LANES)] for n in range(HALF)
        ]
        found = padded_forward(values)
        for k in range(KEPT):
            cos, sin = twist(0, k), twist(1, k)
            real, imag = found[k]
            to = pl.ds(k * rows + sub * 8, 8)
            if k == 0:
                spec_a[sig, to, re] = real
                spec_a[sig, to, im] = jnp.zeros_like(real)
            elif imag is None:
                spec_a[sig, to, re] = real * cos
                spec_a[sig, to, im] = -(real * sin)
            else:
                spec_a[sig, to, re] = real * cos + imag * sin
                spec_a[sig, to, im] = imag * cos - real * sin

    def inverse(ck, sig, sub, store):
        found = {}
        for k in range(KEPT):
            cos, sin = twist(2, k), twist(3, k)
            at = pl.ds(k * rows + sub * 8, 8)
            real = spec_a[sig, at, re]
            imag = spec_a[sig, at, im]
            if k == 0 or k == HALF:
                found[k] = (real * cos - imag * sin, None)
            else:
                found[k] = (real * cos - imag * sin, imag * cos + real * sin)
        values = padded_inverse(found)
        for n in range(HALF):
            store(n // 2, pl.ds(sub * 8, 8), pl.ds((n % 2) * LANES, LANES), values[n])

    def matmul(src, dst, which):
        data = src[...].reshape(-1, 2 * LANES)
        height = data.shape[0]
        high = data.astype(jnp.bfloat16)
        low = (data - high.astype(jnp.float32)).astype(jnp.bfloat16)
        both = jnp.dot(
            jnp.concatenate([high, low], axis=0),
            weight(2 * which),
            preferred_element_type=jnp.float32,
        )
        rest = jnp.dot(high, weight(2 * which + 1), preferred_element_type=jnp.float32)
        dst[...] = (both[:height] + both[height:] + rest).reshape(dst.shape)

    def loop(count, act, unroll=1):
        def step(i, carry):
            act(i)
            return carry

        lax.fori_loop(0, count, step, 0, unroll=unroll)

    def filter_grad(ck):
        drain(recv_x.at[ck, pl.ds(0, 2), pl.ds(0, ctx - 1)], sx_recv.at[ck])
        loop(2 * subs, lambda n: forward(ck, n // subs, lax.rem(n, subs)))
        matmul(spec_a.at[pl.ds(0, 2)], spec_b.at[ck, pl.ds(0, 2)], 0)

        def pointwise(k):
            at = pl.ds(k * rows, rows)
            z_re, z_im = spec_b[ck, 0, at, re], spec_b[ck, 0, at, im]
            d_re, d_im = spec_b[ck, 1, at, re], spec_b[ck, 1, at, im]
            spec_a[0, at, re] = z_re * d_re + z_im * d_im
            spec_a[0, at, im] = z_re * d_im - z_im * d_re

        loop(KEPT, pointwise, 11)
        matmul(spec_a.at[0], spec_a.at[1], 1)

        def store(block, at, lanes, value):
            part_g[ck, block // ring, block % ring, at, lanes] = value

        loop(subs, lambda sub: inverse(ck, 1, sub, store))

        @pl.when((ck == 0) & jnp.logical_not(leads))
        def _():
            pl.semaphore_wait(go_sem, 1)

        for i in far_first:
            copy_g(ck, i).start()

    def convolutions(ck):
        drain(recv_x.at[ck, 2, pl.ds(0, ctx - 1)], sf_recv.at[ck])
        own_f(ck).wait()
        loop(subs, lambda sub: forward(ck, 2, sub))
        matmul(spec_a.at[2], spec_b.at[ck, 2], 0)

        def pointwise(k):
            at = pl.ds(k * rows, rows)
            z_re, z_im = spec_b[ck, 0, at, re], spec_b[ck, 0, at, im]
            d_re, d_im = spec_b[ck, 1, at, re], spec_b[ck, 1, at, im]
            f_re, f_im = spec_b[ck, 2, at, re], spec_b[ck, 2, at, im]
            spec_a[0, at, re] = z_re * f_re - z_im * f_im
            spec_a[0, at, im] = z_re * f_im + z_im * f_re
            spec_a[1, at, re] = f_re * d_re + f_im * d_im
            spec_a[1, at, im] = f_re * d_im - f_im * d_re

        loop(KEPT, pointwise, 11)
        matmul(spec_a.at[pl.ds(0, 2)], spec_a.at[pl.ds(0, 2)], 1)

        def back(n):
            sig, sub = n // subs, lax.rem(n, subs)

            def store(block, at, lanes, value):
                send_y[ck, sig, block, at, lanes] = value

            inverse(ck, sig, sub, store)

        for sig in range(2):
            loop(subs, lambda sub: back(sig * subs + sub))
            outward(lambda i: copy_y(ck, sig, i).start())
        recv_y[ck, 0, me_c] = send_y[ck, 0, me_c]
        recv_y[ck, 1, me_c] = send_y[ck, 1, me_c]

    def reduce(ck):
        drain(recv_g.at[ck], sg_recv.at[ck])
        for part in range(PLANES):
            total = part_g[ck, part, slot]
            for i in range(ring - 1):
                total = total + recv_g[ck, i, part]
            sum_g[ck, part] = total
        for step, part in swaps:
            plane = lax.rem(me_p + 1 + step, PLANES)
            mine = is_self(plane, part)

            @pl.when(jnp.logical_not(mine))
            def _():
                copy_s(ck, plane, part).start()

            @pl.when(mine)
            def _():
                recv_s[ck, part, plane] = sum_g[ck, part]

    scale = 1.0 / math.sqrt(dp * ctx * width)

    def gather(ck):
        for plane, part in swaps:

            @pl.when(jnp.logical_not(is_self(plane, part)))
            def _():
                drain(recv_s.at[ck, part, plane], ss_recv.at[ck, part, plane])

        for part in range(PLANES):
            total = recv_s[ck, part, 0]
            for plane in range(1, PLANES):
                total = total + recv_s[ck, part, plane]
            own_s[ck, part] = total * scale
        for chunk in range(CHUNKS):

            @pl.when(ck == chunk)
            def _():
                for i in far_first:
                    copy_a(chunk, i).start()
                keep(chunk).start()

    def stage(step):
        pl.when(step < CHUNKS)(lambda: first_f(step))
        pl.when(step < CHUNKS)(lambda: filter_grad(step))
        pl.when((step >= 2) & (step < CHUNKS + 2))(lambda: reduce(step - 2))

        @pl.when(step >= 3)
        def _():
            convolutions(step - 3)
            gather(step - 3)

    loop(CHUNKS + 3, stage)

    def outputs(pair, sig):
        for ck in (pair, pair + 1):
            drain(recv_y.at[ck, sig, pl.ds(0, ctx - 1)], sy_recv.at[ck, sig])
        gates = [(q_ref, out_ref), (g_ref, gq_ref)] if sig == 0 else [(v_ref, gk_ref), (k_ref, gv_ref)]

        def block(b):
            at = pl.ds(b * share + pair * rows, 2 * rows)
            value = jnp.concatenate([recv_y[pair, sig, b], recv_y[pair + 1, sig, b]], axis=0)
            for gate, to in gates:
                to[at, :] = (gate[at, :].astype(jnp.float32) * value).astype(jnp.bfloat16)

        loop(ctx, block, 4)

    for pair in range(0, CHUNKS, 2):
        for sig in range(2):
            outputs(pair, sig)

    def finish(ck):
        drain(recv_x.at[ck, pl.ds(0, 2), pl.ds(0, ctx - 1)], sx_send.at[ck])
        drain(recv_x.at[ck, 2, pl.ds(0, ctx - 1)], sf_send.at[ck])
        drain(recv_y.at[ck, :, pl.ds(0, ctx - 1)], sy_send.at[ck])
        drain(recv_g.at[ck], sg_send.at[ck])
        for plane, part in swaps:

            @pl.when(jnp.logical_not(is_self(plane, part)))
            def _():
                drain(sum_g.at[ck, part], ss_send.at[ck, plane, part])


    chunks(finish)
    for ck in range(CHUNKS):
        keep(ck).wait()
        drain(gf_refs[ck].at[:, pl.ds(0, ring - 1)], sa_send.at[ck])
        drain(gf_refs[ck].at[:, pl.ds(0, ring - 1)], sa_recv.at[ck])


def write_out(count, *refs):
    sources, targets, sem = refs[: count + CHUNKS], refs[count + CHUNKS : -1], refs[-1]
    copies = [
        pltpu.make_async_copy(sources[n], targets[n], sem.at[n]) for n in range(count)
    ]
    for ck in range(CHUNKS):
        n = count + ck
        copies.append(
            pltpu.make_async_copy(sources[n], targets[count].at[:, :, ck], sem.at[n])
        )
    for copy in copies:
        copy.start()
    for copy in copies:
        copy.wait()


def shards(ctx, dp, query, key_act, value_act, filter_taps, grad_out):
    _, channels, width = query.shape
    share = channels // ctx
    rows = share // CHUNKS
    ring = dp // PLANES
    constants = tables()
    vmem = pl.BlockSpec(memory_space=pltpu.VMEM)
    hbm = pl.BlockSpec(memory_space=pltpu.HBM)
    half = jax.ShapeDtypeStruct((channels, width), jnp.bfloat16)
    whole = jax.ShapeDtypeStruct((PLANES, ring, CHUNKS, rows, width), jnp.float32)
    part = jax.ShapeDtypeStruct((PLANES, ring, rows, width), jnp.float32)
    dma = pltpu.SemaphoreType.DMA
    full = pltpu.VMEM((channels, width), jnp.bfloat16)
    outs = pl.pallas_call(
        functools.partial(body, ctx, dp),
        out_shape=[half] * 4 + [part] * CHUNKS,
        in_specs=[hbm] * 6,
        out_specs=[vmem] * (4 + CHUNKS),
        scratch_shapes=[
            full,
            full,
            full,
            full,
            pltpu.VMEM(constants.shape, jnp.float32),
            pltpu.VMEM((8 * LANES, 2 * LANES), jnp.bfloat16),
            pltpu.VMEM((CHUNKS, 2, ctx, rows, width), jnp.float32),
            pltpu.VMEM((CHUNKS, 3, ctx, rows, width), jnp.float32),
            pltpu.VMEM((CHUNKS, 2, ctx, rows, width), jnp.float32),
            pltpu.VMEM((CHUNKS, 2, ctx, rows, width), jnp.float32),
            pltpu.VMEM((CHUNKS, PLANES, ring, rows, width), jnp.float32),
            pltpu.VMEM((CHUNKS, ring - 1, PLANES, rows, width), jnp.float32),
            pltpu.VMEM((CHUNKS, PLANES, rows, width), jnp.float32),
            pltpu.VMEM((CHUNKS, PLANES, PLANES, rows, width), jnp.float32),
            pltpu.VMEM((CHUNKS, PLANES, rows, width), jnp.float32),
            pltpu.VMEM((3, KEPT * rows, 2 * LANES), jnp.float32),
            pltpu.VMEM((CHUNKS, 3, KEPT * rows, 2 * LANES), jnp.float32),
            pltpu.SemaphoreType.REGULAR,
            pltpu.SemaphoreType.REGULAR,
            dma((5,)),
            dma((CHUNKS,)),
            dma((CHUNKS,)),
            dma((CHUNKS,)),
            dma((CHUNKS,)),
            dma((CHUNKS,)),
            dma((CHUNKS,)),
            dma((CHUNKS,)),
            dma((CHUNKS, 2)),
            dma((CHUNKS,)),
            dma((CHUNKS,)),
            dma((CHUNKS, PLANES, PLANES)),
            dma((CHUNKS, PLANES, PLANES)),
            dma((CHUNKS,)),
            dma((CHUNKS,)),
        ],
        compiler_params=pltpu.CompilerParams(
            collective_id=0, has_side_effects=True, vmem_limit_bytes=GRANT
        ),
        cost_estimate=pl.CostEstimate(
            flops=3 * 2 * 6 * KEPT * share * 256 * 256, bytes_accessed=4 * 2**20, transcendentals=0
        ),
        name="hyena",
    )(
        query.reshape(channels, width),
        key_act.reshape(channels, width),
        value_act.reshape(channels, width),
        grad_out.reshape(channels, width),
        filter_taps,
        jnp.asarray(constants),
    )
    outs = pl.pallas_call(
        functools.partial(write_out, 4),
        out_shape=[half] * 4 + [whole],
        in_specs=[vmem] * (4 + CHUNKS),
        out_specs=[hbm] * 5,
        scratch_shapes=[dma((4 + CHUNKS,))],
        compiler_params=pltpu.CompilerParams(vmem_limit_bytes=4 * 1024 * 1024),
        name="write_out",
    )(*outs)
    shape = query.shape
    return (
        outs[0].reshape(shape),
        outs[1].reshape(shape),
        outs[2].reshape(shape),
        outs[3].reshape(shape),
        outs[4].reshape(channels, width),
    )


def solution(mesh):
    row = P("dp", None, "ctx")
    taps = P(None, "ctx")
    return jax.shard_map(
        functools.partial(shards, mesh.shape["ctx"], mesh.shape["dp"]),
        mesh=mesh,
        in_specs=(row, row, row, taps, row),
        out_specs=(row, row, row, row, taps),
        check_vma=False,
    )
```

```python
import functools
import math

import jax
import jax.numpy as jnp
import numpy as np
from jax import lax
from jax.experimental import pallas as pl
from jax.experimental.pallas import tpu as pltpu
from jax.sharding import PartitionSpec as P

MESH = pl.DeviceIdType.MESH
LANES = 128
RADIX = 64
HALF = RADIX // 2
KEPT = HALF + 1
STRIDE = 40


def turn(value, numerator, denominator):
    real, imag = value
    numerator %= denominator
    eighth = numerator * 8
    if eighth % denominator == 0:
        step = eighth // denominator
        if step == 0:
            return (real, imag)
        if step == 2:
            return (imag, -real)
        if step == 4:
            return (-real, -imag)
        if step == 6:
            return (-imag, real)
        root = math.sqrt(0.5)
        if step == 1:
            return ((real + imag) * root, (imag - real) * root)
        if step == 3:
            return ((imag - real) * root, (real + imag) * -root)
        if step == 5:
            return ((real + imag) * -root, (real - imag) * root)
        return ((real - imag) * root, (real + imag) * root)
    cos = math.cos(2.0 * math.pi * numerator / denominator)
    sin = math.sin(2.0 * math.pi * numerator / denominator)
    return (real * cos + imag * sin, imag * cos - real * sin)


def complex_fft(values, sign):
    size = len(values)
    if size == 1:
        return values
    even = complex_fft(values[0::2], sign)
    odd = complex_fft(values[1::2], sign)
    low, high = [], []
    for k in range(size // 2):
        real, imag = turn(odd[k], sign * k, size)
        low.append((even[k][0] + real, even[k][1] + imag))
        high.append((even[k][0] - real, even[k][1] - imag))
    return low + high


def odd_forward(values):
    quarter = len(values) // 2
    order = 4 * quarter
    packed = [turn((values[n], -values[n + quarter]), n, order) for n in range(quarter)]
    out = complex_fft(packed, 1)
    found = {}
    for j in range(quarter):
        k = 4 * j + 1
        if k < order // 2:
            found[k] = out[j]
        else:
            found[order - k] = (out[j][0], -out[j][1])
    return found


def real_forward(values):
    size = len(values)
    if size == 2:
        return {0: (values[0] + values[1], None), 1: (values[0] - values[1], None)}
    half = size // 2
    evens = real_forward([values[n] + values[n + half] for n in range(half)])
    found = {2 * k: value for k, value in evens.items()}
    found.update(odd_forward([values[n] - values[n + half] for n in range(half)]))
    return found


def padded_forward(values):
    found = {2 * k: value for k, value in real_forward(values).items()}
    found.update(odd_forward(values))
    return found


def odd_inverse(found, order):
    quarter = order // 4
    packed = []
    for j in range(quarter):
        k = 4 * j + 1
        if k < order // 2:
            packed.append(found[k])
        else:
            real, imag = found[order - k]
            packed.append((real, -imag))
    out = complex_fft(packed, -1)
    out = [turn(out[n], -n, order) for n in range(quarter)]
    return [value[0] for value in out] + [-value[1] for value in out]


def real_inverse(found, size):
    if size == 2:
        return [found[0][0] + found[1][0], found[0][0] - found[1][0]]
    half = size // 2
    evens = real_inverse({k // 2: value for k, value in found.items() if k % 2 == 0}, half)
    odds = odd_inverse(found, size)
    return [evens[n] + odds[n] for n in range(half)] + [evens[n] - odds[n] for n in range(half)]


def padded_inverse(found):
    evens = real_inverse({k // 2: value for k, value in found.items() if k % 2 == 0}, HALF)
    odds = odd_inverse(found, RADIX)
    return [evens[n] + odds[n] for n in range(HALF)]


def tables():
    k = np.arange(LANES)
    angles = 2.0 * np.pi * (k[:, None] * k[None, :] % LANES) / LANES
    cos, sin = np.cos(angles), np.sin(angles)
    forward = np.block([[cos, -sin], [sin, cos]])
    inverse = forward.T

    def split(matrix):
        high = matrix.astype(np.float32).astype(jnp.bfloat16)
        low = (matrix - high.astype(np.float64)).astype(np.float32).astype(jnp.bfloat16)
        return high, low

    matrices = np.stack([*split(forward), *split(inverse)])
    length = RADIX * LANES
    first = np.arange(KEPT)
    angles = 2.0 * np.pi * (first[:, None] * k[None, :]) / length
    scale = np.where((first == 0) | (first == HALF), 1.0, 2.0)[:, None] / length
    twists = np.stack(
        [np.cos(angles), np.sin(angles), np.cos(angles) * scale, np.sin(angles) * scale]
    ).astype(np.float32)
    table = np.zeros((4, STRIDE, 2 * LANES), np.float32)
    table[:, :KEPT, :LANES] = twists
    return np.concatenate(
        [matrices.astype(np.float32).reshape(-1, 2 * LANES), table.reshape(-1, 2 * LANES)]
    )


CHUNKS = 4
PLANES = 2
GRANT = int(52.3 * 1024 * 1024)


def body(
    ctx,
    dp,
    q_hbm,
    k_hbm,
    v_hbm,
    g_hbm,
    f_hbm,
    c_hbm,
    out_ref,
    gq_ref,
    gk_ref,
    gv_ref,
    *rest,
):
    gf_refs = rest[:CHUNKS]
    (
        q_ref,
        k_ref,
        v_ref,
        g_ref,
        c_ref,
        w_ref,
        send_x,
        recv_x,
        send_y,
        recv_y,
        part_g,
        recv_g,
        sum_g,
        recv_s,
        own_s,
        spec_a,
        spec_b,
        plane_sem,
        go_sem,
        load_sem,
        own_sem,
        keep_sem,
        sx_send,
        sx_recv,
        sf_send,
        sf_recv,
        sy_send,
        sy_recv,
        sg_send,
        sg_recv,
        ss_send,
        ss_recv,
        sa_send,
        sa_recv,
    ) = rest[CHUNKS:]
    me_c = lax.axis_index("ctx")
    me_d = lax.axis_index("dp")
    ring = dp // PLANES
    channels, width = q_ref.shape
    share = channels // ctx
    rows = share // CHUNKS
    subs = rows // 8
    me_p, me_z = me_d // ring, lax.rem(me_d, ring)
    c_p, c_z = me_c // ring, lax.rem(me_c, ring)
    slot = lax.rem(me_z + ctx - me_c, ring)

    loads = [
        pltpu.make_async_copy(src, dst, load_sem.at[n])
        for n, (src, dst) in enumerate(
            [
                (k_hbm, k_ref),
                (v_hbm, v_ref),
                (q_hbm, q_ref),
                (g_hbm, g_ref),
                (c_hbm, c_ref),
            ]
        )
    ]
    for load in loads:
        load.start()

    far_first = sorted(range(1, ring), key=lambda i: -min(i, ring - i))

    def each(first, last, act):
        def step(i, carry):
            act(i)
            return carry

        lax.fori_loop(first, last, step, 0, unroll=True)

    def outward(act):
        for i in sorted(range(1, ctx), key=lambda i: -min(i, ctx - i)):
            act(i)

    def ctx_peer(i):
        return (me_d, lax.rem(me_c + i, ctx))

    def ring_peer(i):
        return (me_p * ring + lax.rem(me_z + i, ring), me_c)

    def swap_peer(plane, part):
        return (plane * ring + me_z, part * ring + slot)

    def is_self(plane, part):
        return (c_z == slot) & (plane == me_p) & (part == c_p)

    barrier = pltpu.get_barrier_semaphore()

    def signal(sem, peer):
        pl.semaphore_signal(sem, inc=1, device_id=peer, device_id_type=MESH)

    leads = me_c == 0

    def greet(i):
        peer = ctx_peer(i)
        pl.when(peer[1] != 0)(lambda: signal(barrier, peer))

    each(1, ctx, greet)
    swaps = [(plane, part) for plane in range(PLANES) for part in range(PLANES)]

    for load in loads[:4]:
        load.wait()

    def products(b, carry):
        at = pl.ds(b * share, share)
        mixed = k_ref[at, :].astype(jnp.float32) * v_ref[at, :].astype(jnp.float32)
        dconv = q_ref[at, :].astype(jnp.float32) * g_ref[at, :].astype(jnp.float32)
        for ck in range(CHUNKS):
            send_x[ck, 0, b] = mixed[ck * rows : (ck + 1) * rows]
            send_x[ck, 1, b] = dconv[ck * rows : (ck + 1) * rows]
        return carry

    lax.fori_loop(0, ctx, products, 0)

    @pl.when(jnp.logical_not(leads))
    def _():
        pl.semaphore_wait(barrier, ctx - 1)

    pl.when(me_c == 1)(lambda: signal(plane_sem, (me_d, 0)))

    @pl.when(leads)
    def _():
        pl.semaphore_wait(plane_sem, 1)
        each(1, ring, lambda i: signal(barrier, ring_peer(i)))
        for plane in range(PLANES):
            pl.when(plane != me_p)(lambda: signal(barrier, (plane * ring + me_z, me_c)))

    def remote(src, dst, send, recv, peer):
        return pltpu.make_async_remote_copy(
            src_ref=src,
            dst_ref=dst,
            send_sem=send,
            recv_sem=recv,
            device_id=peer,
            device_id_type=MESH,
        )

    def copy_x(ck, i):
        peer = ctx_peer(i)
        return remote(
            send_x.at[ck, :, peer[1]],
            recv_x.at[ck, pl.ds(0, 2), me_c],
            sx_send.at[ck],
            sx_recv.at[ck],
            peer,
        )

    def copy_f(ck, i):
        peer = ctx_peer(i)
        return remote(
            f_hbm.at[pl.ds(peer[1] * share + ck * rows, rows), :],
            recv_x.at[ck, 2, me_c],
            sf_send.at[ck],
            sf_recv.at[ck],
            peer,
        )

    def own_f(ck):
        return pltpu.make_async_copy(
            f_hbm.at[pl.ds(me_c * share + ck * rows, rows), :],
            recv_x.at[ck, 2, me_c],
            own_sem.at[ck],
        )

    def copy_y(ck, sig, i):
        peer = ctx_peer(i)
        return remote(
            send_y.at[ck, sig, peer[1]],
            recv_y.at[ck, sig, me_c],
            sy_send.at[ck],
            sy_recv.at[ck, sig],
            peer,
        )

    def copy_g(ck, i):
        peer = ring_peer(i)
        return remote(
            part_g.at[ck, :, lax.rem(slot + i, ring)],
            recv_g.at[ck, i - 1],
            sg_send.at[ck],
            sg_recv.at[ck],
            peer,
        )

    def copy_s(ck, plane, part):
        return remote(
            sum_g.at[ck, part],
            recv_s.at[ck, c_p, me_p],
            ss_send.at[ck, plane, part],
            ss_recv.at[ck, c_p, me_p],
            swap_peer(plane, part),
        )

    def copy_a(ck, i):
        return remote(
            own_s.at[ck],
            gf_refs[ck].at[:, slot],
            sa_send.at[ck],
            sa_recv.at[ck],
            ring_peer(i),
        )

    def keep(ck):
        return pltpu.make_async_copy(own_s.at[ck], gf_refs[ck].at[:, slot], keep_sem.at[ck])

    def drain(ref, sem):
        pltpu.make_async_copy(ref, ref, sem).wait()

    def chunks(act):
        def step(ck, carry):
            act(ck)
            return carry

        lax.fori_loop(0, CHUNKS, step, 0)

    chunks(lambda ck: outward(lambda i: copy_x(ck, i).start()))

    @pl.when(leads)
    def _():
        pl.semaphore_wait(barrier, ring - 1 + PLANES - 1)
        each(1, ctx, lambda i: signal(go_sem, ctx_peer(i)))


    def first_f(ck):
        outward(lambda i: copy_f(ck, i).start())
        own_f(ck).start()

    def own_x(ck):
        recv_x[ck, 0, me_c] = send_x[ck, 0, me_c]
        recv_x[ck, 1, me_c] = send_x[ck, 1, me_c]

    chunks(own_x)
    for load in loads[4:]:
        load.wait()
    w_ref[...] = c_ref[pl.ds(0, w_ref.shape[0]), :].astype(jnp.bfloat16)

    def twist(which, k):
        return c_ref[pl.ds(w_ref.shape[0] + which * STRIDE + k, 1), pl.ds(0, LANES)]

    def weight(which):
        return w_ref[pl.ds(which * 2 * LANES, 2 * LANES), :]

    re, im = pl.ds(0, LANES), pl.ds(LANES, LANES)

    def forward(ck, sig, sub):
        at = pl.ds(sub * 8, 8)
        values = [
            recv_x[ck, sig, n // 2, at, pl.ds((n % 2) * LANES, LANES)] for n in range(HALF)
        ]
        found = padded_forward(values)
        for k in range(KEPT):
            cos, sin = twist(0, k), twist(1, k)
            real, imag = found[k]
            to = pl.ds(k * rows + sub * 8, 8)
            if k == 0:
                spec_a[sig, to, re] = real
                spec_a[sig, to, im] = jnp.zeros_like(real)
            elif imag is None:
                spec_a[sig, to, re] = real * cos
                spec_a[sig, to, im] = -(real * sin)
            else:
                spec_a[sig, to, re] = real * cos + imag * sin
                spec_a[sig, to, im] = imag * cos - real * sin

    def inverse(ck, sig, sub, store):
        found = {}
        for k in range(KEPT):
            cos, sin = twist(2, k), twist(3, k)
            at = pl.ds(k * rows + sub * 8, 8)
            real = spec_a[sig, at, re]
            imag = spec_a[sig, at, im]
            if k == 0 or k == HALF:
                found[k] = (real * cos - imag * sin, None)
            else:
                found[k] = (real * cos - imag * sin, imag * cos + real * sin)
        values = padded_inverse(found)
        for n in range(HALF):
            store(n // 2, pl.ds(sub * 8, 8), pl.ds((n % 2) * LANES, LANES), values[n])

    def matmul(src, dst, which):
        data = src[...].reshape(-1, 2 * LANES)
        height = data.shape[0]
        high = data.astype(jnp.bfloat16)
        low = (data - high.astype(jnp.float32)).astype(jnp.bfloat16)
        both = jnp.dot(
            jnp.concatenate([high, low], axis=0),
            weight(2 * which),
            preferred_element_type=jnp.float32,
        )
        rest = jnp.dot(high, weight(2 * which + 1), preferred_element_type=jnp.float32)
        dst[...] = (both[:height] + both[height:] + rest).reshape(dst.shape)

    def loop(count, act, unroll=1):
        def step(i, carry):
            act(i)
            return carry

        lax.fori_loop(0, count, step, 0, unroll=unroll)

    def filter_grad(ck):
        drain(recv_x.at[ck, pl.ds(0, 2), pl.ds(0, ctx - 1)], sx_recv.at[ck])
        loop(2 * subs, lambda n: forward(ck, n // subs, lax.rem(n, subs)))
        matmul(spec_a.at[pl.ds(0, 2)], spec_b.at[ck, pl.ds(0, 2)], 0)

        def pointwise(k):
            at = pl.ds(k * rows, rows)
            z_re, z_im = spec_b[ck, 0, at, re], spec_b[ck, 0, at, im]
            d_re, d_im = spec_b[ck, 1, at, re], spec_b[ck, 1, at, im]
            spec_a[0, at, re] = z_re * d_re + z_im * d_im
            spec_a[0, at, im] = z_re * d_im - z_im * d_re

        loop(KEPT, pointwise, 11)
        matmul(spec_a.at[0], spec_a.at[1], 1)

        def store(block, at, lanes, value):
            part_g[ck, block // ring, block % ring, at, lanes] = value

        loop(subs, lambda sub: inverse(ck, 1, sub, store))

        @pl.when((ck == 0) & jnp.logical_not(leads))
        def _():
            pl.semaphore_wait(go_sem, 1)

        for i in far_first:
            copy_g(ck, i).start()

    def convolutions(ck):
        drain(recv_x.at[ck, 2, pl.ds(0, ctx - 1)], sf_recv.at[ck])
        own_f(ck).wait()
        loop(subs, lambda sub: forward(ck, 2, sub))
        matmul(spec_a.at[2], spec_b.at[ck, 2], 0)

        def pointwise(k):
            at = pl.ds(k * rows, rows)
            z_re, z_im = spec_b[ck, 0, at, re], spec_b[ck, 0, at, im]
            d_re, d_im = spec_b[ck, 1, at, re], spec_b[ck, 1, at, im]
            f_re, f_im = spec_b[ck, 2, at, re], spec_b[ck, 2, at, im]
            spec_a[0, at, re] = z_re * f_re - z_im * f_im
            spec_a[0, at, im] = z_re * f_im + z_im * f_re
            spec_a[1, at, re] = f_re * d_re + f_im * d_im
            spec_a[1, at, im] = f_re * d_im - f_im * d_re

        loop(KEPT, pointwise, 11)
        matmul(spec_a.at[pl.ds(0, 2)], spec_a.at[pl.ds(0, 2)], 1)

        def back(n):
            sig, sub = n // subs, lax.rem(n, subs)

            def store(block, at, lanes, value):
                send_y[ck, sig, block, at, lanes] = value

            inverse(ck, sig, sub, store)

        for sig in range(2):
            loop(subs, lambda sub: back(sig * subs + sub))
            outward(lambda i: copy_y(ck, sig, i).start())
        recv_y[ck, 0, me_c] = send_y[ck, 0, me_c]
        recv_y[ck, 1, me_c] = send_y[ck, 1, me_c]

    def reduce(ck):
        drain(recv_g.at[ck], sg_recv.at[ck])
        for part in range(PLANES):
            total = part_g[ck, part, slot]
            for i in range(ring - 1):
                total = total + recv_g[ck, i, part]
            sum_g[ck, part] = total
            for step in range(PLANES):
                plane = lax.rem(me_p + 1 + step, PLANES)
                mine = is_self(plane, part)

                @pl.when(jnp.logical_not(mine))
                def _():
                    copy_s(ck, plane, part).start()

                @pl.when(mine)
                def _():
                    recv_s[ck, part, plane] = sum_g[ck, part]

    scale = 1.0 / math.sqrt(dp * ctx * width)

    def gather(ck):
        for plane, part in swaps:

            @pl.when(jnp.logical_not(is_self(plane, part)))
            def _():
                drain(recv_s.at[ck, part, plane], ss_recv.at[ck, part, plane])

        for part in range(PLANES):
            total = recv_s[ck, part, 0]
            for plane in range(1, PLANES):
                total = total + recv_s[ck, part, plane]
            own_s[ck, part] = total * scale
        for chunk in range(CHUNKS):

            @pl.when(ck == chunk)
            def _():
                for i in far_first:
                    copy_a(chunk, i).start()
                keep(chunk).start()

    def stage(step):
        pl.when(step < CHUNKS)(lambda: first_f(step))
        pl.when(step < CHUNKS)(lambda: filter_grad(step))
        pl.when((step >= 2) & (step < CHUNKS + 2))(lambda: reduce(step - 2))

        @pl.when(step >= 3)
        def _():
            convolutions(step - 3)
            gather(step - 3)

    loop(CHUNKS + 3, stage)

    def outputs(pair, sig):
        for ck in (pair, pair + 1):
            drain(recv_y.at[ck, sig, pl.ds(0, ctx - 1)], sy_recv.at[ck, sig])
        gates = [(q_ref, out_ref), (g_ref, gq_ref)] if sig == 0 else [(v_ref, gk_ref), (k_ref, gv_ref)]

        def block(b):
            at = pl.ds(b * share + pair * rows, 2 * rows)
            value = jnp.concatenate([recv_y[pair, sig, b], recv_y[pair + 1, sig, b]], axis=0)
            for gate, to in gates:
                to[at, :] = (gate[at, :].astype(jnp.float32) * value).astype(jnp.bfloat16)

        loop(ctx, block, 4)

    for pair in range(0, CHUNKS, 2):
        for sig in range(2):
            outputs(pair, sig)

    def finish(ck):
        drain(recv_x.at[ck, pl.ds(0, 2), pl.ds(0, ctx - 1)], sx_send.at[ck])
        drain(recv_x.at[ck, 2, pl.ds(0, ctx - 1)], sf_send.at[ck])
        drain(recv_y.at[ck, :, pl.ds(0, ctx - 1)], sy_send.at[ck])
        drain(recv_g.at[ck], sg_send.at[ck])
        for plane, part in swaps:

            @pl.when(jnp.logical_not(is_self(plane, part)))
            def _():
                drain(sum_g.at[ck, part], ss_send.at[ck, plane, part])


    chunks(finish)
    for ck in range(CHUNKS):
        keep(ck).wait()
        drain(gf_refs[ck].at[:, pl.ds(0, ring - 1)], sa_send.at[ck])
        drain(gf_refs[ck].at[:, pl.ds(0, ring - 1)], sa_recv.at[ck])


def write_out(count, *refs):
    sources, targets, sem = refs[: count + CHUNKS], refs[count + CHUNKS : -1], refs[-1]
    copies = [
        pltpu.make_async_copy(sources[n], targets[n], sem.at[n]) for n in range(count)
    ]
    for ck in range(CHUNKS):
        n = count + ck
        copies.append(
            pltpu.make_async_copy(sources[n], targets[count].at[:, :, ck], sem.at[n])
        )
    for copy in copies:
        copy.start()
    for copy in copies:
        copy.wait()


def shards(ctx, dp, query, key_act, value_act, filter_taps, grad_out):
    _, channels, width = query.shape
    share = channels // ctx
    rows = share // CHUNKS
    ring = dp // PLANES
    constants = tables()
    vmem = pl.BlockSpec(memory_space=pltpu.VMEM)
    hbm = pl.BlockSpec(memory_space=pltpu.HBM)
    half = jax.ShapeDtypeStruct((channels, width), jnp.bfloat16)
    whole = jax.ShapeDtypeStruct((PLANES, ring, CHUNKS, rows, width), jnp.float32)
    part = jax.ShapeDtypeStruct((PLANES, ring, rows, width), jnp.float32)
    dma = pltpu.SemaphoreType.DMA
    full = pltpu.VMEM((channels, width), jnp.bfloat16)
    outs = pl.pallas_call(
        functools.partial(body, ctx, dp),
        out_shape=[half] * 4 + [part] * CHUNKS,
        in_specs=[hbm] * 6,
        out_specs=[vmem] * (4 + CHUNKS),
        scratch_shapes=[
            full,
            full,
            full,
            full,
            pltpu.VMEM(constants.shape, jnp.float32),
            pltpu.VMEM((8 * LANES, 2 * LANES), jnp.bfloat16),
            pltpu.VMEM((CHUNKS, 2, ctx, rows, width), jnp.float32),
            pltpu.VMEM((CHUNKS, 3, ctx, rows, width), jnp.float32),
            pltpu.VMEM((CHUNKS, 2, ctx, rows, width), jnp.float32),
            pltpu.VMEM((CHUNKS, 2, ctx, rows, width), jnp.float32),
            pltpu.VMEM((CHUNKS, PLANES, ring, rows, width), jnp.float32),
            pltpu.VMEM((CHUNKS, ring - 1, PLANES, rows, width), jnp.float32),
            pltpu.VMEM((CHUNKS, PLANES, rows, width), jnp.float32),
            pltpu.VMEM((CHUNKS, PLANES, PLANES, rows, width), jnp.float32),
            pltpu.VMEM((CHUNKS, PLANES, rows, width), jnp.float32),
            pltpu.VMEM((3, KEPT * rows, 2 * LANES), jnp.float32),
            pltpu.VMEM((CHUNKS, 3, KEPT * rows, 2 * LANES), jnp.float32),
            pltpu.SemaphoreType.REGULAR,
            pltpu.SemaphoreType.REGULAR,
            dma((5,)),
            dma((CHUNKS,)),
            dma((CHUNKS,)),
            dma((CHUNKS,)),
            dma((CHUNKS,)),
            dma((CHUNKS,)),
            dma((CHUNKS,)),
            dma((CHUNKS,)),
            dma((CHUNKS, 2)),
            dma((CHUNKS,)),
            dma((CHUNKS,)),
            dma((CHUNKS, PLANES, PLANES)),
            dma((CHUNKS, PLANES, PLANES)),
            dma((CHUNKS,)),
            dma((CHUNKS,)),
        ],
        compiler_params=pltpu.CompilerParams(
            collective_id=0, has_side_effects=True, vmem_limit_bytes=GRANT
        ),
        cost_estimate=pl.CostEstimate(
            flops=3 * 2 * 6 * KEPT * share * 256 * 256, bytes_accessed=4 * 2**20, transcendentals=0
        ),
        name="hyena",
    )(
        query.reshape(channels, width),
        key_act.reshape(channels, width),
        value_act.reshape(channels, width),
        grad_out.reshape(channels, width),
        filter_taps,
        jnp.asarray(constants),
    )
    outs = pl.pallas_call(
        functools.partial(write_out, 4),
        out_shape=[half] * 4 + [whole],
        in_specs=[vmem] * (4 + CHUNKS),
        out_specs=[hbm] * 5,
        scratch_shapes=[dma((4 + CHUNKS,))],
        compiler_params=pltpu.CompilerParams(vmem_limit_bytes=4 * 1024 * 1024),
        name="write_out",
    )(*outs)
    shape = query.shape
    return (
        outs[0].reshape(shape),
        outs[1].reshape(shape),
        outs[2].reshape(shape),
        outs[3].reshape(shape),
        outs[4].reshape(channels, width),
    )


def solution(mesh):
    row = P("dp", None, "ctx")
    taps = P(None, "ctx")
    return jax.shard_map(
        functools.partial(shards, mesh.shape["ctx"], mesh.shape["dp"]),
        mesh=mesh,
        in_specs=(row, row, row, taps, row),
        out_specs=(row, row, row, row, taps),
        check_vma=False,
    )
```
